128 devices in a mesh: night: 4 (over z), bl: 32 (over y, x, core).
Axes of the slice: x: 4, y: 4, z: 4, core: 2. Of those that a mesh axis runs over, the one named last changes fastest.
Arguments:
- visibilities: float32 [2, 4, 128, 30, 768], P(None, 'night', 'bl'), may hold values from -6 to 6
- corrupted_sample_markers: int32 [4, 768], P('night'), may hold values from 0 to 1073741823
- antenna_gain_table: float32 [2, 4, 352, 768], P(None, 'night', 'bl'), may hold values from -4 to 4
- baseline_antennas: int32 [128, 2], P('bl'), may hold values from 0 to 351
- first_bin: int32 [4], P('night'), may hold values from 0 to 96
- tap_offsets: int32 [4, 32], P('night'), may hold values from 0 to 26
- tap_weights: float32 [4, 32, 4], P('night'), may hold values from 0.1 to 0.5
- lst_delay: float32 [4, 32], P('night'), may hold values from -1 to 1
- fringe_rate: float32 [128], P('bl'), may hold values from -3 to 3
Outputs:
- binned: float32 [2, 128, 128, 768], P(None, ('night', 'bl'))
- weight_total: float32 [128, 768], P(('night', 'bl'))
The draws below stay inside these ranges and needn't reach their ends.
All inputs are finite; a program needn't handle non-finite values.
Results may differ from the reference program's by a relative error of at most 0.0001.
Values sent between devices are 32-bit elements; how exact they have to be, the bound alone decides.
A program may use at most 64 MiB of HBM per device.

```python
import jax
import jax.numpy as jnp
from jax import lax

CHANNEL_COUNT = 768
ANTENNA_COUNT = 352
SAMPLES_PER_DARK = 30
TAPS = 4
NIGHT_COUNT = 4
BASELINE_COUNT = 128
LBINS = 128
NBIN = 32


def plant(result, rng, smallest, high):
    longest = result.shape.index(max(result.shape))
    spots = []
    for shift in (0, 1):
        where = [jax.random.randint(jax.random.fold_in(rng, axis), (), 0, length) for axis, length in enumerate(result.shape)]
        where[longest] = (where[longest] + shift) % result.shape[longest]
        spots.append(tuple(where))
    return result.at[spots[0]].set(smallest).at[spots[1]].set(high)


def shard_levels(own_key, extent, shards, least, high):
    def one(dim, parts):
        draws = jax.random.uniform(jax.random.fold_in(jax.random.fold_in(own_key, 6), dim), (parts,), jnp.float32, least / len(shards), high / len(shards))
        return jnp.repeat(jnp.exp(draws), extent[dim] // parts).reshape((-1,) + (1,) * (len(extent) - dim - 1))

    level = one(*shards[0])
    for cut in shards[1:]:
        level = level * one(*cut)
    return level


def normal_values(stream_key, dims, scale, limit, pieces=(), held_as=jnp.bfloat16):
    drawn = jax.random.normal(stream_key, dims, jnp.float32) * scale
    if len(pieces) > 0:
        drawn = shard_levels(stream_key, dims, pieces, -0.22, 0.18) * drawn
    return jnp.clip(drawn, min=-limit, max=limit).astype(held_as)


def setup_inputs(seed: int = 0) -> dict:
    streams_of = jax.random.split(jax.random.key(seed), 10)
    visibilities = normal_values(streams_of[0], (2, NIGHT_COUNT, BASELINE_COUNT, SAMPLES_PER_DARK, CHANNEL_COUNT), 1.0, 6.0, ((1, 4), (2, 32)), jnp.float32)
    corrupted_sample_markers = plant(jax.random.randint(streams_of[1], (NIGHT_COUNT, CHANNEL_COUNT), 0, 1073741824), jax.random.fold_in(streams_of[1], 1), 0, 1073741823).astype(jnp.int32)
    antenna_gain_table = normal_values(streams_of[2], (2, NIGHT_COUNT, ANTENNA_COUNT, CHANNEL_COUNT), 0.7, 4.0, ((1, 4), (2, 32)), jnp.float32)
    baseline_antennas = plant(jax.random.randint(streams_of[3], (BASELINE_COUNT, 2), 0, ANTENNA_COUNT), jax.random.fold_in(streams_of[3], 1), 0, ANTENNA_COUNT - 1).astype(jnp.int32)
    first_bin = plant(jax.random.randint(streams_of[4], (NIGHT_COUNT,), 0, LBINS - NBIN + 1), jax.random.fold_in(streams_of[4], 1), 0, LBINS - NBIN).astype(jnp.int32)
    tap_offsets = plant(jax.random.randint(streams_of[5], (NIGHT_COUNT, NBIN), 0, SAMPLES_PER_DARK - TAPS + 1), jax.random.fold_in(streams_of[5], 1), 0, SAMPLES_PER_DARK - TAPS).astype(jnp.int32)
    tap_weights = jnp.clip(0.1 + 0.4 * jax.random.uniform(streams_of[6], (NIGHT_COUNT, NBIN, TAPS), jnp.float32) ** shard_levels(streams_of[6], (NIGHT_COUNT, NBIN, TAPS), ((0, 4),), -0.2, 0.2), 0.1, 0.5)
    lst_delay = jnp.clip(jax.random.uniform(streams_of[7], (NIGHT_COUNT, NBIN), jnp.float32, -1.0, 1.0) * shard_levels(streams_of[7], (NIGHT_COUNT, NBIN), ((0, 4),), -0.4, 0.0), -1.0, 1.0)
    fringe_rate = jnp.clip(jax.random.uniform(streams_of[8], (BASELINE_COUNT,), jnp.float32, -3.0, 3.0) * shard_levels(streams_of[8], (BASELINE_COUNT,), ((0, 32),), -0.4, 0.0), -3.0, 3.0)
    return dict(visibilities=visibilities, corrupted_sample_markers=corrupted_sample_markers, antenna_gain_table=antenna_gain_table, baseline_antennas=baseline_antennas, first_bin=first_bin, tap_offsets=tap_offsets, tap_weights=tap_weights, lst_delay=lst_delay, fringe_rate=fringe_rate)


finest_accuracy = lax.Precision.HIGHEST


def unpack_reject_markers(packed, sample_indices):
    sample = jnp.arange(sample_indices, dtype=jnp.int32)
    flag_bits = jnp.bitwise_and(jnp.right_shift(packed[..., None, :], sample[:, None]), 1)
    return 1.0 - flag_bits.astype(jnp.float32)


def tap_matrix(offsets, weights, sample_indices):
    sample = jnp.arange(sample_indices, dtype=jnp.int32)
    tap_index = jnp.arange(weights.shape[-1], dtype=jnp.int32)
    matches = sample == (offsets[..., None, None] + tap_index[:, None])
    return jnp.sum(jnp.where(matches, weights[..., None], jnp.float32(0.0)), axis=-2)


def reference(visibilities, corrupted_sample_markers, antenna_gain_table, baseline_antennas, first_bin, tap_offsets, tap_weights, lst_delay, fringe_rate):
    first_gain = antenna_gain_table[:, :, baseline_antennas[:, 0]]
    second_gain = antenna_gain_table[:, :, baseline_antennas[:, 1]]
    gain_real = first_gain[0] * second_gain[0] + first_gain[1] * second_gain[1]
    gain_imag = first_gain[1] * second_gain[0] - first_gain[0] * second_gain[1]
    clean_sample_selector = unpack_reject_markers(corrupted_sample_markers, SAMPLES_PER_DARK)
    interpolant_kernels = tap_matrix(tap_offsets, tap_weights, SAMPLES_PER_DARK)
    evening_share = jnp.einsum("bdr,bro->bdo", interpolant_kernels, clean_sample_selector, precision=finest_accuracy)
    frequency = 1.0 + jnp.arange(CHANNEL_COUNT, dtype=jnp.float32) / CHANNEL_COUNT
    summed = jnp.zeros((2, LBINS, BASELINE_COUNT, CHANNEL_COUNT), jnp.float32)
    weight_total = jnp.zeros((LBINS, CHANNEL_COUNT), jnp.float32)
    anchor = jnp.zeros((), jnp.int32)
    for evening_index in range(NIGHT_COUNT):
        real_part = visibilities[0, evening_index]
        imag_part = visibilities[1, evening_index]
        gain_re = gain_real[evening_index][:, None, :]
        gain_im = gain_imag[evening_index][:, None, :]
        retained_selector = clean_sample_selector[evening_index][None]
        calibrated = jnp.stack([(gain_re * real_part - gain_im * imag_part) * retained_selector,
                                (gain_re * imag_part + gain_im * real_part) * retained_selector])
        binned_night = jnp.einsum("lt,xbtc->xlbc", interpolant_kernels[evening_index], calibrated, precision=finest_accuracy)
        angle = fringe_rate[None, :, None] * lst_delay[evening_index][:, None, None] * frequency[None, None, :]
        cosine = jnp.cos(angle)
        sine_part = jnp.sin(angle)
        rotated = jnp.stack([cosine * binned_night[0] - sine_part * binned_night[1],
                             sine_part * binned_night[0] + cosine * binned_night[1]])
        first = first_bin[evening_index].astype(jnp.int32)
        current = lax.dynamic_slice(summed, (anchor, first, anchor, anchor), (2, NBIN, BASELINE_COUNT, CHANNEL_COUNT))
        summed = lax.dynamic_update_slice(summed, current + rotated, (anchor, first, anchor, anchor))
        current_weight = lax.dynamic_slice(weight_total, (first, anchor), (NBIN, CHANNEL_COUNT))
        weight_total = lax.dynamic_update_slice(weight_total, current_weight + evening_share[evening_index], (first, anchor))
    binned = summed / jnp.maximum(weight_total, 0.5)[None, :, None, :]
    return binned, weight_total
```

```python
import functools
import math

import jax
import jax.numpy as jnp
import numpy as np
from jax import lax
from jax.experimental import pallas as pl
from jax.experimental.pallas import tpu as pltpu
from jax.sharding import PartitionSpec as P

MESH = pl.DeviceIdType.MESH
F32 = jnp.float32
I32 = jnp.int32

NIGHTS = 4
DEVS = 32
BINS = 32
ROWS = 8
CH = 768
SAMPLES = 30
TAPS = 4
OWN_ANT = 11
STAGES = 3
WIDE = 256
HALF = 128
GHALF = 384


def _fit(kind, terms):
    k = np.arange(200)
    u = 0.125 * (1 + np.cos(np.pi * (k + 0.5) / 200))
    r = np.sqrt(u)
    y = np.sin(2 * np.pi * r) / r if kind == "sin" else np.cos(2 * np.pi * r)
    cheb = np.polynomial.chebyshev.Chebyshev.fit(u, y, terms - 1, domain=[0, 0.25])
    return [float(v) for v in cheb.convert(kind=np.polynomial.Polynomial).coef]


SIN_C = _fit("sin", 8)
COS_C = _fit("cos", 8)


def horner(coef, u):
    acc = jnp.full_like(u, coef[-1])
    for c in coef[-2::-1]:
        acc = acc * u + c
    return acc


def swap4(v):
    return pltpu.roll(v, 4, 0)


def flag(cond):
    return jnp.where(cond, jnp.float32(1.0), jnp.float32(0.0))


def comm_kernel(
    vis, gains, imeta_v, fmeta_v, bas_v, fr8, imeta_s, fmeta_s, delay_s,
    landed, wt_ref,
    V, UV, Y, S, gy, gx, bx_v, by_v, bx_s, by_s, m0, m1, c0, c1, G, GZ,
    zi, zf, zis, zfs, s1p, s1n, s2p, s2n, r1p, r1n, r2p, r2n, r3p, r3n,
    local_sem, gsend, gyr, gxr, bsend, bxr, byr, msend, mrecv,
    send0, send1, recv0, recv1, zsend, zrecv, gzs, gzr, asend, arecv,
):
    n = lax.axis_index("night")
    me = lax.axis_index("bl")
    core = lax.rem(me, 2)
    x = lax.rem(me // 2, 4)
    y = me // 8

    def bl_of(yy, xx, cc):
        return (yy * 4 + xx) * 2 + cc

    def rcopy(src, dst, ss, rs, dev):
        return pltpu.make_async_remote_copy(
            src_ref=src, dst_ref=dst, send_sem=ss, recv_sem=rs, device_id=dev, device_id_type=MESH
        )

    load_vis = pltpu.make_async_copy(vis, V, local_sem.at[0])
    load_vis.start()
    own_gy = pltpu.make_async_copy(gains.at[:, :, pl.ds(0, GHALF)], gy.at[y], local_sem.at[1])
    own_gy.start()
    own_gx = pltpu.make_async_copy(gains.at[:, :, pl.ds(GHALF, GHALF)], gx.at[x], local_sem.at[2])
    own_gx.start()

    barrier = pltpu.get_barrier_semaphore()

    def greet_z(k, _):
        pl.semaphore_signal(barrier, inc=1, device_id=(lax.rem(n + k, 4), me), device_id_type=MESH)
        return _

    def greet_bl(k, _):
        pl.semaphore_signal(barrier, inc=1, device_id=(n, lax.rem(me + k, DEVS)), device_id_type=MESH)
        return _

    lax.fori_loop(1, NIGHTS, greet_z, 0)
    lax.fori_loop(1, DEVS, greet_bl, 0)
    pl.semaphore_wait(barrier, NIGHTS - 1 + DEVS - 1)

    zi[n] = imeta_v[...]
    zf[n] = fmeta_v[...]
    bx_v[x * 2 + core] = bas_v[...]
    by_v[y * 2 + core] = bas_v[...]

    def gain_a(k):
        ty = lax.rem(y + k, 4)
        tx = lax.rem(x + k, 4)
        return (
            rcopy(gains.at[:, :, pl.ds(0, GHALF)], gy.at[y], gsend.at[0, k], gyr.at[y], (n, bl_of(ty, x, core))),
            rcopy(gains.at[:, :, pl.ds(GHALF, GHALF)], gx.at[x], gsend.at[1, k], gxr.at[x], (n, bl_of(y, tx, core))),
        )

    for k in (1, 3, 2):
        for c in gain_a(k):
            c.start()

    def slot_dev(k, own):
        s = lax.rem(own + k, 8)
        return s, s // 2, lax.rem(s, 2)

    def bas_x(k):
        s, tx, tc = slot_dev(k, x * 2 + core)
        mine = x * 2 + core
        return rcopy(bas_v, bx_v.at[mine], bsend.at[0, k], bxr.at[mine], (n, bl_of(y, tx, tc)))

    def bas_y(k):
        s, ty, tc = slot_dev(k, y * 2 + core)
        mine = y * 2 + core
        return rcopy(bas_v, by_v.at[mine], bsend.at[1, k], byr.at[mine], (n, bl_of(ty, x, tc)))

    def start_bas(k, _):
        bas_x(k).start()
        bas_y(k).start()
        return _

    lax.fori_loop(1, 8, start_bas, 0)

    def meta(k):
        t = lax.rem(n + k, 4)
        return (
            rcopy(imeta_v, zi.at[n], msend.at[0, k], mrecv.at[0, n], (t, me)),
            rcopy(fmeta_v, zf.at[n], msend.at[1, k], mrecv.at[1, n], (t, me)),
        )

    for k in (1, 3, 2):
        for c in meta(k):
            c.start()

    first = imeta_s[32]

    def shift_of(f, night, e):
        return (lax.shift_right_logical(f, 5) + jnp.where(e < (f & 31), 1, 0) - night) & 3

    lane = lax.broadcasted_iota(I32, (ROWS, WIDE), 1).astype(F32)
    row = lax.broadcasted_iota(I32, (ROWS, WIDE), 0)
    sign = jnp.where(row < 4, jnp.float32(-1.0), jnp.float32(1.0))

    load_vis.wait()

    def prepare(st):
        at = st * WIDE

        def per_sample(t, _):
            bits = (imeta_v[:, pl.ds(HALF + at, WIDE)] >> t) & 1
            keep = 1.0 - bits.astype(F32)
            for i in range(ROWS):
                UV[t, pl.ds(i, 1), pl.ds(at, WIDE)] = V[i // 4, i % 4, pl.ds(t, 1), pl.ds(at, WIDE)] * keep
            return _

        lax.fori_loop(0, SAMPLES, per_sample, 0)
        freq = 1.0 + (lane + float(at)) * (1.0 / CH)
        rate = fr8[...] * freq

        def per_bin(e, _):
            l = (e - first) & 31
            off = imeta_s[l]
            acc = fmeta_s[l * 4] * UV[off, :, pl.ds(at, WIDE)]
            for k in range(1, TAPS):
                acc = acc + fmeta_s[l * 4 + k] * UV[off + k, :, pl.ds(at, WIDE)]
            turns = rate * delay_s[l]
            r = turns - jnp.floor(turns + 0.5)
            u = r * r
            sine = horner(SIN_C, u) * (r * sign)
            cosine = horner(COS_C, u)
            Y[st, e] = cosine * acc + sine * swap4(acc)
            return _

        lax.fori_loop(0, BINS, per_bin, 0)

    up = lax.rem(n + 1, 4)
    down = lax.rem(n + 3, 4)
    far = lax.rem(n + 2, 4)

    def zcopy(st, which):
        src = (s1p, s1n, s2p, s2n)[which]
        dst = (r1p, r1n, r2p, r2n)[which]
        to = up if which % 2 == 0 else down
        return rcopy(src.at[st], dst.at[st], zsend.at[st, which], zrecv.at[st, which], (to, me))

    def forward(which):
        src, dst = ((r1p, r3p), (r1n, r3n))[which]
        to = (up, down)[which]
        return rcopy(src.at[0], dst, zsend.at[STAGES, which], zrecv.at[STAGES, which], (to, me))

    lo = pl.ds(0, HALF)
    hi = pl.ds(HALF, HALF)

    def build_first(st):
        def per_bin(e, _):
            s = shift_of(first, n, e)
            a, b = Y[st, e, :, lo], Y[st, e, :, hi]
            two = flag(s == 2)
            s1p[st, e] = two * a + flag(s == 1) * b
            s1n[st, e] = two * b + flag(s == 3) * a
            return _

        lax.fori_loop(0, BINS, per_bin, 0)

    prepare(0)
    build_first(0)
    zcopy(0, 0).start()
    zcopy(0, 1).start()

    def early_second(e, _):
        s = shift_of(first, n, e)
        s2p[0, e] = flag(s == 1) * Y[0, e, :, lo]
        s2n[0, e] = flag(s == 3) * Y[0, e, :, hi]
        return _

    lax.fori_loop(0, BINS, early_second, 0)
    zcopy(0, 2).start()
    zcopy(0, 3).start()

    def wait_bas(k, _):
        sx = lax.rem(x * 2 + core + k, 8)
        sy = lax.rem(y * 2 + core + k, 8)
        rcopy(bas_v, bx_v.at[sx], bsend.at[0, k], bxr.at[sx], (n, me)).wait_recv()
        rcopy(bas_v, by_v.at[sy], bsend.at[1, k], byr.at[sy], (n, me)).wait_recv()
        return _

    lax.fori_loop(1, 8, wait_bas, 0)
    to_s0 = pltpu.make_async_copy(bx_v, bx_s, local_sem.at[3])
    to_s1 = pltpu.make_async_copy(by_v, by_s, local_sem.at[4])
    to_s0.start()
    to_s1.start()
    own_gy.wait()
    own_gx.wait()
    for k in (1, 2, 3):
        sy, sx = lax.rem(y + k, 4), lax.rem(x + k, 4)
        rcopy(gy.at[sy], gy.at[sy], gsend.at[0, k], gyr.at[sy], (n, me)).wait_recv()
        rcopy(gx.at[sx], gx.at[sx], gsend.at[1, k], gxr.at[sx], (n, me)).wait_recv()
    to_s0.wait()
    to_s1.wait()

    def pick(slot, asked, table, out, mine_a, along):
        for r in range(ROWS):
            a = asked[slot, 0, r]
            owner = a // OWN_ANT
            at = a - owner * OWN_ANT
            oc = owner & 1
            ox = (owner >> 1) & 3
            oy = owner >> 3
            fixed, moving = (ox, oy) if along == 0 else (oy, ox)
            w = flag((fixed == mine_a) & (oc == core))
            for p in range(2):
                out[slot, p, pl.ds(r, 1), :] = w * table[moving, p, pl.ds(at, 1), :]

    def gain_b0(k):
        s, tx, tc = slot_dev(k, x * 2 + core)
        mine = x * 2 + core
        return rcopy(m0.at[s], c0.at[mine], send0.at[k], recv0.at[mine], (n, bl_of(y, tx, tc)))

    def gain_b1(k):
        s, ty, tc = slot_dev(k, y * 2 + core)
        mine = y * 2 + core
        return rcopy(m1.at[s], c1.at[mine], send1.at[k], recv1.at[mine], (n, bl_of(ty, x, tc)))

    def send_rows(k, _):
        pick(lax.rem(x * 2 + core + k, 8), bx_s, gy, m0, x, 0)
        gain_b0(k).start()
        pick(lax.rem(y * 2 + core + k, 8), by_s, gx, m1, y, 1)
        gain_b1(k).start()
        return _

    lax.fori_loop(1, 8, send_rows, 0)
    pick(x * 2 + core, bx_s, gy, m0, x, 0)
    pick(y * 2 + core, by_s, gx, m1, y, 1)
    c0[x * 2 + core] = m0[x * 2 + core]
    c1[y * 2 + core] = m1[y * 2 + core]

    for k in (1, 2, 3):
        o = lax.rem(n + k, 4)
        rcopy(imeta_v, zi.at[o], msend.at[0, k], mrecv.at[0, o], (n, me)).wait_recv()
        rcopy(fmeta_v, zf.at[o], msend.at[1, k], mrecv.at[1, o], (n, me)).wait_recv()
    to_s2 = pltpu.make_async_copy(zi.at[:, :, pl.ds(0, HALF)], zis, local_sem.at[5])
    to_s3 = pltpu.make_async_copy(zf, zfs, local_sem.at[6])
    to_s2.start()
    to_s3.start()

    for w in (0, 1):
        zcopy(0, w).wait_recv()
        forward(w).start()

    prepare(1)
    prepare(2)

    to_s2.wait()
    to_s3.wait()
    first_down, first_up, first_far = zis[down, 0, 32], zis[up, 0, 32], zis[far, 0, 32]

    total = jnp.zeros((1, CH), F32)
    bin_here = n * BINS + me
    for k in range(NIGHTS):
        l = bin_here - zis[k, 0, 32]
        valid = flag((l >= 0) & (l < BINS))
        lc = jnp.clip(l, 0, BINS - 1)
        off = zis[k, 0, lc]
        for t in range(TAPS):
            bits = (zi[k, :, pl.ds(HALF, CH)] >> (off + t)) & 1
            total = total + (valid * zfs[k, 0, lc * 4 + t]) * (1.0 - bits.astype(F32))
    wt_ref[...] = total

    def wait_rows(k, _):
        sx = lax.rem(x * 2 + core + k, 8)
        sy = lax.rem(y * 2 + core + k, 8)
        rcopy(m0.at[sx], c0.at[sx], send0.at[k], recv0.at[sx], (n, me)).wait_recv()
        rcopy(m1.at[sy], c1.at[sy], send1.at[k], recv1.at[sy], (n, me)).wait_recv()
        return _

    lax.fori_loop(1, 8, wait_rows, 0)
    for h, c in ((0, c0), (1, c1)):
        parts = []
        for p in range(2):
            acc = c[0, p]
            for s in range(1, 8):
                acc = acc + c[s, p]
            parts.append(acc)
        A, B = parts
        G[0, :, pl.ds(h * GHALF, GHALF)] = A * swap4(A) + B * swap4(B)
        G[1, :, pl.ds(h * GHALF, GHALF)] = A * swap4(B) - B * swap4(A)
    GZ[n] = G[:, :, pl.ds(0, WIDE)]

    def gz(k):
        return rcopy(GZ.at[n], GZ.at[n], gzs.at[k], gzr.at[n], (lax.rem(n + k, 4), me))

    for k in (1, 3, 2):
        gz(k).start()

    for st in (1, 2):
        gr, gs = G[0, :, pl.ds(st * WIDE, WIDE)], G[1, :, pl.ds(st * WIDE, WIDE)]

        def apply(e, _, st=st, gr=gr, gs=gs):
            v = Y[st, e]
            v = gr * v + gs * swap4(v)
            Y[st, e] = v
            s = shift_of(first, n, e)
            a, b = v[:, :HALF], v[:, HALF:]
            two = flag(s == 2)
            s1p[st, e] = two * a + flag(s == 1) * b
            s1n[st, e] = two * b + flag(s == 3) * a
            return _

        lax.fori_loop(0, BINS, apply, 0)
        zcopy(st, 0).start()
        zcopy(st, 1).start()

    for st in (1, 2):
        zcopy(st, 0).wait_recv()
        zcopy(st, 1).wait_recv()

        def second(e, _, st=st):
            s = shift_of(first, n, e)
            s2p[st, e] = flag(s == 1) * Y[st, e, :, lo] + flag(shift_of(first_down, down, e) == 2) * r1p[st, e]
            s2n[st, e] = flag(s == 3) * Y[st, e, :, hi] + flag(shift_of(first_up, up, e) == 2) * r1n[st, e]
            return _

        lax.fori_loop(0, BINS, second, 0)
        zcopy(st, 2).start()
        zcopy(st, 3).start()

    def bin_copy(st, k):
        t = lax.rem(me + k, DEVS)
        return rcopy(S.at[st, t], landed.at[st, me], asend.at[st], arecv.at[st], (n, t))

    def send_bins(st):
        def go(k, _):
            bin_copy(st, k).start()
            return _

        lax.fori_loop(1, DEVS, go, 0)
        landed[st, me] = S[st, me]

    for k in (1, 2, 3):
        o = lax.rem(n + k, 4)
        rcopy(GZ.at[o], GZ.at[o], gzs.at[k], gzr.at[o], (n, me)).wait_recv()
    zcopy(0, 2).wait_recv()
    zcopy(0, 3).wait_recv()
    forward(0).wait_recv()
    forward(1).wait_recv()

    def combine0(e, _):
        here = flag(shift_of(first, n, e) == 0)
        from_down = flag(shift_of(first_down, down, e) == 1)
        from_up = flag(shift_of(first_up, up, e) == 3)
        from_far = flag(shift_of(first_far, far, e) == 2)

        def part(half, terms):
            acc = None
            for night, v in terms:
                w = GZ[night, 0, :, half] * v + GZ[night, 1, :, half] * swap4(v)
                acc = w if acc is None else acc + w
            S[0, e, :, half] = acc

        part(lo, ((n, here * Y[0, e, :, lo]), (up, from_up * r1n[0, e]), (down, r2p[0, e]), (far, from_far * r3p[e])))
        part(hi, ((n, here * Y[0, e, :, hi]), (down, from_down * r1p[0, e]), (up, r2n[0, e]), (far, from_far * r3n[e])))
        return _

    lax.fori_loop(0, BINS, combine0, 0)
    send_bins(0)

    for st in (1, 2):
        zcopy(st, 2).wait_recv()
        zcopy(st, 3).wait_recv()

        def combine(e, _, st=st):
            here = flag(shift_of(first, n, e) == 0)
            from_down = flag(shift_of(first_down, down, e) == 1)
            from_up = flag(shift_of(first_up, up, e) == 3)
            S[st, e, :, lo] = here * Y[st, e, :, lo] + from_up * r1n[st, e] + r2p[st, e]
            S[st, e, :, hi] = here * Y[st, e, :, hi] + from_down * r1p[st, e] + r2n[st, e]
            return _

        lax.fori_loop(0, BINS, combine, 0)
        send_bins(st)

    for k in (1, 2, 3):
        for c in gain_a(k):
            c.wait_send()
        for c in meta(k):
            c.wait_send()
        gz(k).wait_send()

    def done(k, _):
        bas_x(k).wait_send()
        bas_y(k).wait_send()
        gain_b0(k).wait_send()
        gain_b1(k).wait_send()
        return _

    lax.fori_loop(1, 8, done, 0)
    for st in range(STAGES):
        for w in range(4):
            zcopy(st, w).wait_send()
    for w in (0, 1):
        forward(w).wait_send()
    for st in range(STAGES):
        whole = rcopy(
            S.at[st, pl.ds(0, DEVS - 1)], landed.at[st, pl.ds(0, DEVS - 1)], asend.at[st], arecv.at[st], (n, me)
        )
        whole.wait_send()
        whole.wait_recv()


def final_kernel(landed, wt, out, wt_out):
    row = lax.broadcasted_iota(I32, (ROWS, WIDE), 0)
    low = row < 4
    wt_out[...] = wt[...]
    for st in range(STAGES):
        cols = pl.ds(st * WIDE, WIDE)
        inv = jnp.broadcast_to(1.0 / jnp.maximum(wt[:, cols], 0.5), (ROWS, WIDE))

        def pair(k, _, st=st, cols=cols, inv=inv):
            a = landed[st, 2 * k] * inv
            b = landed[st, 2 * k + 1] * inv
            at = pl.multiple_of(k * 8, 8)
            out[0, pl.ds(at, 8), cols] = jnp.where(low, a, swap4(b))
            out[1, pl.ds(at, 8), cols] = jnp.where(low, swap4(a), b)
            return _

        lax.fori_loop(0, DEVS // 2, pair, 0)


def per_device(
    visibilities, corrupted_sample_markers, antenna_gain_table, baseline_antennas, first_bin, tap_offsets, tap_weights,
    lst_delay, fringe_rate,
):
    vis = visibilities.reshape(2, 4, SAMPLES, CH)
    gains = antenna_gain_table.reshape(2, OWN_ANT, CH)
    small = jnp.concatenate([tap_offsets.reshape(32), first_bin, jnp.zeros((95,), I32)])
    imeta = jnp.concatenate([small, corrupted_sample_markers.reshape(CH)]).reshape(1, HALF + CH)
    fmeta = tap_weights.reshape(1, HALF)
    bas = jnp.concatenate([baseline_antennas.T.reshape(8), jnp.zeros((120,), I32)]).reshape(1, HALF)
    fr8 = jnp.broadcast_to(jnp.tile(fringe_rate * (1.0 / (2.0 * math.pi)), 2)[:, None], (ROWS, WIDE))

    vm = pl.BlockSpec(memory_space=pltpu.VMEM)
    sm = pl.BlockSpec(memory_space=pltpu.SMEM)
    hbm = pl.BlockSpec(memory_space=pl.ANY)
    D = pltpu.SemaphoreType.DMA
    msg = (STAGES, BINS, ROWS, HALF)
    landed, wt = pl.pallas_call(
        comm_kernel,
        out_shape=(
            jax.ShapeDtypeStruct((STAGES, DEVS, ROWS, WIDE), F32),
            jax.ShapeDtypeStruct((1, CH), F32),
        ),
        in_specs=[hbm, hbm, vm, vm, vm, vm, sm, sm, sm],
        out_specs=(vm, vm),
        scratch_shapes=[
            pltpu.VMEM((2, 4, SAMPLES, CH), F32),
            pltpu.VMEM((SAMPLES, ROWS, CH), F32),
            pltpu.VMEM((STAGES, BINS, ROWS, WIDE), F32),
            pltpu.VMEM((STAGES, BINS, ROWS, WIDE), F32),
            pltpu.VMEM((4, 2, OWN_ANT, GHALF), F32),
            pltpu.VMEM((4, 2, OWN_ANT, GHALF), F32),
            pltpu.VMEM((8, 1, HALF), I32),
            pltpu.VMEM((8, 1, HALF), I32),
            pltpu.SMEM((8, 1, HALF), I32),
            pltpu.SMEM((8, 1, HALF), I32),
            pltpu.VMEM((8, 2, ROWS, GHALF), F32),
            pltpu.VMEM((8, 2, ROWS, GHALF), F32),
            pltpu.VMEM((8, 2, ROWS, GHALF), F32),
            pltpu.VMEM((8, 2, ROWS, GHALF), F32),
            pltpu.VMEM((2, ROWS, CH), F32),
            pltpu.VMEM((NIGHTS, 2, ROWS, WIDE), F32),
            pltpu.VMEM((NIGHTS, 1, HALF + CH), I32),
            pltpu.VMEM((NIGHTS, 1, HALF), F32),
            pltpu.SMEM((NIGHTS, 1, HALF), I32),
            pltpu.SMEM((NIGHTS, 1, HALF), F32),
        ]
        + [pltpu.VMEM(msg, F32)] * 8
        + [pltpu.VMEM(msg[1:], F32)] * 2
        + [
            D((7,)), D((2, 4)), D((4,)), D((4,)), D((2, 8)), D((8,)), D((8,)), D((2, 4)), D((2, 4)),
            D((8,)), D((8,)), D((8,)), D((8,)), D((STAGES + 1, 4)), D((STAGES + 1, 4)), D((4,)), D((4,)),
            D((STAGES,)), D((STAGES,)),
        ],
        compiler_params=pltpu.CompilerParams(
            collective_id=0, has_side_effects=True, vmem_limit_bytes=40 * 1024 * 1024
        ),
        name="exchange",
    )(vis, gains, imeta, fmeta, bas, fr8, small, fmeta.reshape(HALF), lst_delay.reshape(BINS))

    binned, weight_total = pl.pallas_call(
        final_kernel,
        out_shape=(jax.ShapeDtypeStruct((2, 4 * DEVS, CH), F32), jax.ShapeDtypeStruct((1, CH), F32)),
        in_specs=[vm, vm],
        out_specs=(vm, vm),
        compiler_params=pltpu.CompilerParams(vmem_limit_bytes=16 * 1024 * 1024),
        name="assemble",
    )(landed, wt)
    return binned.reshape(2, 1, 4 * DEVS, CH), weight_total


def solution(mesh):
    placed = (
        P(None, "night", "bl", None, None),
        P("night", None),
        P(None, "night", "bl", None),
        P("bl", None),
        P("night"),
        P("night", None),
        P("night", None, None),
        P("night", None),
        P("bl"),
    )
    return jax.shard_map(
        per_device,
        mesh=mesh,
        in_specs=placed,
        out_specs=(P(None, ("night", "bl"), None, None), P(("night", "bl"), None)),
        check_vma=False,
    )
```

```python
import functools
import math

import jax
import jax.numpy as jnp
import numpy as np
from jax import lax
from jax.experimental import pallas as pl
from jax.experimental.pallas import tpu as pltpu
from jax.sharding import PartitionSpec as P

MESH = pl.DeviceIdType.MESH
F32 = jnp.float32
I32 = jnp.int32

NIGHTS = 4
DEVS = 32
BINS = 32
ROWS = 8
CH = 768
SAMPLES = 30
TAPS = 4
OWN_ANT = 11
STAGES = 3
WIDE = 256
HALF = 128
GHALF = 384


def _fit(kind, terms):
    k = np.arange(200)
    u = 0.125 * (1 + np.cos(np.pi * (k + 0.5) / 200))
    r = np.sqrt(u)
    y = np.sin(2 * np.pi * r) / r if kind == "sin" else np.cos(2 * np.pi * r)
    cheb = np.polynomial.chebyshev.Chebyshev.fit(u, y, terms - 1, domain=[0, 0.25])
    return [float(v) for v in cheb.convert(kind=np.polynomial.Polynomial).coef]


SIN_C = _fit("sin", 8)
COS_C = _fit("cos", 8)


def horner(coef, u):
    acc = jnp.full_like(u, coef[-1])
    for c in coef[-2::-1]:
        acc = acc * u + c
    return acc


def swap4(v):
    return pltpu.roll(v, 4, 0)


def flag(cond):
    return jnp.where(cond, jnp.float32(1.0), jnp.float32(0.0))


def comm_kernel(
    vis, gains, flags_h, offs_h, first_h, weights_h, delay_h, bas_h, rate_h,
    landed, wt_ref,
    offs_s, first_s, weights_s, delay_s, rate_s, V, UV, Y, S, gy, gx, bx_v, by_v, bx_s, by_s, m0, m1, c0, c1, G, GZ,
    zflags, zfirst, zoffs, zw, zfirst_s, zoffs_s, zw_s, s1p, s1n, s2p, s2n, r1p, r1n, r2p, r2n, r3p, r3n,
    local_sem, gsend, gyr, gxr, bsend, bxr, byr, msend, mrecv,
    send0, send1, recv0, recv1, zsend, zrecv, gzs, gzr, asend, arecv,
):
    n = lax.axis_index("night")
    me = lax.axis_index("bl")
    core = lax.rem(me, 2)
    x = lax.rem(me // 2, 4)
    y = me // 8

    def bl_of(yy, xx, cc):
        return (yy * 4 + xx) * 2 + cc

    def rcopy(src, dst, ss, rs, dev):
        return pltpu.make_async_remote_copy(
            src_ref=src, dst_ref=dst, send_sem=ss, recv_sem=rs, device_id=dev, device_id_type=MESH
        )

    load_vis = pltpu.make_async_copy(vis, V, local_sem.at[0])
    own_gy = pltpu.make_async_copy(gains.at[:, :, :, pl.ds(0, GHALF)], gy.at[y], local_sem.at[1])
    own_gx = pltpu.make_async_copy(gains.at[:, :, :, pl.ds(GHALF, GHALF)], gx.at[x], local_sem.at[2])
    small = [
        pltpu.make_async_copy(a, b, local_sem.at[7 + i])
        for i, (a, b) in enumerate(
            (
                (first_h, first_s), (offs_h, offs_s), (weights_h, weights_s), (delay_h, delay_s), (rate_h, rate_s),
                (flags_h, zflags.at[n]), (offs_h, zoffs.at[n]), (weights_h, zw.at[n]),
                (bas_h, bx_v.at[x * 2 + core]), (bas_h, by_v.at[y * 2 + core]),
            )
        )
    ]
    for c in (*small, load_vis, own_gy, own_gx):
        c.start()

    barrier = pltpu.get_barrier_semaphore()

    def greet_z(k, _):
        pl.semaphore_signal(barrier, inc=1, device_id=(lax.rem(n + k, 4), me), device_id_type=MESH)
        return _

    def greet_bl(k, _):
        pl.semaphore_signal(barrier, inc=1, device_id=(n, lax.rem(me + k, DEVS)), device_id_type=MESH)
        return _

    lax.fori_loop(1, NIGHTS, greet_z, 0)
    lax.fori_loop(1, DEVS, greet_bl, 0)
    pl.semaphore_wait(barrier, NIGHTS - 1 + DEVS - 1)

    def gain_a(k):
        ty = lax.rem(y + k, 4)
        tx = lax.rem(x + k, 4)
        return (
            rcopy(gains.at[:, :, :, pl.ds(0, GHALF)], gy.at[y], gsend.at[0, k], gyr.at[y], (n, bl_of(ty, x, core))),
            rcopy(gains.at[:, :, :, pl.ds(GHALF, GHALF)], gx.at[x], gsend.at[1, k], gxr.at[x], (n, bl_of(y, tx, core))),
        )

    for k in (1, 3, 2):
        for c in gain_a(k):
            c.start()

    def slot_dev(k, own):
        s = lax.rem(own + k, 8)
        return s, s // 2, lax.rem(s, 2)

    def bas_x(k):
        s, tx, tc = slot_dev(k, x * 2 + core)
        mine = x * 2 + core
        return rcopy(bas_h, bx_v.at[mine], bsend.at[0, k], bxr.at[mine], (n, bl_of(y, tx, tc)))

    def bas_y(k):
        s, ty, tc = slot_dev(k, y * 2 + core)
        mine = y * 2 + core
        return rcopy(bas_h, by_v.at[mine], bsend.at[1, k], byr.at[mine], (n, bl_of(ty, x, tc)))

    def start_bas(k, _):
        bas_x(k).start()
        bas_y(k).start()
        return _

    lax.fori_loop(1, 8, start_bas, 0)

    for c in small:
        c.wait()
    first = first_s[0]
    zfirst[n] = jnp.full((1, HALF), first, I32)

    def meta(k):
        t = lax.rem(n + k, 4)
        return [
            rcopy(a, b, msend.at[i, k], mrecv.at[i, n], (t, me))
            for i, (a, b) in enumerate(
                (
                    (flags_h, zflags.at[n]), (offs_h, zoffs.at[n]), (weights_h, zw.at[n]),
                    (zfirst.at[n], zfirst.at[n]),
                )
            )
        ]

    for k in (1, 3, 2):
        for c in meta(k):
            c.start()

    def shift_of(f, night, e):
        return (lax.shift_right_logical(f, 5) + jnp.where(e < (f & 31), 1, 0) - night) & 3

    lane = lax.broadcasted_iota(I32, (ROWS, WIDE), 1).astype(F32)
    row = lax.broadcasted_iota(I32, (ROWS, WIDE), 0)
    sign = jnp.where(row < 4, jnp.float32(-1.0), jnp.float32(1.0))

    which = row & 3
    rates = jnp.where(
        which < 2, jnp.where(which == 0, rate_s[0], rate_s[1]), jnp.where(which == 2, rate_s[2], rate_s[3])
    ) * (1.0 / (2.0 * math.pi))

    load_vis.wait()

    def prepare(st):
        at = st * WIDE

        def per_sample(t, _):
            bits = (zflags[n, :, pl.ds(at, WIDE)] >> t) & 1
            both = jnp.concatenate([V[0, t, :, pl.ds(at, WIDE)], V[1, t, :, pl.ds(at, WIDE)]], axis=0)
            UV[t, :, pl.ds(at, WIDE)] = both * (1.0 - bits.astype(F32))
            return _

        lax.fori_loop(0, SAMPLES, per_sample, 0)
        freq = 1.0 + (lane + float(at)) * (1.0 / CH)
        rate = rates * freq

        def per_bin(e, _):
            l = (e - first) & 31
            off = offs_s[0, l]
            acc = weights_s[0, l] * UV[off, :, pl.ds(at, WIDE)]
            for k in range(1, TAPS):
                acc = acc + weights_s[k, l] * UV[off + k, :, pl.ds(at, WIDE)]
            turns = rate * delay_s[0, l]
            r = turns - jnp.floor(turns + 0.5)
            u = r * r
            sine = horner(SIN_C, u) * (r * sign)
            cosine = horner(COS_C, u)
            Y[st, e] = cosine * acc + sine * swap4(acc)
            return _

        lax.fori_loop(0, BINS, per_bin, 0)

    up = lax.rem(n + 1, 4)
    down = lax.rem(n + 3, 4)
    far = lax.rem(n + 2, 4)

    def zcopy(st, which):
        src = (s1p, s1n, s2p, s2n)[which]
        dst = (r1p, r1n, r2p, r2n)[which]
        to = up if which % 2 == 0 else down
        return rcopy(src.at[st], dst.at[st], zsend.at[st, which], zrecv.at[st, which], (to, me))

    def forward(which):
        src, dst = ((r1p, r3p), (r1n, r3n))[which]
        to = (up, down)[which]
        return rcopy(src.at[0], dst, zsend.at[STAGES, which], zrecv.at[STAGES, which], (to, me))

    lo = pl.ds(0, HALF)
    hi = pl.ds(HALF, HALF)

    def build_first(st):
        def per_bin(e, _):
            s = shift_of(first, n, e)
            a, b = Y[st, e, :, lo], Y[st, e, :, hi]
            two = flag(s == 2)
            s1p[st, e] = two * a + flag(s == 1) * b
            s1n[st, e] = two * b + flag(s == 3) * a
            return _

        lax.fori_loop(0, BINS, per_bin, 0)

    prepare(0)
    build_first(0)
    zcopy(0, 0).start()
    zcopy(0, 1).start()

    def early_second(e, _):
        s = shift_of(first, n, e)
        s2p[0, e] = flag(s == 1) * Y[0, e, :, lo]
        s2n[0, e] = flag(s == 3) * Y[0, e, :, hi]
        return _

    lax.fori_loop(0, BINS, early_second, 0)
    zcopy(0, 2).start()
    zcopy(0, 3).start()

    def wait_bas(k, _):
        sx = lax.rem(x * 2 + core + k, 8)
        sy = lax.rem(y * 2 + core + k, 8)
        rcopy(bas_h, bx_v.at[sx], bsend.at[0, k], bxr.at[sx], (n, me)).wait_recv()
        rcopy(bas_h, by_v.at[sy], bsend.at[1, k], byr.at[sy], (n, me)).wait_recv()
        return _

    lax.fori_loop(1, 8, wait_bas, 0)
    to_s0 = pltpu.make_async_copy(bx_v, bx_s, local_sem.at[3])
    to_s1 = pltpu.make_async_copy(by_v, by_s, local_sem.at[4])
    to_s0.start()
    to_s1.start()
    own_gy.wait()
    own_gx.wait()
    for k in (1, 2, 3):
        sy, sx = lax.rem(y + k, 4), lax.rem(x + k, 4)
        rcopy(gy.at[sy], gy.at[sy], gsend.at[0, k], gyr.at[sy], (n, me)).wait_recv()
        rcopy(gx.at[sx], gx.at[sx], gsend.at[1, k], gxr.at[sx], (n, me)).wait_recv()
    to_s0.wait()
    to_s1.wait()

    def pick(slot, asked, table, out, mine_a, along):
        for r in range(ROWS):
            a = asked[slot, r // 4, r % 4]
            owner = a // OWN_ANT
            at = a - owner * OWN_ANT
            oc = owner & 1
            ox = (owner >> 1) & 3
            oy = owner >> 3
            fixed, moving = (ox, oy) if along == 0 else (oy, ox)
            w = flag((fixed == mine_a) & (oc == core))
            for p in range(2):
                out[slot, p, pl.ds(r, 1), :] = w * table[moving, p, at]

    def gain_b0(k):
        s, tx, tc = slot_dev(k, x * 2 + core)
        mine = x * 2 + core
        return rcopy(m0.at[s], c0.at[mine], send0.at[k], recv0.at[mine], (n, bl_of(y, tx, tc)))

    def gain_b1(k):
        s, ty, tc = slot_dev(k, y * 2 + core)
        mine = y * 2 + core
        return rcopy(m1.at[s], c1.at[mine], send1.at[k], recv1.at[mine], (n, bl_of(ty, x, tc)))

    def send_rows(k, _):
        pick(lax.rem(x * 2 + core + k, 8), bx_s, gy, m0, x, 0)
        gain_b0(k).start()
        pick(lax.rem(y * 2 + core + k, 8), by_s, gx, m1, y, 1)
        gain_b1(k).start()
        return _

    lax.fori_loop(1, 8, send_rows, 0)
    pick(x * 2 + core, bx_s, gy, m0, x, 0)
    pick(y * 2 + core, by_s, gx, m1, y, 1)
    c0[x * 2 + core] = m0[x * 2 + core]
    c1[y * 2 + core] = m1[y * 2 + core]

    for k in (1, 2, 3):
        o = lax.rem(n + k, 4)
        for i, (a, b) in enumerate(
            ((flags_h, zflags.at[o]), (offs_h, zoffs.at[o]), (weights_h, zw.at[o]), (zfirst.at[o], zfirst.at[o]))
        ):
            rcopy(a, b, msend.at[i, k], mrecv.at[i, o], (n, me)).wait_recv()
    to_smem = [
        pltpu.make_async_copy(a, b, local_sem.at[17 + i])
        for i, (a, b) in enumerate(((zoffs, zoffs_s), (zw, zw_s), (zfirst, zfirst_s)))
    ]
    for c in to_smem:
        c.start()

    for w in (0, 1):
        zcopy(0, w).wait_recv()
        forward(w).start()

    prepare(1)
    prepare(2)

    for c in to_smem:
        c.wait()
    first_down, first_up, first_far = zfirst_s[down, 0, 0], zfirst_s[up, 0, 0], zfirst_s[far, 0, 0]

    total = jnp.zeros((1, CH), F32)
    bin_here = n * BINS + me
    for k in range(NIGHTS):
        l = bin_here - zfirst_s[k, 0, 0]
        valid = flag((l >= 0) & (l < BINS))
        lc = jnp.clip(l, 0, BINS - 1)
        off = zoffs_s[k, 0, lc]
        for t in range(TAPS):
            bits = (zflags[k] >> (off + t)) & 1
            total = total + (valid * zw_s[k, t, lc]) * (1.0 - bits.astype(F32))
    wt_ref[...] = total

    def wait_rows(k, _):
        sx = lax.rem(x * 2 + core + k, 8)
        sy = lax.rem(y * 2 + core + k, 8)
        rcopy(m0.at[sx], c0.at[sx], send0.at[k], recv0.at[sx], (n, me)).wait_recv()
        rcopy(m1.at[sy], c1.at[sy], send1.at[k], recv1.at[sy], (n, me)).wait_recv()
        return _

    lax.fori_loop(1, 8, wait_rows, 0)
    for h, c in ((0, c0), (1, c1)):
        parts = []
        for p in range(2):
            acc = c[0, p]
            for s in range(1, 8):
                acc = acc + c[s, p]
            parts.append(acc)
        A, B = parts
        G[0, :, pl.ds(h * GHALF, GHALF)] = A * swap4(A) + B * swap4(B)
        G[1, :, pl.ds(h * GHALF, GHALF)] = A * swap4(B) - B * swap4(A)
    GZ[n] = G[:, :, pl.ds(0, WIDE)]

    def gz(k):
        return rcopy(GZ.at[n], GZ.at[n], gzs.at[k], gzr.at[n], (lax.rem(n + k, 4), me))

    for k in (1, 3, 2):
        gz(k).start()

    for st in (1, 2):
        gr, gs = G[0, :, pl.ds(st * WIDE, WIDE)], G[1, :, pl.ds(st * WIDE, WIDE)]

        def apply(e, _, st=st, gr=gr, gs=gs):
            v = Y[st, e]
            v = gr * v + gs * swap4(v)
            Y[st, e] = v
            s = shift_of(first, n, e)
            a, b = v[:, :HALF], v[:, HALF:]
            two = flag(s == 2)
            s1p[st, e] = two * a + flag(s == 1) * b
            s1n[st, e] = two * b + flag(s == 3) * a
            return _

        lax.fori_loop(0, BINS, apply, 0)
        zcopy(st, 0).start()
        zcopy(st, 1).start()

    for st in (1, 2):
        zcopy(st, 0).wait_recv()
        zcopy(st, 1).wait_recv()

        def second(e, _, st=st):
            s = shift_of(first, n, e)
            s2p[st, e] = flag(s == 1) * Y[st, e, :, lo] + flag(shift_of(first_down, down, e) == 2) * r1p[st, e]
            s2n[st, e] = flag(s == 3) * Y[st, e, :, hi] + flag(shift_of(first_up, up, e) == 2) * r1n[st, e]
            return _

        lax.fori_loop(0, BINS, second, 0)
        zcopy(st, 2).start()
        zcopy(st, 3).start()

    def bin_copy(st, k):
        t = lax.rem(me + k, DEVS)
        return rcopy(S.at[st, t], landed.at[st, me], asend.at[st], arecv.at[st], (n, t))

    def send_bins(st):
        def go(k, _):
            bin_copy(st, k).start()
            return _

        lax.fori_loop(1, DEVS, go, 0)
        landed[st, me] = S[st, me]

    for k in (1, 2, 3):
        o = lax.rem(n + k, 4)
        rcopy(GZ.at[o], GZ.at[o], gzs.at[k], gzr.at[o], (n, me)).wait_recv()
    zcopy(0, 2).wait_recv()
    zcopy(0, 3).wait_recv()
    forward(0).wait_recv()
    forward(1).wait_recv()

    def combine0(e, _):
        here = flag(shift_of(first, n, e) == 0)
        from_down = flag(shift_of(first_down, down, e) == 1)
        from_up = flag(shift_of(first_up, up, e) == 3)
        from_far = flag(shift_of(first_far, far, e) == 2)

        def part(half, terms):
            acc = None
            for night, v in terms:
                w = GZ[night, 0, :, half] * v + GZ[night, 1, :, half] * swap4(v)
                acc = w if acc is None else acc + w
            S[0, e, :, half] = acc

        part(lo, ((n, here * Y[0, e, :, lo]), (up, from_up * r1n[0, e]), (down, r2p[0, e]), (far, from_far * r3p[e])))
        part(hi, ((n, here * Y[0, e, :, hi]), (down, from_down * r1p[0, e]), (up, r2n[0, e]), (far, from_far * r3n[e])))
        return _

    lax.fori_loop(0, BINS, combine0, 0)
    send_bins(0)

    for st in (1, 2):
        zcopy(st, 2).wait_recv()
        zcopy(st, 3).wait_recv()

        def combine(e, _, st=st):
            here = flag(shift_of(first, n, e) == 0)
            from_down = flag(shift_of(first_down, down, e) == 1)
            from_up = flag(shift_of(first_up, up, e) == 3)
            S[st, e, :, lo] = here * Y[st, e, :, lo] + from_up * r1n[st, e] + r2p[st, e]
            S[st, e, :, hi] = here * Y[st, e, :, hi] + from_down * r1p[st, e] + r2n[st, e]
            return _

        lax.fori_loop(0, BINS, combine, 0)
        send_bins(st)

    for k in (1, 2, 3):
        for c in gain_a(k):
            c.wait_send()
        for c in meta(k):
            c.wait_send()
        gz(k).wait_send()

    def done(k, _):
        bas_x(k).wait_send()
        bas_y(k).wait_send()
        gain_b0(k).wait_send()
        gain_b1(k).wait_send()
        return _

    lax.fori_loop(1, 8, done, 0)
    for st in range(STAGES):
        for w in range(4):
            zcopy(st, w).wait_send()
    for w in (0, 1):
        forward(w).wait_send()
    for st in range(STAGES):
        whole = rcopy(
            S.at[st, pl.ds(0, DEVS - 1)], landed.at[st, pl.ds(0, DEVS - 1)], asend.at[st], arecv.at[st], (n, me)
        )
        whole.wait_send()
        whole.wait_recv()


def final_kernel(landed, wt, out, wt_out):
    row = lax.broadcasted_iota(I32, (ROWS, WIDE), 0)
    low = row < 4
    wt_out[...] = wt[...]
    for st in range(STAGES):
        cols = pl.ds(st * WIDE, WIDE)
        inv = jnp.broadcast_to(1.0 / jnp.maximum(wt[:, cols], 0.5), (ROWS, WIDE))

        def pair(k, _, st=st, cols=cols, inv=inv):
            a = landed[st, 2 * k] * inv
            b = landed[st, 2 * k + 1] * inv
            at = pl.multiple_of(k * 8, 8)
            out[0, pl.ds(at, 8), cols] = jnp.where(low, a, swap4(b))
            out[1, pl.ds(at, 8), cols] = jnp.where(low, swap4(a), b)
            return _

        lax.fori_loop(0, DEVS // 2, pair, 0)


def per_device(
    visibilities, corrupted_sample_markers, antenna_gain_table, baseline_antennas, first_bin, tap_offsets, tap_weights,
    lst_delay, fringe_rate,
):
    vis = jnp.transpose(visibilities[:, 0], (0, 2, 1, 3))
    gains = jnp.transpose(antenna_gain_table, (0, 2, 1, 3))
    weights = jnp.transpose(tap_weights[0], (1, 0))
    bas = jnp.transpose(baseline_antennas, (1, 0))

    vm = pl.BlockSpec(memory_space=pltpu.VMEM)
    hbm = pl.BlockSpec(memory_space=pltpu.HBM)
    D = pltpu.SemaphoreType.DMA
    msg = (STAGES, BINS, ROWS, HALF)
    landed, wt = pl.pallas_call(
        comm_kernel,
        out_shape=(
            jax.ShapeDtypeStruct((STAGES, DEVS, ROWS, WIDE), F32),
            jax.ShapeDtypeStruct((1, CH), F32),
        ),
        in_specs=[hbm] * 9,
        out_specs=(vm, vm),
        scratch_shapes=[
            pltpu.SMEM((1, BINS), I32),
            pltpu.SMEM((1,), I32),
            pltpu.SMEM((TAPS, BINS), F32),
            pltpu.SMEM((1, BINS), F32),
            pltpu.SMEM((4,), F32),
            pltpu.VMEM((2, SAMPLES, 4, CH), F32),
            pltpu.VMEM((SAMPLES, ROWS, CH), F32),
            pltpu.VMEM((STAGES, BINS, ROWS, WIDE), F32),
            pltpu.VMEM((STAGES, BINS, ROWS, WIDE), F32),
            pltpu.VMEM((4, 2, OWN_ANT, 1, GHALF), F32),
            pltpu.VMEM((4, 2, OWN_ANT, 1, GHALF), F32),
            pltpu.VMEM((8, 2, 4), I32),
            pltpu.VMEM((8, 2, 4), I32),
            pltpu.SMEM((8, 2, 4), I32),
            pltpu.SMEM((8, 2, 4), I32),
            pltpu.VMEM((8, 2, ROWS, GHALF), F32),
            pltpu.VMEM((8, 2, ROWS, GHALF), F32),
            pltpu.VMEM((8, 2, ROWS, GHALF), F32),
            pltpu.VMEM((8, 2, ROWS, GHALF), F32),
            pltpu.VMEM((2, ROWS, CH), F32),
            pltpu.VMEM((NIGHTS, 2, ROWS, WIDE), F32),
            pltpu.VMEM((NIGHTS, 1, CH), I32),
            pltpu.VMEM((NIGHTS, 1, HALF), I32),
            pltpu.VMEM((NIGHTS, 1, BINS), I32),
            pltpu.VMEM((NIGHTS, TAPS, BINS), F32),
            pltpu.SMEM((NIGHTS, 1, HALF), I32),
            pltpu.SMEM((NIGHTS, 1, BINS), I32),
            pltpu.SMEM((NIGHTS, TAPS, BINS), F32),
        ]
        + [pltpu.VMEM(msg, F32)] * 8
        + [pltpu.VMEM(msg[1:], F32)] * 2
        + [
            D((20,)), D((2, 4)), D((4,)), D((4,)), D((2, 8)), D((8,)), D((8,)), D((4, 4)), D((4, 4)),
            D((8,)), D((8,)), D((8,)), D((8,)), D((STAGES + 1, 4)), D((STAGES + 1, 4)), D((4,)), D((4,)),
            D((STAGES,)), D((STAGES,)),
        ],
        compiler_params=pltpu.CompilerParams(
            collective_id=0, has_side_effects=True, vmem_limit_bytes=40 * 1024 * 1024
        ),
        name="exchange",
    )(vis, gains, corrupted_sample_markers, tap_offsets, first_bin, weights, lst_delay, bas, fringe_rate)

    binned, weight_total = pl.pallas_call(
        final_kernel,
        out_shape=(jax.ShapeDtypeStruct((2, 4 * DEVS, CH), F32), jax.ShapeDtypeStruct((1, CH), F32)),
        in_specs=[vm, vm],
        out_specs=(vm, vm),
        compiler_params=pltpu.CompilerParams(vmem_limit_bytes=16 * 1024 * 1024),
        name="assemble",
    )(landed, wt)
    return binned.reshape(2, 1, 4 * DEVS, CH), weight_total


def solution(mesh):
    placed = (
        P(None, "night", "bl", None, None),
        P("night", None),
        P(None, "night", "bl", None),
        P("bl", None),
        P("night"),
        P("night", None),
        P("night", None, None),
        P("night", None),
        P("bl"),
    )
    return jax.shard_map(
        per_device,
        mesh=mesh,
        in_specs=placed,
        out_specs=(P(None, ("night", "bl"), None, None), P(("night", "bl"), None)),
        check_vma=False,
    )
```

```python
import functools
import math

import jax
import jax.numpy as jnp
import numpy as np
from jax import lax
from jax.experimental import pallas as pl
from jax.experimental.pallas import tpu as pltpu
from jax.sharding import PartitionSpec as P

MESH = pl.DeviceIdType.MESH
F32 = jnp.float32
I32 = jnp.int32

NIGHTS = 4
DEVS = 32
BINS = 32
ROWS = 8
CH = 768
SAMPLES = 30
TAPS = 4
OWN_ANT = 11
STAGES = 3
WIDE = 256
HALF = 128
GHALF = 384


def _fit(kind, terms):
    k = np.arange(200)
    u = 0.125 * (1 + np.cos(np.pi * (k + 0.5) / 200))
    r = np.sqrt(u)
    y = np.sin(2 * np.pi * r) / r if kind == "sin" else np.cos(2 * np.pi * r)
    cheb = np.polynomial.chebyshev.Chebyshev.fit(u, y, terms - 1, domain=[0, 0.25])
    return [float(v) for v in cheb.convert(kind=np.polynomial.Polynomial).coef]


SIN_C = _fit("sin", 8)
COS_C = _fit("cos", 8)


def horner(coef, u):
    acc = jnp.full_like(u, coef[-1])
    for c in coef[-2::-1]:
        acc = acc * u + c
    return acc


def swap4(v):
    return pltpu.roll(v, 4, 0)


def flag(cond):
    return jnp.where(cond, jnp.float32(1.0), jnp.float32(0.0))


def comm_kernel(
    vis, gains, flags_h, offs_h, first_h, weights_h, delay_h, bas_h, rate_h,
    out_ref, wt_ref,
    offs_s, first_s, weights_s, delay_s, rate_s, V, UV, Y, Y2, S, landed, gy, gx, bx_v, by_v, bx_s, by_s, m0, m1, c0, c1, G, GZ,
    zflags, zfirst, zoffs, zw, zfirst_s, zoffs_s, zw_s, s1p, s1n, s2p, s2n, r1p, r1n, r2p, r2n, r3p, r3n,
    local_sem, gsend, gyr, gxr, bsend, bxr, byr, msend, mrecv,
    send0, send1, recv0, recv1, zsend, zrecv, gzs, gzr, asend, arecv,
):
    n = lax.axis_index("night")
    me = lax.axis_index("bl")
    core = lax.rem(me, 2)
    x = lax.rem(me // 2, 4)
    y = me // 8

    def bl_of(yy, xx, cc):
        return (yy * 4 + xx) * 2 + cc

    def rcopy(src, dst, ss, rs, dev):
        return pltpu.make_async_remote_copy(
            src_ref=src, dst_ref=dst, send_sem=ss, recv_sem=rs, device_id=dev, device_id_type=MESH
        )

    load_vis = [
        pltpu.make_async_copy(
            vis.at[:, :, :, pl.ds(st * WIDE, WIDE)], V.at[:, :, :, pl.ds(st * WIDE, WIDE)], local_sem.at[20 + st]
        )
        for st in range(STAGES)
    ]
    own_gy = pltpu.make_async_copy(gains.at[:, :, :, pl.ds(0, GHALF)], gy.at[y], local_sem.at[1])
    own_gx = pltpu.make_async_copy(gains.at[:, :, :, pl.ds(GHALF, GHALF)], gx.at[x], local_sem.at[2])
    small = [
        pltpu.make_async_copy(a, b, local_sem.at[7 + i])
        for i, (a, b) in enumerate(
            (
                (first_h, first_s), (offs_h, offs_s), (weights_h, weights_s), (delay_h, delay_s), (rate_h, rate_s),
                (flags_h, zflags.at[n]), (offs_h, zoffs.at[n]), (weights_h, zw.at[n]),
                (bas_h, bx_v.at[x * 2 + core]), (bas_h, by_v.at[y * 2 + core]),
            )
        )
    ]
    for c in (*small, *load_vis, own_gy, own_gx):
        c.start()

    barrier = pltpu.get_barrier_semaphore()

    def greet(device):
        pl.semaphore_signal(barrier, inc=1, device_id=device, device_id_type=MESH)

    for k in (1, 2, 3):
        greet((lax.rem(n + k, 4), me))
    greet((n, bl_of(y, x, 1 - core)))
    for k in (1, 2, 3):
        for cc in range(2):
            greet((n, bl_of(y, lax.rem(x + k, 4), cc)))
            greet((n, bl_of(lax.rem(y + k, 4), x, cc)))
    pl.semaphore_wait(barrier, 16)

    def gain_a(k):
        ty = lax.rem(y + k, 4)
        tx = lax.rem(x + k, 4)
        return (
            rcopy(gains.at[:, :, :, pl.ds(0, GHALF)], gy.at[y], gsend.at[0, k], gyr.at[y], (n, bl_of(ty, x, core))),
            rcopy(gains.at[:, :, :, pl.ds(GHALF, GHALF)], gx.at[x], gsend.at[1, k], gxr.at[x], (n, bl_of(y, tx, core))),
        )

    def slot_dev(k, own):
        s = lax.rem(own + k, 8)
        return s, s // 2, lax.rem(s, 2)

    def bas_x(k):
        s, tx, tc = slot_dev(k, x * 2 + core)
        mine = x * 2 + core
        return rcopy(bas_h, bx_v.at[mine], bsend.at[0, k], bxr.at[mine], (n, bl_of(y, tx, tc)))

    def bas_y(k):
        s, ty, tc = slot_dev(k, y * 2 + core)
        mine = y * 2 + core
        return rcopy(bas_h, by_v.at[mine], bsend.at[1, k], byr.at[mine], (n, bl_of(ty, x, tc)))

    def start_bas(k, _):
        bas_x(k).start()
        bas_y(k).start()
        return _

    lax.fori_loop(1, 8, start_bas, 0)
    for k in (1, 3, 2):
        for c in gain_a(k):
            c.start()

    for c in small:
        c.wait()
    first = first_s[0]
    zfirst[n] = jnp.full((1, HALF), first, I32)

    def meta(k):
        t = lax.rem(n + k, 4)
        return [
            rcopy(a, b, msend.at[i, k], mrecv.at[i, n], (t, me))
            for i, (a, b) in enumerate(
                (
                    (flags_h, zflags.at[n]), (offs_h, zoffs.at[n]), (weights_h, zw.at[n]),
                    (zfirst.at[n], zfirst.at[n]),
                )
            )
        ]

    def shift_of(f, night, e):
        return (lax.shift_right_logical(f, 5) + jnp.where(e < (f & 31), 1, 0) - night) & 3

    lane = lax.broadcasted_iota(I32, (ROWS, WIDE), 1).astype(F32)
    row = lax.broadcasted_iota(I32, (ROWS, WIDE), 0)
    sign = jnp.where(row < 4, jnp.float32(-1.0), jnp.float32(1.0))

    which = row & 3
    rates = jnp.where(
        which < 2, jnp.where(which == 0, rate_s[0], rate_s[1]), jnp.where(which == 2, rate_s[2], rate_s[3])
    ) * (1.0 / (2.0 * math.pi))

    def prepare(st):
        at = st * WIDE
        load_vis[st].wait()

        def per_sample(t, _):
            bits = (zflags[n, :, pl.ds(at, WIDE)] >> t) & 1
            both = jnp.concatenate([V[0, t, :, pl.ds(at, WIDE)], V[1, t, :, pl.ds(at, WIDE)]], axis=0)
            UV[t, :, pl.ds(at, WIDE)] = both * (1.0 - bits.astype(F32))
            return _

        lax.fori_loop(0, SAMPLES, per_sample, 0)
        freq = 1.0 + (lane + float(at)) * (1.0 / CH)
        rate = rates * freq

        def per_bin(e, _):
            l = (e - first) & 31
            off = offs_s[0, l]
            acc = weights_s[0, l] * UV[off, :, pl.ds(at, WIDE)]
            for k in range(1, TAPS):
                acc = acc + weights_s[k, l] * UV[off + k, :, pl.ds(at, WIDE)]
            turns = rate * delay_s[0, l]
            r = turns - jnp.floor(turns + 0.5)
            u = r * r
            sine = horner(SIN_C, u) * (r * sign)
            cosine = horner(COS_C, u)
            Y[st, e] = cosine * acc + sine * swap4(acc)
            return _

        lax.fori_loop(0, BINS, per_bin, 0)

    up = lax.rem(n + 1, 4)
    down = lax.rem(n + 3, 4)
    far = lax.rem(n + 2, 4)

    def zcopy(st, which):
        src = (s1p, s1n, s2p, s2n)[which]
        dst = (r1p, r1n, r2p, r2n)[which]
        to = up if which % 2 == 0 else down
        return rcopy(src.at[st], dst.at[st], zsend.at[st, which], zrecv.at[st, which], (to, me))

    def forward(which):
        src, dst = ((r1p, r3p), (r1n, r3n))[which]
        to = (up, down)[which]
        return rcopy(src.at[0], dst, zsend.at[STAGES, which], zrecv.at[STAGES, which], (to, me))

    lo = pl.ds(0, HALF)
    hi = pl.ds(HALF, HALF)

    def build_first(st):
        def per_bin(e, _):
            s = shift_of(first, n, e)
            a, b = Y[st, e, :, lo], Y[st, e, :, hi]
            two = flag(s == 2)
            s1p[st, e] = two * a + flag(s == 1) * b
            s1n[st, e] = two * b + flag(s == 3) * a
            return _

        lax.fori_loop(0, BINS, per_bin, 0)

    prepare(0)
    build_first(0)
    zcopy(0, 0).start()
    zcopy(0, 1).start()

    def early_second(e, _):
        s = shift_of(first, n, e)
        s2p[0, e] = flag(s == 1) * Y[0, e, :, lo]
        s2n[0, e] = flag(s == 3) * Y[0, e, :, hi]
        return _

    lax.fori_loop(0, BINS, early_second, 0)
    zcopy(0, 2).start()
    zcopy(0, 3).start()

    for k in (1, 3, 2):
        for c in meta(k):
            c.start()

    def wait_bas(k, _):
        sx = lax.rem(x * 2 + core + k, 8)
        sy = lax.rem(y * 2 + core + k, 8)
        rcopy(bas_h, bx_v.at[sx], bsend.at[0, k], bxr.at[sx], (n, me)).wait_recv()
        rcopy(bas_h, by_v.at[sy], bsend.at[1, k], byr.at[sy], (n, me)).wait_recv()
        return _

    lax.fori_loop(1, 8, wait_bas, 0)
    to_s0 = pltpu.make_async_copy(bx_v, bx_s, local_sem.at[3])
    to_s1 = pltpu.make_async_copy(by_v, by_s, local_sem.at[4])
    to_s0.start()
    to_s1.start()
    own_gy.wait()
    own_gx.wait()
    for k in (1, 2, 3):
        sy, sx = lax.rem(y + k, 4), lax.rem(x + k, 4)
        rcopy(gy.at[sy], gy.at[sy], gsend.at[0, k], gyr.at[sy], (n, me)).wait_recv()
        rcopy(gx.at[sx], gx.at[sx], gsend.at[1, k], gxr.at[sx], (n, me)).wait_recv()
    to_s0.wait()
    to_s1.wait()

    def pick(slot, asked, table, out, mine_a, along):
        for r in range(ROWS):
            a = asked[slot, r // 4, r % 4]
            owner = a // OWN_ANT
            at = a - owner * OWN_ANT
            oc = owner & 1
            ox = (owner >> 1) & 3
            oy = owner >> 3
            fixed, moving = (ox, oy) if along == 0 else (oy, ox)
            w = flag((fixed == mine_a) & (oc == core))
            for p in range(2):
                out[slot, p, pl.ds(r, 1), :] = w * table[moving, p, at]

    def gain_b0(k):
        s, tx, tc = slot_dev(k, x * 2 + core)
        mine = x * 2 + core
        return rcopy(m0.at[s], c0.at[mine], send0.at[k], recv0.at[mine], (n, bl_of(y, tx, tc)))

    def gain_b1(k):
        s, ty, tc = slot_dev(k, y * 2 + core)
        mine = y * 2 + core
        return rcopy(m1.at[s], c1.at[mine], send1.at[k], recv1.at[mine], (n, bl_of(ty, x, tc)))

    def send_rows(k, _):
        pick(lax.rem(x * 2 + core + k, 8), bx_s, gy, m0, x, 0)
        gain_b0(k).start()
        pick(lax.rem(y * 2 + core + k, 8), by_s, gx, m1, y, 1)
        gain_b1(k).start()
        return _

    lax.fori_loop(1, 8, send_rows, 0)
    pick(x * 2 + core, bx_s, gy, m0, x, 0)
    pick(y * 2 + core, by_s, gx, m1, y, 1)
    c0[x * 2 + core] = m0[x * 2 + core]
    c1[y * 2 + core] = m1[y * 2 + core]

    for k in (1, 2, 3):
        o = lax.rem(n + k, 4)
        for i, (a, b) in enumerate(
            ((flags_h, zflags.at[o]), (offs_h, zoffs.at[o]), (weights_h, zw.at[o]), (zfirst.at[o], zfirst.at[o]))
        ):
            rcopy(a, b, msend.at[i, k], mrecv.at[i, o], (n, me)).wait_recv()
    to_smem = [
        pltpu.make_async_copy(a, b, local_sem.at[17 + i])
        for i, (a, b) in enumerate(((zoffs, zoffs_s), (zw, zw_s), (zfirst, zfirst_s)))
    ]
    for c in to_smem:
        c.start()

    for w in (0, 1):
        zcopy(0, w).wait_recv()
        forward(w).start()

    prepare(1)
    prepare(2)

    def wait_rows(k, _):
        sx = lax.rem(x * 2 + core + k, 8)
        sy = lax.rem(y * 2 + core + k, 8)
        rcopy(m0.at[sx], c0.at[sx], send0.at[k], recv0.at[sx], (n, me)).wait_recv()
        rcopy(m1.at[sy], c1.at[sy], send1.at[k], recv1.at[sy], (n, me)).wait_recv()
        return _

    lax.fori_loop(1, 8, wait_rows, 0)
    for h, c in ((0, c0), (1, c1)):
        parts = []
        for p in range(2):
            acc = c[0, p]
            for s in range(1, 8):
                acc = acc + c[s, p]
            parts.append(acc)
        A, B = parts
        G[0, :, pl.ds(h * GHALF, GHALF)] = A * swap4(A) + B * swap4(B)
        G[1, :, pl.ds(h * GHALF, GHALF)] = A * swap4(B) - B * swap4(A)
    GZ[n] = G[:, :, pl.ds(0, WIDE)]

    def gz(k):
        return rcopy(GZ.at[n], GZ.at[n], gzs.at[k], gzr.at[n], (lax.rem(n + k, 4), me))

    for k in (1, 3, 2):
        gz(k).start()

    def with_gain(st, build):
        gr, gs = G[0, :, pl.ds(st * WIDE, WIDE)], G[1, :, pl.ds(st * WIDE, WIDE)]

        def per_bin(e, _):
            v = Y[st, e]
            v = gr * v + gs * swap4(v)
            Y[st, e] = v
            if build:
                first_message(st, e, shift_of(first, n, e), v[:, :HALF], v[:, HALF:])
            return _

        lax.fori_loop(0, BINS, per_bin, 0)

    def first_message(st, e, s, a, b):
        two = flag(s == 2)
        s1p[st, e] = two * a + flag(s == 1) * b
        s1n[st, e] = two * b + flag(s == 3) * a

    def bin_copy(st, k):
        t = lax.rem(me + k, DEVS)
        if st == 2:
            return rcopy(Y.at[2, t], Y2.at[me], asend.at[2], arecv.at[2], (n, t))
        return rcopy(S.at[st, t], landed.at[st, me], asend.at[st], arecv.at[st], (n, t))

    def send_bins(st):
        def go(k, _):
            bin_copy(st, k).start()
            return _

        lax.fori_loop(1, DEVS, go, 0)
        if st == 2:
            Y2[me] = Y[2, me]
        else:
            landed[st, me] = S[st, me]

    def all_bins(st):
        part = pl.ds(0, DEVS - 1)
        if st == 2:
            return rcopy(Y.at[2, part], Y2.at[part], asend.at[2], arecv.at[2], (n, me))
        return rcopy(S.at[st, part], landed.at[st, part], asend.at[st], arecv.at[st], (n, me))

    with_gain(1, True)
    zcopy(1, 0).start()
    zcopy(1, 1).start()
    with_gain(2, False)
    send_bins(2)

    for c in to_smem:
        c.wait()
    first_down, first_up, first_far = zfirst_s[down, 0, 0], zfirst_s[up, 0, 0], zfirst_s[far, 0, 0]
    total = jnp.zeros((1, CH), F32)
    bin_here = n * BINS + me
    for k in range(NIGHTS):
        l = bin_here - zfirst_s[k, 0, 0]
        valid = flag((l >= 0) & (l < BINS))
        lc = jnp.clip(l, 0, BINS - 1)
        off = zoffs_s[k, 0, lc]
        for t in range(TAPS):
            bits = (zflags[k] >> (off + t)) & 1
            total = total + (valid * zw_s[k, t, lc]) * (1.0 - bits.astype(F32))
    wt_ref[...] = total
    scale = 1.0 / jnp.maximum(total, 0.5)

    def put(st, k, a, b, inv):
        a, b = a * inv, b * inv
        low = row < 4
        at = pl.multiple_of(k * 8, 8)
        cols = pl.ds(st * WIDE, WIDE)
        out_ref[0, pl.ds(at, 8), cols] = jnp.where(low, a, swap4(b))
        out_ref[1, pl.ds(at, 8), cols] = jnp.where(low, swap4(a), b)

    def scale_of(st):
        return jnp.broadcast_to(scale[:, st * WIDE : (st + 1) * WIDE], (ROWS, WIDE))

    for k in (1, 2, 3):
        o = lax.rem(n + k, 4)
        rcopy(GZ.at[o], GZ.at[o], gzs.at[k], gzr.at[o], (n, me)).wait_recv()
    zcopy(0, 2).wait_recv()
    zcopy(0, 3).wait_recv()
    forward(0).wait_recv()
    forward(1).wait_recv()

    def combine0(e, _):
        here = flag(shift_of(first, n, e) == 0)
        from_down = flag(shift_of(first_down, down, e) == 1)
        from_up = flag(shift_of(first_up, up, e) == 3)
        from_far = flag(shift_of(first_far, far, e) == 2)

        def part(half, terms):
            acc = None
            for night, v in terms:
                w = GZ[night, 0, :, half] * v + GZ[night, 1, :, half] * swap4(v)
                acc = w if acc is None else acc + w
            S[0, e, :, half] = acc

        part(lo, ((n, here * Y[0, e, :, lo]), (up, from_up * r1n[0, e]), (down, r2p[0, e]), (far, from_far * r3p[e])))
        part(hi, ((n, here * Y[0, e, :, hi]), (down, from_down * r1p[0, e]), (up, r2n[0, e]), (far, from_far * r3n[e])))
        return _

    lax.fori_loop(0, BINS, combine0, 0)
    send_bins(0)

    def second_message(st, i, e, a, b):
        s = shift_of(first, n, e)
        s2p[st, i] = flag(s == 1) * a + flag(shift_of(first_down, down, e) == 2) * r1p[st, i]
        s2n[st, i] = flag(s == 3) * b + flag(shift_of(first_up, up, e) == 2) * r1n[st, i]

    def merged(st, i, e, a, b):
        here = flag(shift_of(first, n, e) == 0)
        from_down = flag(shift_of(first_down, down, e) == 1)
        from_up = flag(shift_of(first_up, up, e) == 3)
        return (
            here * a + from_up * r1n[st, i] + r2p[st, i],
            here * b + from_down * r1p[st, i] + r2n[st, i],
        )

    zcopy(1, 0).wait_recv()
    zcopy(1, 1).wait_recv()

    def second1(e, _):
        second_message(1, e, e, Y[1, e, :, lo], Y[1, e, :, hi])
        return _

    lax.fori_loop(0, BINS, second1, 0)
    zcopy(1, 2).start()
    zcopy(1, 3).start()

    all_bins(2).wait_recv()

    def first2(d, _):
        first_message(2, d, shift_of(first, n, me), Y2[d, :, lo], Y2[d, :, hi])
        return _

    lax.fori_loop(0, DEVS, first2, 0)
    zcopy(2, 0).start()
    zcopy(2, 1).start()

    zcopy(1, 2).wait_recv()
    zcopy(1, 3).wait_recv()

    def combine1(e, _):
        a, b = merged(1, e, e, Y[1, e, :, lo], Y[1, e, :, hi])
        S[1, e, :, lo] = a
        S[1, e, :, hi] = b
        return _

    lax.fori_loop(0, BINS, combine1, 0)
    send_bins(1)

    zcopy(2, 0).wait_recv()
    zcopy(2, 1).wait_recv()

    def second2(d, _):
        second_message(2, d, me, Y2[d, :, lo], Y2[d, :, hi])
        return _

    lax.fori_loop(0, DEVS, second2, 0)
    zcopy(2, 2).start()
    zcopy(2, 3).start()

    for st in (0, 1):
        all_bins(st).wait_recv()
        inv = scale_of(st)

        def assemble(k, _, st=st, inv=inv):
            put(st, k, landed[st, 2 * k], landed[st, 2 * k + 1], inv)
            return _

        lax.fori_loop(0, DEVS // 2, assemble, 0)

    zcopy(2, 2).wait_recv()
    zcopy(2, 3).wait_recv()
    inv2 = scale_of(2)

    def finish(k, _):
        pair = []
        for d in (2 * k, 2 * k + 1):
            a, b = merged(2, d, me, Y2[d, :, lo], Y2[d, :, hi])
            pair.append(jnp.concatenate([a, b], axis=1))
        put(2, k, pair[0], pair[1], inv2)
        return _

    lax.fori_loop(0, DEVS // 2, finish, 0)

    for k in (1, 2, 3):
        for c in gain_a(k):
            c.wait_send()
        for c in meta(k):
            c.wait_send()
        gz(k).wait_send()

    def done(k, _):
        bas_x(k).wait_send()
        bas_y(k).wait_send()
        gain_b0(k).wait_send()
        gain_b1(k).wait_send()
        return _

    lax.fori_loop(1, 8, done, 0)
    for st in range(STAGES):
        for w in range(4):
            zcopy(st, w).wait_send()
    for w in (0, 1):
        forward(w).wait_send()
    for st in range(STAGES):
        all_bins(st).wait_send()


def per_device(
    visibilities, corrupted_sample_markers, antenna_gain_table, baseline_antennas, first_bin, tap_offsets, tap_weights,
    lst_delay, fringe_rate,
):
    vis = jnp.transpose(visibilities[:, 0], (0, 2, 1, 3))
    gains = jnp.transpose(antenna_gain_table, (0, 2, 1, 3))
    weights = jnp.transpose(tap_weights[0], (1, 0))
    bas = jnp.transpose(baseline_antennas, (1, 0))

    def held(a):
        return pltpu.with_memory_space_constraint(a, pltpu.HBM)

    vm = pl.BlockSpec(memory_space=pltpu.VMEM)
    hbm = pl.BlockSpec(memory_space=pltpu.HBM)
    D = pltpu.SemaphoreType.DMA
    msg = (STAGES, BINS, ROWS, HALF)
    binned, weight_total = pl.pallas_call(
        comm_kernel,
        out_shape=(
            pltpu.VMEM((2, 4 * DEVS, CH), F32),
            jax.ShapeDtypeStruct((1, CH), F32),
        ),
        in_specs=[hbm] * 9,
        out_specs=(vm, vm),
        scratch_shapes=[
            pltpu.SMEM((1, BINS), I32),
            pltpu.SMEM((1,), I32),
            pltpu.SMEM((TAPS, BINS), F32),
            pltpu.SMEM((1, BINS), F32),
            pltpu.SMEM((4,), F32),
            pltpu.VMEM((2, SAMPLES, 4, CH), F32),
            pltpu.VMEM((SAMPLES, ROWS, CH), F32),
            pltpu.VMEM((STAGES, BINS, ROWS, WIDE), F32),
            pltpu.VMEM((DEVS, ROWS, WIDE), F32),
            pltpu.VMEM((2, BINS, ROWS, WIDE), F32),
            pltpu.VMEM((2, DEVS, ROWS, WIDE), F32),
            pltpu.VMEM((4, 2, OWN_ANT, 1, GHALF), F32),
            pltpu.VMEM((4, 2, OWN_ANT, 1, GHALF), F32),
            pltpu.VMEM((8, 2, 4), I32),
            pltpu.VMEM((8, 2, 4), I32),
            pltpu.SMEM((8, 2, 4), I32),
            pltpu.SMEM((8, 2, 4), I32),
            pltpu.VMEM((8, 2, ROWS, GHALF), F32),
            pltpu.VMEM((8, 2, ROWS, GHALF), F32),
            pltpu.VMEM((8, 2, ROWS, GHALF), F32),
            pltpu.VMEM((8, 2, ROWS, GHALF), F32),
            pltpu.VMEM((2, ROWS, CH), F32),
            pltpu.VMEM((NIGHTS, 2, ROWS, WIDE), F32),
            pltpu.VMEM((NIGHTS, 1, CH), I32),
            pltpu.VMEM((NIGHTS, 1, HALF), I32),
            pltpu.VMEM((NIGHTS, 1, BINS), I32),
            pltpu.VMEM((NIGHTS, TAPS, BINS), F32),
            pltpu.SMEM((NIGHTS, 1, HALF), I32),
            pltpu.SMEM((NIGHTS, 1, BINS), I32),
            pltpu.SMEM((NIGHTS, TAPS, BINS), F32),
        ]
        + [pltpu.VMEM(msg, F32)] * 8
        + [pltpu.VMEM(msg[1:], F32)] * 2
        + [
            D((23,)), D((2, 4)), D((4,)), D((4,)), D((2, 8)), D((8,)), D((8,)), D((4, 4)), D((4, 4)),
            D((8,)), D((8,)), D((8,)), D((8,)), D((STAGES + 1, 4)), D((STAGES + 1, 4)), D((4,)), D((4,)),
            D((STAGES,)), D((STAGES,)),
        ],
        compiler_params=pltpu.CompilerParams(
            collective_id=0, has_side_effects=True, vmem_limit_bytes=48 * 1024 * 1024
        ),
        name="exchange",
    )(
        held(vis), held(gains), held(corrupted_sample_markers), held(tap_offsets), first_bin, held(weights),
        held(lst_delay), held(bas), held(fringe_rate),
    )
    return binned.reshape(2, 1, 4 * DEVS, CH), weight_total


def solution(mesh):
    placed = (
        P(None, "night", "bl", None, None),
        P("night", None),
        P(None, "night", "bl", None),
        P("bl", None),
        P("night"),
        P("night", None),
        P("night", None, None),
        P("night", None),
        P("bl"),
    )
    return jax.shard_map(
        per_device,
        mesh=mesh,
        in_specs=placed,
        out_specs=(P(None, ("night", "bl"), None, None), P(("night", "bl"), None)),
        check_vma=False,
    )
```

```python
import functools
import math

import jax
import jax.numpy as jnp
import numpy as np
from jax import lax
from jax.experimental import pallas as pl
from jax.experimental.pallas import tpu as pltpu
from jax.sharding import PartitionSpec as P

MESH = pl.DeviceIdType.MESH
F32 = jnp.float32
I32 = jnp.int32

NIGHTS = 4
DEVS = 32
BINS = 32
ROWS = 8
CH = 768
SAMPLES = 30
TAPS = 4
OWN_ANT = 11
STAGES = 3
WIDE = 256
HALF = 128
SOON = 128
LATER = 256
EARLY = 512
HB = 16


def _fit(kind, terms):
    k = np.arange(200)
    u = 0.125 * (1 + np.cos(np.pi * (k + 0.5) / 200))
    r = np.sqrt(u)
    y = np.sin(2 * np.pi * r) / r if kind == "sin" else np.cos(2 * np.pi * r)
    cheb = np.polynomial.chebyshev.Chebyshev.fit(u, y, terms - 1, domain=[0, 0.25])
    return [float(v) for v in cheb.convert(kind=np.polynomial.Polynomial).coef]


SIN_C = _fit("sin", 8)
COS_C = _fit("cos", 8)


def horner(coef, u):
    acc = jnp.full_like(u, coef[-1])
    for c in coef[-2::-1]:
        acc = acc * u + c
    return acc


def swap4(v):
    return pltpu.roll(v, 4, 0)


def flag(cond):
    return jnp.where(cond, jnp.float32(1.0), jnp.float32(0.0))


def comm_kernel(
    vis, gains, flags_h, offs_h, first_h, weights_h, delay_h, bas_h, rate_h,
    out_ref, wt_ref,
    offs_s, first_s, weights_s, delay_s, rate_s, V, UV, Y, Y2, S, landed, gyu, gxu, gyl, gxl, bx_v, by_v, bx_s, by_s,
    m0, m1, c0, c1, q0, q1, d0, d1, G, GP, GZ,
    zflags, zfirst, zoffs, zw, zfirst_s, zoffs_s, zw_s, s1p, s1n, s2p, s2n, r1p, r1n, r2p, r2n, r3p, r3n,
    local_sem, gsend, grecv, bsend, bxr, byr, msend, mrecv,
    rsend, rrecv, zsend, zrecv, gzs, gzr, asend, arecv,
):
    n = lax.axis_index("night")
    me = lax.axis_index("bl")
    core = lax.rem(me, 2)
    x = lax.rem(me // 2, 4)
    y = me // 8

    def bl_of(yy, xx, cc):
        return (yy * 4 + xx) * 2 + cc

    def rcopy(src, dst, ss, rs, dev):
        return pltpu.make_async_remote_copy(
            src_ref=src, dst_ref=dst, send_sem=ss, recv_sem=rs, device_id=dev, device_id_type=MESH
        )

    def loop(count, body, unroll=4, start=0):
        def step(i, c):
            body(i)
            return c

        lax.fori_loop(start, count, step, 0, unroll=unroll)

    load_vis = [
        pltpu.make_async_copy(
            vis.at[:, :, :, pl.ds(st * WIDE, WIDE)], V.at[:, :, :, pl.ds(st * WIDE, WIDE)], local_sem.at[st]
        )
        for st in range(STAGES)
    ]

    def table(which, late):
        begin = ((512, 640), (0, 256))[late][which]
        return gains.at[:, :, :, pl.ds(begin, LATER if late else SOON)], ((gyu, gxu), (gyl, gxl))[late][which]

    own_gains = []
    for late in (0, 1):
        for which in (0, 1):
            src, dst = table(which, late)
            own_gains.append(pltpu.make_async_copy(src, dst.at[(y, x)[which]], local_sem.at[3 + 2 * late + which]))
    small = [
        pltpu.make_async_copy(a, b, local_sem.at[7 + i])
        for i, (a, b) in enumerate(
            (
                (first_h, first_s), (offs_h, offs_s), (weights_h, weights_s), (delay_h, delay_s), (rate_h, rate_s),
                (flags_h, zflags.at[n]), (offs_h, zoffs.at[n]), (weights_h, zw.at[n]),
                (bas_h, bx_v.at[x * 2 + core]), (bas_h, by_v.at[y * 2 + core]),
            )
        )
    ]
    for c in (load_vis[0], *small[:6]):
        c.start()

    barrier = pltpu.get_barrier_semaphore()

    def greet(device):
        pl.semaphore_signal(barrier, inc=1, device_id=device, device_id_type=MESH)

    for k in (1, 2, 3):
        greet((lax.rem(n + k, 4), me))
    greet((n, bl_of(y, x, 1 - core)))
    for k in (1, 2, 3):
        for cc in range(2):
            greet((n, bl_of(y, lax.rem(x + k, 4), cc)))
            greet((n, bl_of(lax.rem(y + k, 4), x, cc)))
    for c in (*small[6:], *own_gains, *load_vis[1:]):
        c.start()

    lane = lax.broadcasted_iota(I32, (ROWS, WIDE), 1).astype(F32)
    row = lax.broadcasted_iota(I32, (ROWS, WIDE), 0)
    sign = jnp.where(row < 4, jnp.float32(-1.0), jnp.float32(1.0))
    for c in small[:6]:
        c.wait()
    first = first_s[0]
    zfirst[n] = jnp.full((1, HALF), first, I32)
    which_row = row & 3
    rates = jnp.where(
        which_row < 2,
        jnp.where(which_row == 0, rate_s[0], rate_s[1]),
        jnp.where(which_row == 2, rate_s[2], rate_s[3]),
    ) * (1.0 / (2.0 * math.pi))

    def samples(st):
        at = st * WIDE
        load_vis[st].wait()

        def per_sample(t):
            bits = (zflags[n, :, pl.ds(at, WIDE)] >> t) & 1
            both = jnp.concatenate([V[0, t, :, pl.ds(at, WIDE)], V[1, t, :, pl.ds(at, WIDE)]], axis=0)
            UV[t, :, pl.ds(at, WIDE)] = both * (1.0 - bits.astype(F32))

        loop(SAMPLES, per_sample, unroll=5)

    def shift_of(f, night, e):
        return (lax.shift_right_logical(f, 5) + jnp.where(e < (f & 31), 1, 0) - night) & 3

    def phases(st):
        return rates * (1.0 + (lane + float(st * WIDE)) * (1.0 / CH))

    def turned(st, rate, e):
        at = st * WIDE
        l = (e - first) & 31
        off = offs_s[0, l]
        acc = weights_s[0, l] * UV[off, :, pl.ds(at, WIDE)]
        for k in range(1, TAPS):
            acc = acc + weights_s[k, l] * UV[off + k, :, pl.ds(at, WIDE)]
        turns = rate * delay_s[0, l]
        r = turns - jnp.floor(turns + 0.5)
        u = r * r
        return horner(COS_C, u) * acc + (horner(SIN_C, u) * (r * sign)) * swap4(acc)

    up = lax.rem(n + 1, 4)
    down = lax.rem(n + 3, 4)
    far = lax.rem(n + 2, 4)

    def zcopy(st, which, h):
        src = (s1p, s1n, s2p, s2n)[which].at[st, pl.ds(h * HB, HB)]
        dst = (r1p, r1n, r2p, r2n)[which].at[st, pl.ds(h * HB, HB)]
        to = up if which % 2 == 0 else down
        return rcopy(src, dst, zsend.at[st, which, h], zrecv.at[st, which, h], (to, me))

    def forward(st, which, h):
        src, dst = ((r1p, r3p), (r1n, r3n))[which]
        part = pl.ds(h * HB, HB)
        to = (up, down)[which]
        return rcopy(
            src.at[st, part], dst.at[st, part], zsend.at[STAGES + st, which, h], zrecv.at[STAGES + st, which, h], (to, me)
        )

    lo = pl.ds(0, HALF)
    hi = pl.ds(HALF, HALF)

    def first_message(st, i, s, a, b):
        two = flag(s == 2)
        s1p[st, i] = two * a + flag(s == 1) * b
        s1n[st, i] = two * b + flag(s == 3) * a

    def second_message(st, i, e, a, b):
        s = shift_of(first, n, e)
        s2p[st, i] = flag(s == 1) * a + flag(shift_of(first_down, down, e) == 2) * r1p[st, i]
        s2n[st, i] = flag(s == 3) * b + flag(shift_of(first_up, up, e) == 2) * r1n[st, i]

    def early(st):
        samples(st)
        rate = phases(st)

        def per_bin(e):
            v = turned(st, rate, e)
            Y[st, e] = v
            a, b = v[:, :HALF], v[:, HALF:]
            s = shift_of(first, n, e)
            first_message(st, e, s, a, b)
            s2p[st, e] = flag(s == 1) * a
            s2n[st, e] = flag(s == 3) * b

        loop(BINS, per_bin)

    def start_early(st, message):
        for h in (0, 1):
            for w in (0, 1):
                zcopy(st, 2 * message + w, h).start()

    early(0)
    pl.semaphore_wait(barrier, 16)
    start_early(0, 0)
    start_early(0, 1)
    for c in (*small[6:], *own_gains):
        c.wait()

    def gain_a(which, late, k):
        _, tab = table(which, late)
        mine = (y, x)[which]
        to = bl_of(lax.rem(y + k, 4), x, core) if which == 0 else bl_of(y, lax.rem(x + k, 4), core)
        return rcopy(tab.at[mine], tab.at[mine], gsend.at[which, late, k], grecv.at[which, late, mine], (n, to))

    def gain_a_wait(which, late):
        _, tab = table(which, late)
        for k in (1, 2, 3):
            o = lax.rem((y, x)[which] + k, 4)
            rcopy(tab.at[o], tab.at[o], gsend.at[which, late, k], grecv.at[which, late, o], (n, me)).wait_recv()

    def slot_dev(k, own):
        s = lax.rem(own + k, 8)
        return s, s // 2, lax.rem(s, 2)

    def bas_x(k):
        s, tx, tc = slot_dev(k, x * 2 + core)
        mine = x * 2 + core
        return rcopy(bx_v.at[mine], bx_v.at[mine], bsend.at[0, k], bxr.at[mine], (n, bl_of(y, tx, tc)))

    def bas_y(k):
        s, ty, tc = slot_dev(k, y * 2 + core)
        mine = y * 2 + core
        return rcopy(by_v.at[mine], by_v.at[mine], bsend.at[1, k], byr.at[mine], (n, bl_of(ty, x, tc)))

    for k in (1, 3, 2):
        for which in (0, 1):
            gain_a(which, 0, k).start()

    def start_bas(k):
        bas_x(k).start()
        bas_y(k).start()

    loop(8, start_bas, unroll=1, start=1)
    for k in (1, 3, 2):
        for which in (0, 1):
            gain_a(which, 1, k).start()
    early(1)
    start_early(1, 0)

    def meta(k):
        t = lax.rem(n + k, 4)
        return [
            rcopy(a, b, msend.at[i, k], mrecv.at[i, n], (t, me))
            for i, (a, b) in enumerate(
                (
                    (zflags.at[n], zflags.at[n]), (zoffs.at[n], zoffs.at[n]), (zw.at[n], zw.at[n]),
                    (zfirst.at[n], zfirst.at[n]),
                )
            )
        ]

    def wait_bas(k):
        sx = lax.rem(x * 2 + core + k, 8)
        sy = lax.rem(y * 2 + core + k, 8)
        rcopy(bx_v.at[sx], bx_v.at[sx], bsend.at[0, k], bxr.at[sx], (n, me)).wait_recv()
        rcopy(by_v.at[sy], by_v.at[sy], bsend.at[1, k], byr.at[sy], (n, me)).wait_recv()

    loop(8, wait_bas, unroll=1, start=1)
    to_s0 = pltpu.make_async_copy(bx_v, bx_s, local_sem.at[17])
    to_s1 = pltpu.make_async_copy(by_v, by_s, local_sem.at[18])
    to_s0.start()
    to_s1.start()
    gain_a_wait(0, 0)
    gain_a_wait(1, 0)
    to_s0.wait()
    to_s1.wait()

    slots = (lambda k: lax.rem(x * 2 + core + k, 8), lambda k: lax.rem(y * 2 + core + k, 8))
    asked_of = (bx_s, by_s)
    mine_of = (x * 2 + core, y * 2 + core)

    def pick(which, late, slot):
        out = ((m0, m1), (q0, q1))[late][which]
        _, tab = table(which, late)
        for r in range(ROWS):
            a = asked_of[which][slot, r // 4, r % 4]
            owner = lax.shift_right_logical(a * 5958, 16)
            at = a - owner * OWN_ANT
            ox, oy = (owner >> 1) & 3, owner >> 3
            fixed, moving, here = (ox, oy, x) if which == 0 else (oy, ox, y)
            w = flag((fixed == here) & ((owner & 1) == core))
            for p in range(2):
                out[slot, p, pl.ds(r, 1), :] = w * tab[moving, p, at]

    def gain_b(which, late, k):
        s, t, tc = slot_dev(k, mine_of[which])
        src = ((m0, m1), (q0, q1))[late][which]
        dst = ((c0, c1), (d0, d1))[late][which]
        to = bl_of(y, t, tc) if which == 0 else bl_of(t, x, tc)
        i = 2 * late + which
        return rcopy(src.at[s], dst.at[mine_of[which]], rsend.at[i, k], rrecv.at[i, mine_of[which]], (n, to))

    def send_rows(late):
        def go(k):
            for which in (0, 1):
                pick(which, late, slots[which](k))
                gain_b(which, late, k).start()

        loop(8, go, unroll=1, start=1)
        for which in (0, 1):
            pick(which, late, mine_of[which])
            dst = ((c0, c1), (d0, d1))[late][which]
            src = ((m0, m1), (q0, q1))[late][which]
            dst[mine_of[which]] = src[mine_of[which]]

    def gain_products(late):
        def wait(k):
            for which in (0, 1):
                s = slots[which](k)
                src = ((m0, m1), (q0, q1))[late][which]
                dst = ((c0, c1), (d0, d1))[late][which]
                i = 2 * late + which
                rcopy(src.at[s], dst.at[s], rsend.at[i, k], rrecv.at[i, s], (n, me)).wait_recv()

        loop(8, wait, unroll=1, start=1)
        for which in (0, 1):
            got = ((c0, c1), (d0, d1))[late][which]
            parts = []
            for p in range(2):
                acc = got[0, p]
                for s in range(1, 8):
                    acc = acc + got[s, p]
                parts.append(acc)
            A, B = parts
            cols = pl.ds(((512, 640), (0, 256))[late][which], LATER if late else SOON)
            G[0, :, cols] = A * swap4(A) + B * swap4(B)
            G[1, :, cols] = A * swap4(B) - B * swap4(A)

    send_rows(0)

    def pass_on(st):
        for h in (0, 1):
            for w in (0, 1):
                zcopy(st, w, h).wait_recv()
                forward(st, w, h).start()

    pass_on(0)
    start_early(1, 1)
    gain_a_wait(0, 1)
    gain_a_wait(1, 1)
    send_rows(1)
    for k in (1, 3, 2):
        for c in meta(k):
            c.start()

    samples(2)
    rate2 = phases(2)

    def last(e):
        Y[2, e] = turned(2, rate2, e)

    loop(BINS, last)
    gain_products(0)

    def bin_copy(st, t):
        if st >= 2:
            src = Y.at[2, t, :, pl.ds((st - 2) * HALF, HALF)]
            return rcopy(src, Y2.at[st - 2, me], asend.at[st], arecv.at[st], (n, t))
        return rcopy(S.at[st, t], landed.at[st, me], asend.at[st], arecv.at[st], (n, t))

    def all_bins(st):
        part = pl.ds(0, DEVS - 1)
        if st >= 2:
            return rcopy(Y2.at[st - 2, part], Y2.at[st - 2, part], asend.at[st], arecv.at[st], (n, me))
        return rcopy(S.at[st, part], landed.at[st, part], asend.at[st], arecv.at[st], (n, me))

    low_early = lax.broadcasted_iota(I32, (ROWS, EARLY), 0) < 4

    def gz(k):
        return rcopy(GP.at[n], GP.at[n], gzs.at[k], gzr.at[n], (lax.rem(n + k, 4), me))

    def share_gains():
        gain_products(1)
        GP[n] = jnp.where(low_early, G[0, :, pl.ds(0, EARLY)], G[1, :, pl.ds(0, EARLY)])
        for k in (2, 1, 3):
            gz(k).start()

    for g in (0, 1):
        cols = pl.ds(EARLY + g * HALF, HALF)
        gr, gs = G[0, :, cols], G[1, :, cols]
        part = pl.ds(g * HALF, HALF)

        def with_gain(t):
            v = Y[2, t, :, part]
            return gr * v + gs * swap4(v)

        def send_last(k):
            t = lax.rem(me + k, DEVS)
            Y[2, t, :, part] = with_gain(t)
            bin_copy(2 + g, t).start()

        loop(DEVS, send_last, unroll=1, start=1)
        Y2[g, me] = with_gain(me)
        if g == 0:
            share_gains()
    pass_on(1)

    for k in (1, 2, 3):
        o = lax.rem(n + k, 4)
        for i, (a, b) in enumerate(
            ((zflags.at[o], zflags.at[o]), (zoffs.at[o], zoffs.at[o]), (zw.at[o], zw.at[o]), (zfirst.at[o], zfirst.at[o]))
        ):
            rcopy(a, b, msend.at[i, k], mrecv.at[i, o], (n, me)).wait_recv()
    to_smem = [
        pltpu.make_async_copy(a, b, local_sem.at[19 + i])
        for i, (a, b) in enumerate(((zoffs, zoffs_s), (zw, zw_s), (zfirst, zfirst_s)))
    ]
    for c in to_smem:
        c.start()
    for c in to_smem:
        c.wait()
    first_down, first_up, first_far = zfirst_s[down, 0, 0], zfirst_s[up, 0, 0], zfirst_s[far, 0, 0]

    total = jnp.zeros((1, CH), F32)
    bin_here = n * BINS + me
    for k in range(NIGHTS):
        l = bin_here - zfirst_s[k, 0, 0]
        valid = flag((l >= 0) & (l < BINS))
        lc = jnp.clip(l, 0, BINS - 1)
        off = zoffs_s[k, 0, lc]
        for t in range(TAPS):
            bits = (zflags[k] >> (off + t)) & 1
            total = total + (valid * zw_s[k, t, lc]) * (1.0 - bits.astype(F32))
    wt_ref[...] = total
    scale = 1.0 / jnp.maximum(total, 0.5)

    def put(begin, k, a, b, inv):
        a, b = a * inv, b * inv
        low = lax.broadcasted_iota(I32, a.shape, 0) < 4
        at = pl.multiple_of(k * 8, 8)
        cols = pl.ds(begin, a.shape[1])
        out_ref[0, pl.ds(at, 8), cols] = jnp.where(low, a, swap4(b))
        out_ref[1, pl.ds(at, 8), cols] = jnp.where(low, swap4(a), b)

    def scale_of(st):
        return jnp.broadcast_to(scale[:, st * WIDE : (st + 1) * WIDE], (ROWS, WIDE))

    def last_first(g):
        all_bins(2 + g).wait_recv()
        s = shift_of(first, n, me)
        loop(HB, lambda j: first_message(2, g * HB + j, s, Y2[g, j], Y2[g, HB + j]))
        zcopy(2, 0, g).start()
        zcopy(2, 1, g).start()

    def last_second(g):
        zcopy(2, 0, g).wait_recv()
        zcopy(2, 1, g).wait_recv()
        loop(HB, lambda j: second_message(2, g * HB + j, me, Y2[g, j], Y2[g, HB + j]))
        zcopy(2, 2, g).start()
        zcopy(2, 3, g).start()

    last_first(0)

    for k in (1, 2, 3):
        o = lax.rem(n + k, 4)
        rcopy(GP.at[o], GP.at[o], gzs.at[k], gzr.at[o], (n, me)).wait_recv()
    for k in range(NIGHTS):
        packed = GP[k]
        turned_over = swap4(packed)
        GZ[k, 0] = jnp.where(low_early, packed, turned_over)
        GZ[k, 1] = jnp.where(low_early, -turned_over, packed)

    def combine(st, e):
        here = flag(shift_of(first, n, e) == 0)
        from_down = flag(shift_of(first_down, down, e) == 1)
        from_up = flag(shift_of(first_up, up, e) == 3)
        from_far = flag(shift_of(first_far, far, e) == 2)

        def part(half, terms):
            cols = pl.ds(st * WIDE + half * HALF, HALF)
            acc = None
            for night, v in terms:
                w = GZ[night, 0, :, cols] * v + GZ[night, 1, :, cols] * swap4(v)
                acc = w if acc is None else acc + w
            return acc

        a = part(
            0,
            (
                (n, here * Y[st, e, :, lo]), (up, from_up * r1n[st, e]), (down, r2p[st, e]),
                (far, from_far * r3p[st, e]),
            ),
        )
        b = part(
            1,
            (
                (n, here * Y[st, e, :, hi]), (down, from_down * r1p[st, e]), (up, r2n[st, e]),
                (far, from_far * r3n[st, e]),
            ),
        )
        return a, b

    def finish_early(st):
        for h in (0, 1):
            zcopy(st, 2, h).wait_recv()
            zcopy(st, 3, h).wait_recv()
            forward(st, 0, h).wait_recv()
            forward(st, 1, h).wait_recv()

        def go(k):
            t = lax.rem(me + k, DEVS)
            a, b = combine(st, t)
            S[st, t, :, lo] = a
            S[st, t, :, hi] = b
            bin_copy(st, t).start()

        loop(DEVS, go, unroll=1, start=1)
        a, b = combine(st, me)
        landed[st, me, :, lo] = a
        landed[st, me, :, hi] = b

    finish_early(0)
    last_first(1)
    finish_early(1)
    last_second(0)
    last_second(1)

    def assemble(st):
        all_bins(st).wait_recv()
        inv = scale_of(st)
        loop(DEVS // 2, lambda k: put(st * WIDE, k, landed[st, 2 * k], landed[st, 2 * k + 1], inv))

    assemble(0)
    here2 = flag(shift_of(first, n, me) == 0)
    down2 = flag(shift_of(first_down, down, me) == 1)
    up2 = flag(shift_of(first_up, up, me) == 3)
    for g in (0, 1):
        zcopy(2, 2, g).wait_recv()
        zcopy(2, 3, g).wait_recv()
        inv2 = scale_of(2)[:, g * HALF : (g + 1) * HALF]

        def finish(k):
            lower = [
                here2 * Y2[g, j] + up2 * r1n[2, g * HB + j] + r2p[2, g * HB + j] for j in (2 * k, 2 * k + 1)
            ]
            upper = [
                here2 * Y2[g, HB + j] + down2 * r1p[2, g * HB + j] + r2n[2, g * HB + j] for j in (2 * k, 2 * k + 1)
            ]
            put(EARLY + g * HALF, k, *lower, inv2)
            put(EARLY + g * HALF, HB // 2 + k, *upper, inv2)

        loop(HB // 2, finish)
    assemble(1)

    for k in (1, 2, 3):
        for which in (0, 1):
            for late in (0, 1):
                gain_a(which, late, k).wait_send()
        for c in meta(k):
            c.wait_send()
        gz(k).wait_send()

    def done(k):
        bas_x(k).wait_send()
        bas_y(k).wait_send()
        for which in (0, 1):
            for late in (0, 1):
                gain_b(which, late, k).wait_send()

    loop(8, done, unroll=1, start=1)
    for h in (0, 1):
        for st in range(STAGES):
            for w in range(4):
                zcopy(st, w, h).wait_send()
        for w in (0, 1):
            for st in (0, 1):
                forward(st, w, h).wait_send()
    for st in range(STAGES + 1):
        all_bins(st).wait_send()


def place_kernel(binned, wt, out, wt_out, sems):
    copies = [
        pltpu.make_async_copy(binned.at[p, pl.ds(k * 64, 64)], out.at[p, pl.ds(k * 64, 64)], sems.at[2 * p + k])
        for p in range(2)
        for k in range(2)
    ]
    copies.append(pltpu.make_async_copy(wt, wt_out, sems.at[4]))
    for c in copies:
        c.start()
    for c in copies:
        c.wait()


def per_device(
    visibilities, corrupted_sample_markers, antenna_gain_table, baseline_antennas, first_bin, tap_offsets, tap_weights,
    lst_delay, fringe_rate,
):
    vis = jnp.transpose(visibilities[:, 0], (0, 2, 1, 3))
    gains = jnp.transpose(antenna_gain_table, (0, 2, 1, 3))
    weights = jnp.transpose(tap_weights[0], (1, 0))
    bas = jnp.transpose(baseline_antennas, (1, 0))

    def held(a):
        return pltpu.with_memory_space_constraint(a, pltpu.HBM)

    vm = pl.BlockSpec(memory_space=pltpu.VMEM)
    hbm = pl.BlockSpec(memory_space=pltpu.HBM)
    D = pltpu.SemaphoreType.DMA
    msg = (STAGES, BINS, ROWS, HALF)
    binned, weight_total = pl.pallas_call(
        comm_kernel,
        out_shape=(
            pltpu.VMEM((2, 4 * DEVS, CH), F32),
            pltpu.VMEM((1, CH), F32),
        ),
        in_specs=[hbm] * 9,
        out_specs=(vm, vm),
        scratch_shapes=[
            pltpu.SMEM((1, BINS), I32),
            pltpu.SMEM((1,), I32),
            pltpu.SMEM((TAPS, BINS), F32),
            pltpu.SMEM((1, BINS), F32),
            pltpu.SMEM((4,), F32),
            pltpu.VMEM((2, SAMPLES, 4, CH), F32),
            pltpu.VMEM((SAMPLES, ROWS, CH), F32),
            pltpu.VMEM((STAGES, BINS, ROWS, WIDE), F32),
            pltpu.VMEM((2, DEVS, ROWS, HALF), F32),
            pltpu.VMEM((2, BINS, ROWS, WIDE), F32),
            pltpu.VMEM((2, DEVS, ROWS, WIDE), F32),
            *([pltpu.VMEM((4, 2, OWN_ANT, 1, SOON), F32)] * 2),
            *([pltpu.VMEM((4, 2, OWN_ANT, 1, LATER), F32)] * 2),
            pltpu.VMEM((8, 2, 4), I32),
            pltpu.VMEM((8, 2, 4), I32),
            pltpu.SMEM((8, 2, 4), I32),
            pltpu.SMEM((8, 2, 4), I32),
            *([pltpu.VMEM((8, 2, ROWS, SOON), F32)] * 4),
            *([pltpu.VMEM((8, 2, ROWS, LATER), F32)] * 4),
            pltpu.VMEM((2, ROWS, CH), F32),
            pltpu.VMEM((NIGHTS, ROWS, EARLY), F32),
            pltpu.VMEM((NIGHTS, 2, ROWS, EARLY), F32),
            pltpu.VMEM((NIGHTS, 1, CH), I32),
            pltpu.VMEM((NIGHTS, 1, HALF), I32),
            pltpu.VMEM((NIGHTS, 1, BINS), I32),
            pltpu.VMEM((NIGHTS, TAPS, BINS), F32),
            pltpu.SMEM((NIGHTS, 1, HALF), I32),
            pltpu.SMEM((NIGHTS, 1, BINS), I32),
            pltpu.SMEM((NIGHTS, TAPS, BINS), F32),
        ]
        + [pltpu.VMEM(msg, F32)] * 8
        + [pltpu.VMEM((2,) + msg[1:], F32)] * 2
        + [
            D((22,)), D((2, 2, 4)), D((2, 2, 4)), D((2, 8)), D((8,)), D((8,)), D((4, 4)), D((4, 4)),
            D((4, 8)), D((4, 8)), D((STAGES + 2, 4, 2)), D((STAGES + 2, 4, 2)), D((4,)), D((4,)),
            D((STAGES + 1,)), D((STAGES + 1,)),
        ],
        compiler_params=pltpu.CompilerParams(
            collective_id=0, has_side_effects=True, vmem_limit_bytes=48 * 1024 * 1024
        ),
        name="exchange",
    )(
        held(vis), held(gains), held(corrupted_sample_markers), held(tap_offsets), first_bin, held(weights),
        held(lst_delay), held(bas), held(fringe_rate),
    )
    binned, weight_total = pl.pallas_call(
        place_kernel,
        out_shape=(jax.ShapeDtypeStruct((2, 4 * DEVS, CH), F32), jax.ShapeDtypeStruct((1, CH), F32)),
        in_specs=[vm, vm],
        out_specs=(hbm, hbm),
        scratch_shapes=[D((5,))],
        compiler_params=pltpu.CompilerParams(vmem_limit_bytes=8 * 1024 * 1024),
        name="place",
    )(binned, weight_total)
    return binned.reshape(2, 1, 4 * DEVS, CH), weight_total


def solution(mesh):
    placed = (
        P(None, "night", "bl", None, None),
        P("night", None),
        P(None, "night", "bl", None),
        P("bl", None),
        P("night"),
        P("night", None),
        P("night", None, None),
        P("night", None),
        P("bl"),
    )
    return jax.shard_map(
        per_device,
        mesh=mesh,
        in_specs=placed,
        out_specs=(P(None, ("night", "bl"), None, None), P(("night", "bl"), None)),
        check_vma=False,
    )
```

```python
import functools
import math

import jax
import jax.numpy as jnp
import numpy as np
from jax import lax
from jax.experimental import pallas as pl
from jax.experimental.pallas import tpu as pltpu
from jax.sharding import PartitionSpec as P

MESH = pl.DeviceIdType.MESH
F32 = jnp.float32
I32 = jnp.int32

NIGHTS = 4
DEVS = 32
BINS = 32
ROWS = 8
CH = 768
SAMPLES = 30
TAPS = 4
OWN_ANT = 11
STAGES = 3
WIDE = 256
HALF = 128
SOON = 128
LATER = 256
EARLY = 512
HB = 16


def _fit(kind, terms):
    k = np.arange(200)
    u = 0.125 * (1 + np.cos(np.pi * (k + 0.5) / 200))
    r = np.sqrt(u)
    y = np.sin(2 * np.pi * r) / r if kind == "sin" else np.cos(2 * np.pi * r)
    cheb = np.polynomial.chebyshev.Chebyshev.fit(u, y, terms - 1, domain=[0, 0.25])
    return [float(v) for v in cheb.convert(kind=np.polynomial.Polynomial).coef]


SIN_C = _fit("sin", 8)
COS_C = _fit("cos", 8)


def horner(coef, u):
    acc = jnp.full_like(u, coef[-1])
    for c in coef[-2::-1]:
        acc = acc * u + c
    return acc


def swap4(v):
    return pltpu.roll(v, 4, 0)


def flag(cond):
    return jnp.where(cond, jnp.float32(1.0), jnp.float32(0.0))


def comm_kernel(
    vis, gains, flags_h, offs_h, first_h, weights_h, delay_h, bas_h, rate_h,
    out_ref, wt_ref,
    offs_s, first_s, weights_s, delay_s, rate_s, V, UV, Y, Y2, S, landed, gyu, gxu, gyl, gxl, bx_v, by_v, bx_s, by_s,
    m0, m1, c0, c1, q0, q1, d0, d1, G, GP, GZ,
    zflags, zfirst, zoffs, zw, zfirst_s, zoffs_s, zw_s, s1p, s1n, s2p, s2n, r1p, r1n, r2p, r2n, r3p, r3n,
    local_sem, gsend, grecv, bsend, bxr, byr, msend, mrecv,
    rsend, rrecv, zsend, zrecv, gzs, gzr, asend, arecv,
):
    n = lax.axis_index("night")
    me = lax.axis_index("bl")
    core = lax.rem(me, 2)
    x = lax.rem(me // 2, 4)
    y = me // 8

    def bl_of(yy, xx, cc):
        return (yy * 4 + xx) * 2 + cc

    def rcopy(src, dst, ss, rs, dev):
        return pltpu.make_async_remote_copy(
            src_ref=src, dst_ref=dst, send_sem=ss, recv_sem=rs, device_id=dev, device_id_type=MESH
        )

    def loop(count, body, unroll=4, start=0):
        def step(i, c):
            body(i)
            return c

        lax.fori_loop(start, count, step, 0, unroll=unroll)

    load_vis = [
        pltpu.make_async_copy(
            vis.at[:, :, :, pl.ds(st * WIDE, WIDE)], V.at[:, :, :, pl.ds(st * WIDE, WIDE)], local_sem.at[st]
        )
        for st in range(STAGES)
    ]

    def table(which, late):
        begin = ((512, 640), (0, 256))[late][which]
        return gains.at[:, :, :, pl.ds(begin, LATER if late else SOON)], ((gyu, gxu), (gyl, gxl))[late][which]

    own_gains = []
    for late in (0, 1):
        for which in (0, 1):
            src, dst = table(which, late)
            own_gains.append(pltpu.make_async_copy(src, dst.at[(y, x)[which]], local_sem.at[3 + 2 * late + which]))
    small = [
        pltpu.make_async_copy(a, b, local_sem.at[7 + i])
        for i, (a, b) in enumerate(
            (
                (first_h, first_s), (offs_h, offs_s), (weights_h, weights_s), (delay_h, delay_s), (rate_h, rate_s),
                (flags_h, zflags.at[n]), (offs_h, zoffs.at[n]), (weights_h, zw.at[n]),
                (bas_h, bx_v.at[x * 2 + core]), (bas_h, by_v.at[y * 2 + core]),
            )
        )
    ]
    for c in (load_vis[0], *small[:6]):
        c.start()

    barrier = pltpu.get_barrier_semaphore()

    def greet(device):
        pl.semaphore_signal(barrier, inc=1, device_id=device, device_id_type=MESH)

    for k in (1, 2, 3):
        greet((lax.rem(n + k, 4), me))
    greet((n, bl_of(y, x, 1 - core)))
    for k in (1, 2, 3):
        for cc in range(2):
            greet((n, bl_of(y, lax.rem(x + k, 4), cc)))
            greet((n, bl_of(lax.rem(y + k, 4), x, cc)))
    for c in (*small[6:], *own_gains, *load_vis[1:]):
        c.start()

    lane = lax.broadcasted_iota(I32, (ROWS, WIDE), 1).astype(F32)
    row = lax.broadcasted_iota(I32, (ROWS, WIDE), 0)
    sign = jnp.where(row < 4, jnp.float32(-1.0), jnp.float32(1.0))
    for c in small[:6]:
        c.wait()
    first = first_s[0]
    zfirst[n] = jnp.full((1, HALF), first, I32)
    which_row = row & 3
    rates = jnp.where(
        which_row < 2,
        jnp.where(which_row == 0, rate_s[0], rate_s[1]),
        jnp.where(which_row == 2, rate_s[2], rate_s[3]),
    ) * (1.0 / (2.0 * math.pi))

    def samples(st):
        at = st * WIDE
        load_vis[st].wait()

        def per_sample(t):
            bits = (zflags[n, :, pl.ds(at, WIDE)] >> t) & 1
            both = jnp.concatenate([V[0, t, :, pl.ds(at, WIDE)], V[1, t, :, pl.ds(at, WIDE)]], axis=0)
            UV[t, :, pl.ds(at, WIDE)] = both * (1.0 - bits.astype(F32))

        loop(SAMPLES, per_sample, unroll=5)

    def shift_of(f, night, e):
        return (lax.shift_right_logical(f, 5) + jnp.where(e < (f & 31), 1, 0) - night) & 3

    def phases(st):
        return rates * (1.0 + (lane + float(st * WIDE)) * (1.0 / CH))

    def turned(st, rate, e):
        at = st * WIDE
        l = (e - first) & 31
        off = offs_s[0, l]
        acc = weights_s[0, l] * UV[off, :, pl.ds(at, WIDE)]
        for k in range(1, TAPS):
            acc = acc + weights_s[k, l] * UV[off + k, :, pl.ds(at, WIDE)]
        turns = rate * delay_s[0, l]
        r = turns - jnp.floor(turns + 0.5)
        u = r * r
        return horner(COS_C, u) * acc + (horner(SIN_C, u) * (r * sign)) * swap4(acc)

    up = lax.rem(n + 1, 4)
    down = lax.rem(n + 3, 4)
    far = lax.rem(n + 2, 4)

    def zcopy(st, which, h):
        src = (s1p, s1n, s2p, s2n)[which].at[st, pl.ds(h * HB, HB)]
        dst = (r1p, r1n, r2p, r2n)[which].at[st, pl.ds(h * HB, HB)]
        to = up if which % 2 == 0 else down
        return rcopy(src, dst, zsend.at[st, which, h], zrecv.at[st, which, h], (to, me))

    def forward(st, which, h):
        src, dst = ((r1p, r3p), (r1n, r3n))[which]
        part = pl.ds(h * HB, HB)
        to = (up, down)[which]
        return rcopy(
            src.at[st, part], dst.at[st, part], zsend.at[STAGES + st, which, h], zrecv.at[STAGES + st, which, h], (to, me)
        )

    lo = pl.ds(0, HALF)
    hi = pl.ds(HALF, HALF)

    def first_message(st, i, s, a, b):
        two = flag(s == 2)
        s1p[st, i] = two * a + flag(s == 1) * b
        s1n[st, i] = two * b + flag(s == 3) * a

    def second_message(st, i, e, a, b):
        s = shift_of(first, n, e)
        s2p[st, i] = flag(s == 1) * a + flag(shift_of(first_down, down, e) == 2) * r1p[st, i]
        s2n[st, i] = flag(s == 3) * b + flag(shift_of(first_up, up, e) == 2) * r1n[st, i]

    def early(st):
        samples(st)
        rate = phases(st)

        def per_bin(e):
            v = turned(st, rate, e)
            Y[st, e] = v
            a, b = v[:, :HALF], v[:, HALF:]
            s = shift_of(first, n, e)
            first_message(st, e, s, a, b)
            s2p[st, e] = flag(s == 1) * a
            s2n[st, e] = flag(s == 3) * b

        loop(BINS, per_bin)

    def start_early(st, message):
        for h in (0, 1):
            for w in (0, 1):
                zcopy(st, 2 * message + w, h).start()

    early(0)
    pl.semaphore_wait(barrier, 16)
    start_early(0, 0)
    start_early(0, 1)
    for c in (*small[6:], *own_gains):
        c.wait()

    def gain_a(which, late, k):
        _, tab = table(which, late)
        mine = (y, x)[which]
        to = bl_of(lax.rem(y + k, 4), x, core) if which == 0 else bl_of(y, lax.rem(x + k, 4), core)
        return rcopy(tab.at[mine], tab.at[mine], gsend.at[which, late, k], grecv.at[which, late, mine], (n, to))

    def gain_a_wait(which, late):
        _, tab = table(which, late)
        for k in (1, 2, 3):
            o = lax.rem((y, x)[which] + k, 4)
            rcopy(tab.at[o], tab.at[o], gsend.at[which, late, k], grecv.at[which, late, o], (n, me)).wait_recv()

    def slot_dev(k, own):
        s = lax.rem(own + k, 8)
        return s, s // 2, lax.rem(s, 2)

    def bas_x(k):
        s, tx, tc = slot_dev(k, x * 2 + core)
        mine = x * 2 + core
        return rcopy(bx_v.at[mine], bx_v.at[mine], bsend.at[0, k], bxr.at[mine], (n, bl_of(y, tx, tc)))

    def bas_y(k):
        s, ty, tc = slot_dev(k, y * 2 + core)
        mine = y * 2 + core
        return rcopy(by_v.at[mine], by_v.at[mine], bsend.at[1, k], byr.at[mine], (n, bl_of(ty, x, tc)))

    for k in (1, 3, 2):
        for which in (0, 1):
            gain_a(which, 0, k).start()

    def start_bas(k):
        bas_x(k).start()
        bas_y(k).start()

    loop(8, start_bas, unroll=1, start=1)

    def meta(k):
        t = lax.rem(n + k, 4)
        return [
            rcopy(a, b, msend.at[i, k], mrecv.at[i, n], (t, me))
            for i, (a, b) in enumerate(
                (
                    (zflags.at[n], zflags.at[n]), (zoffs.at[n], zoffs.at[n]), (zw.at[n], zw.at[n]),
                    (zfirst.at[n], zfirst.at[n]),
                )
            )
        ]

    for k in (1, 3, 2):
        for c in meta(k):
            c.start()
    for k in (1, 3, 2):
        for which in (0, 1):
            gain_a(which, 1, k).start()
    early(1)
    start_early(1, 0)

    def pass_on(st):
        for h in (0, 1):
            for w in (0, 1):
                zcopy(st, w, h).wait_recv()
                forward(st, w, h).start()

    pass_on(0)
    start_early(1, 1)

    def wait_bas(k):
        sx = lax.rem(x * 2 + core + k, 8)
        sy = lax.rem(y * 2 + core + k, 8)
        rcopy(bx_v.at[sx], bx_v.at[sx], bsend.at[0, k], bxr.at[sx], (n, me)).wait_recv()
        rcopy(by_v.at[sy], by_v.at[sy], bsend.at[1, k], byr.at[sy], (n, me)).wait_recv()

    loop(8, wait_bas, unroll=1, start=1)
    to_s0 = pltpu.make_async_copy(bx_v, bx_s, local_sem.at[17])
    to_s1 = pltpu.make_async_copy(by_v, by_s, local_sem.at[18])
    to_s0.start()
    to_s1.start()
    gain_a_wait(0, 0)
    gain_a_wait(1, 0)
    to_s0.wait()
    to_s1.wait()

    slots = (lambda k: lax.rem(x * 2 + core + k, 8), lambda k: lax.rem(y * 2 + core + k, 8))
    asked_of = (bx_s, by_s)
    mine_of = (x * 2 + core, y * 2 + core)

    def pick(which, late, slot):
        out = ((m0, m1), (q0, q1))[late][which]
        _, tab = table(which, late)
        for r in range(ROWS):
            a = asked_of[which][slot, r // 4, r % 4]
            owner = lax.shift_right_logical(a * 5958, 16)
            at = a - owner * OWN_ANT
            ox, oy = (owner >> 1) & 3, owner >> 3
            fixed, moving, here = (ox, oy, x) if which == 0 else (oy, ox, y)
            w = flag((fixed == here) & ((owner & 1) == core))
            for p in range(2):
                out[slot, p, pl.ds(r, 1), :] = w * tab[moving, p, at]

    def gain_b(which, late, k):
        s, t, tc = slot_dev(k, mine_of[which])
        src = ((m0, m1), (q0, q1))[late][which]
        dst = ((c0, c1), (d0, d1))[late][which]
        to = bl_of(y, t, tc) if which == 0 else bl_of(t, x, tc)
        i = 2 * late + which
        return rcopy(src.at[s], dst.at[mine_of[which]], rsend.at[i, k], rrecv.at[i, mine_of[which]], (n, to))

    def send_rows(late):
        def go(k):
            for which in (0, 1):
                pick(which, late, slots[which](k))
                gain_b(which, late, k).start()

        loop(8, go, unroll=1, start=1)
        for which in (0, 1):
            pick(which, late, mine_of[which])
            dst = ((c0, c1), (d0, d1))[late][which]
            src = ((m0, m1), (q0, q1))[late][which]
            dst[mine_of[which]] = src[mine_of[which]]

    def gain_products(late):
        def wait(k):
            for which in (0, 1):
                s = slots[which](k)
                src = ((m0, m1), (q0, q1))[late][which]
                dst = ((c0, c1), (d0, d1))[late][which]
                i = 2 * late + which
                rcopy(src.at[s], dst.at[s], rsend.at[i, k], rrecv.at[i, s], (n, me)).wait_recv()

        loop(8, wait, unroll=1, start=1)
        for which in (0, 1):
            got = ((c0, c1), (d0, d1))[late][which]
            parts = []
            for p in range(2):
                acc = got[0, p]
                for s in range(1, 8):
                    acc = acc + got[s, p]
                parts.append(acc)
            A, B = parts
            cols = pl.ds(((512, 640), (0, 256))[late][which], LATER if late else SOON)
            G[0, :, cols] = A * swap4(A) + B * swap4(B)
            G[1, :, cols] = A * swap4(B) - B * swap4(A)

    send_rows(0)

    gain_a_wait(0, 1)
    gain_a_wait(1, 1)
    send_rows(1)

    samples(2)
    rate2 = phases(2)

    def last(e):
        Y[2, e] = turned(2, rate2, e)

    loop(BINS, last)
    gain_products(0)

    def bin_copy(st, t):
        if st >= 2:
            src = Y.at[2, t, :, pl.ds((st - 2) * HALF, HALF)]
            return rcopy(src, Y2.at[st - 2, me], asend.at[st], arecv.at[st], (n, t))
        return rcopy(S.at[st, t], landed.at[st, me], asend.at[st], arecv.at[st], (n, t))

    def all_bins(st):
        part = pl.ds(0, DEVS - 1)
        if st >= 2:
            return rcopy(Y2.at[st - 2, part], Y2.at[st - 2, part], asend.at[st], arecv.at[st], (n, me))
        return rcopy(S.at[st, part], landed.at[st, part], asend.at[st], arecv.at[st], (n, me))

    low_early = lax.broadcasted_iota(I32, (ROWS, EARLY), 0) < 4

    def gz(k):
        return rcopy(GP.at[n], GP.at[n], gzs.at[k], gzr.at[n], (lax.rem(n + k, 4), me))

    def load_meta():
        for k in (1, 2, 3):
            o = lax.rem(n + k, 4)
            for i, (a, b) in enumerate(
                ((zflags.at[o], zflags.at[o]), (zoffs.at[o], zoffs.at[o]), (zw.at[o], zw.at[o]), (zfirst.at[o], zfirst.at[o]))
            ):
                rcopy(a, b, msend.at[i, k], mrecv.at[i, o], (n, me)).wait_recv()
        to_smem = [
            pltpu.make_async_copy(a, b, local_sem.at[19 + i])
            for i, (a, b) in enumerate(((zoffs, zoffs_s), (zw, zw_s), (zfirst, zfirst_s)))
        ]
        for c in to_smem:
            c.start()
        return to_smem

    def share_gains():
        gain_products(1)
        GP[n] = jnp.where(low_early, G[0, :, pl.ds(0, EARLY)], G[1, :, pl.ds(0, EARLY)])
        for k in (2, 1, 3):
            gz(k).start()

    for g in (0, 1):
        cols = pl.ds(EARLY + g * HALF, HALF)
        gr, gs = G[0, :, cols], G[1, :, cols]
        part = pl.ds(g * HALF, HALF)

        def with_gain(t):
            v = Y[2, t, :, part]
            return gr * v + gs * swap4(v)

        def send_last(k):
            t = lax.rem(me + k, DEVS)
            Y[2, t, :, part] = with_gain(t)
            bin_copy(2 + g, t).start()

        loop(DEVS, send_last, unroll=1, start=1)
        Y2[g, me] = with_gain(me)
        if g == 0:
            share_gains()
            to_smem = load_meta()
    pass_on(1)

    for c in to_smem:
        c.wait()
    first_down, first_up, first_far = zfirst_s[down, 0, 0], zfirst_s[up, 0, 0], zfirst_s[far, 0, 0]

    total = jnp.zeros((1, CH), F32)
    bin_here = n * BINS + me
    for k in range(NIGHTS):
        l = bin_here - zfirst_s[k, 0, 0]
        valid = flag((l >= 0) & (l < BINS))
        lc = jnp.clip(l, 0, BINS - 1)
        off = zoffs_s[k, 0, lc]
        for t in range(TAPS):
            bits = (zflags[k] >> (off + t)) & 1
            total = total + (valid * zw_s[k, t, lc]) * (1.0 - bits.astype(F32))
    wt_ref[...] = total
    scale = 1.0 / jnp.maximum(total, 0.5)

    def put(begin, k, a, b, inv):
        a, b = a * inv, b * inv
        low = lax.broadcasted_iota(I32, a.shape, 0) < 4
        at = pl.multiple_of(k * 8, 8)
        cols = pl.ds(begin, a.shape[1])
        out_ref[0, pl.ds(at, 8), cols] = jnp.where(low, a, swap4(b))
        out_ref[1, pl.ds(at, 8), cols] = jnp.where(low, swap4(a), b)

    def scale_of(st):
        return jnp.broadcast_to(scale[:, st * WIDE : (st + 1) * WIDE], (ROWS, WIDE))

    def last_first(g):
        all_bins(2 + g).wait_recv()
        s = shift_of(first, n, me)
        loop(HB, lambda j: first_message(2, g * HB + j, s, Y2[g, j], Y2[g, HB + j]))
        zcopy(2, 0, g).start()
        zcopy(2, 1, g).start()

    def last_second(g):
        zcopy(2, 0, g).wait_recv()
        zcopy(2, 1, g).wait_recv()
        loop(HB, lambda j: second_message(2, g * HB + j, me, Y2[g, j], Y2[g, HB + j]))
        zcopy(2, 2, g).start()
        zcopy(2, 3, g).start()

    def unpack_gains():
        for k in (1, 2, 3):
            o = lax.rem(n + k, 4)
            rcopy(GP.at[o], GP.at[o], gzs.at[k], gzr.at[o], (n, me)).wait_recv()
        for k in range(NIGHTS):
            packed = GP[k]
            turned_over = swap4(packed)
            GZ[k, 0] = jnp.where(low_early, packed, turned_over)
            GZ[k, 1] = jnp.where(low_early, -turned_over, packed)

    def combine(st, e):
        here = flag(shift_of(first, n, e) == 0)
        from_down = flag(shift_of(first_down, down, e) == 1)
        from_up = flag(shift_of(first_up, up, e) == 3)
        from_far = flag(shift_of(first_far, far, e) == 2)

        def part(half, terms):
            cols = pl.ds(st * WIDE + half * HALF, HALF)
            acc = None
            for night, v in terms:
                w = GZ[night, 0, :, cols] * v + GZ[night, 1, :, cols] * swap4(v)
                acc = w if acc is None else acc + w
            return acc

        a = part(
            0,
            (
                (n, here * Y[st, e, :, lo]), (up, from_up * r1n[st, e]), (down, r2p[st, e]),
                (far, from_far * r3p[st, e]),
            ),
        )
        b = part(
            1,
            (
                (n, here * Y[st, e, :, hi]), (down, from_down * r1p[st, e]), (up, r2n[st, e]),
                (far, from_far * r3n[st, e]),
            ),
        )
        return a, b

    def finish_early(st):
        for h in (0, 1):
            zcopy(st, 2, h).wait_recv()
            zcopy(st, 3, h).wait_recv()
            forward(st, 0, h).wait_recv()
            forward(st, 1, h).wait_recv()

        def go(k):
            t = lax.rem(me + k, DEVS)
            a, b = combine(st, t)
            S[st, t, :, lo] = a
            S[st, t, :, hi] = b
            bin_copy(st, t).start()

        loop(DEVS, go, unroll=1, start=1)
        a, b = combine(st, me)
        landed[st, me, :, lo] = a
        landed[st, me, :, hi] = b

    last_first(0)
    unpack_gains()
    finish_early(0)
    last_first(1)
    finish_early(1)
    last_second(0)
    last_second(1)

    def assemble(st):
        all_bins(st).wait_recv()
        inv = scale_of(st)
        loop(DEVS // 2, lambda k: put(st * WIDE, k, landed[st, 2 * k], landed[st, 2 * k + 1], inv))

    assemble(0)
    here2 = flag(shift_of(first, n, me) == 0)
    down2 = flag(shift_of(first_down, down, me) == 1)
    up2 = flag(shift_of(first_up, up, me) == 3)
    for g in (0, 1):
        zcopy(2, 2, g).wait_recv()
        zcopy(2, 3, g).wait_recv()
        inv2 = scale_of(2)[:, g * HALF : (g + 1) * HALF]

        def finish(k):
            lower = [
                here2 * Y2[g, j] + up2 * r1n[2, g * HB + j] + r2p[2, g * HB + j] for j in (2 * k, 2 * k + 1)
            ]
            upper = [
                here2 * Y2[g, HB + j] + down2 * r1p[2, g * HB + j] + r2n[2, g * HB + j] for j in (2 * k, 2 * k + 1)
            ]
            put(EARLY + g * HALF, k, *lower, inv2)
            put(EARLY + g * HALF, HB // 2 + k, *upper, inv2)

        loop(HB // 2, finish)
    assemble(1)

    for k in (1, 2, 3):
        for which in (0, 1):
            for late in (0, 1):
                gain_a(which, late, k).wait_send()
        for c in meta(k):
            c.wait_send()
        gz(k).wait_send()

    def done(k):
        bas_x(k).wait_send()
        bas_y(k).wait_send()
        for which in (0, 1):
            for late in (0, 1):
                gain_b(which, late, k).wait_send()

    loop(8, done, unroll=1, start=1)
    for h in (0, 1):
        for st in range(STAGES):
            for w in range(4):
                zcopy(st, w, h).wait_send()
        for w in (0, 1):
            for st in (0, 1):
                forward(st, w, h).wait_send()
    for st in range(STAGES + 1):
        all_bins(st).wait_send()


def place_kernel(binned, wt, out, wt_out, sems):
    copies = [
        pltpu.make_async_copy(binned.at[p, pl.ds(k * 64, 64)], out.at[p, pl.ds(k * 64, 64)], sems.at[2 * p + k])
        for p in range(2)
        for k in range(2)
    ]
    copies.append(pltpu.make_async_copy(wt, wt_out, sems.at[4]))
    for c in copies:
        c.start()
    for c in copies:
        c.wait()


def per_device(
    visibilities, corrupted_sample_markers, antenna_gain_table, baseline_antennas, first_bin, tap_offsets, tap_weights,
    lst_delay, fringe_rate,
):
    vis = jnp.transpose(visibilities[:, 0], (0, 2, 1, 3))
    gains = jnp.transpose(antenna_gain_table, (0, 2, 1, 3))
    weights = jnp.transpose(tap_weights[0], (1, 0))
    bas = jnp.transpose(baseline_antennas, (1, 0))

    def held(a):
        return pltpu.with_memory_space_constraint(a, pltpu.HBM)

    vm = pl.BlockSpec(memory_space=pltpu.VMEM)
    hbm = pl.BlockSpec(memory_space=pltpu.HBM)
    D = pltpu.SemaphoreType.DMA
    msg = (STAGES, BINS, ROWS, HALF)
    binned, weight_total = pl.pallas_call(
        comm_kernel,
        out_shape=(
            pltpu.VMEM((2, 4 * DEVS, CH), F32),
            pltpu.VMEM((1, CH), F32),
        ),
        in_specs=[hbm] * 9,
        out_specs=(vm, vm),
        scratch_shapes=[
            pltpu.SMEM((1, BINS), I32),
            pltpu.SMEM((1,), I32),
            pltpu.SMEM((TAPS, BINS), F32),
            pltpu.SMEM((1, BINS), F32),
            pltpu.SMEM((4,), F32),
            pltpu.VMEM((2, SAMPLES, 4, CH), F32),
            pltpu.VMEM((SAMPLES, ROWS, CH), F32),
            pltpu.VMEM((STAGES, BINS, ROWS, WIDE), F32),
            pltpu.VMEM((2, DEVS, ROWS, HALF), F32),
            pltpu.VMEM((2, BINS, ROWS, WIDE), F32),
            pltpu.VMEM((2, DEVS, ROWS, WIDE), F32),
            *([pltpu.VMEM((4, 2, OWN_ANT, 1, SOON), F32)] * 2),
            *([pltpu.VMEM((4, 2, OWN_ANT, 1, LATER), F32)] * 2),
            pltpu.VMEM((8, 2, 4), I32),
            pltpu.VMEM((8, 2, 4), I32),
            pltpu.SMEM((8, 2, 4), I32),
            pltpu.SMEM((8, 2, 4), I32),
            *([pltpu.VMEM((8, 2, ROWS, SOON), F32)] * 4),
            *([pltpu.VMEM((8, 2, ROWS, LATER), F32)] * 4),
            pltpu.VMEM((2, ROWS, CH), F32),
            pltpu.VMEM((NIGHTS, ROWS, EARLY), F32),
            pltpu.VMEM((NIGHTS, 2, ROWS, EARLY), F32),
            pltpu.VMEM((NIGHTS, 1, CH), I32),
            pltpu.VMEM((NIGHTS, 1, HALF), I32),
            pltpu.VMEM((NIGHTS, 1, BINS), I32),
            pltpu.VMEM((NIGHTS, TAPS, BINS), F32),
            pltpu.SMEM((NIGHTS, 1, HALF), I32),
            pltpu.SMEM((NIGHTS, 1, BINS), I32),
            pltpu.SMEM((NIGHTS, TAPS, BINS), F32),
        ]
        + [pltpu.VMEM(msg, F32)] * 8
        + [pltpu.VMEM((2,) + msg[1:], F32)] * 2
        + [
            D((22,)), D((2, 2, 4)), D((2, 2, 4)), D((2, 8)), D((8,)), D((8,)), D((4, 4)), D((4, 4)),
            D((4, 8)), D((4, 8)), D((STAGES + 2, 4, 2)), D((STAGES + 2, 4, 2)), D((4,)), D((4,)),
            D((STAGES + 1,)), D((STAGES + 1,)),
        ],
        compiler_params=pltpu.CompilerParams(
            collective_id=0, has_side_effects=True, vmem_limit_bytes=48 * 1024 * 1024
        ),
        name="exchange",
    )(
        held(vis), held(gains), held(corrupted_sample_markers), held(tap_offsets), first_bin, held(weights),
        held(lst_delay), held(bas), held(fringe_rate),
    )
    binned, weight_total = pl.pallas_call(
        place_kernel,
        out_shape=(jax.ShapeDtypeStruct((2, 4 * DEVS, CH), F32), jax.ShapeDtypeStruct((1, CH), F32)),
        in_specs=[vm, vm],
        out_specs=(hbm, hbm),
        scratch_shapes=[D((5,))],
        compiler_params=pltpu.CompilerParams(vmem_limit_bytes=8 * 1024 * 1024),
        name="place",
    )(binned, weight_total)
    return binned.reshape(2, 1, 4 * DEVS, CH), weight_total


def solution(mesh):
    placed = (
        P(None, "night", "bl", None, None),
        P("night", None),
        P(None, "night", "bl", None),
        P("bl", None),
        P("night"),
        P("night", None),
        P("night", None, None),
        P("night", None),
        P("bl"),
    )
    return jax.shard_map(
        per_device,
        mesh=mesh,
        in_specs=placed,
        out_specs=(P(None, ("night", "bl"), None, None), P(("night", "bl"), None)),
        check_vma=False,
    )
```

```python
import functools
import math

import jax
import jax.numpy as jnp
import numpy as np
from jax import lax
from jax.experimental import pallas as pl
from jax.experimental.pallas import tpu as pltpu
from jax.sharding import PartitionSpec as P

MESH = pl.DeviceIdType.MESH
F32 = jnp.float32
I32 = jnp.int32

NIGHTS = 4
DEVS = 32
BINS = 32
ROWS = 8
CH = 768
SAMPLES = 30
TAPS = 4
OWN_ANT = 11
STAGES = 3
WIDE = 256
HALF = 128
SOON = 128
LATER = 256
EARLY = 512
HB = 16


def _fit(kind, terms):
    k = np.arange(200)
    u = 0.125 * (1 + np.cos(np.pi * (k + 0.5) / 200))
    r = np.sqrt(u)
    y = np.sin(2 * np.pi * r) / r if kind == "sin" else np.cos(2 * np.pi * r)
    cheb = np.polynomial.chebyshev.Chebyshev.fit(u, y, terms - 1, domain=[0, 0.25])
    return [float(v) for v in cheb.convert(kind=np.polynomial.Polynomial).coef]


SIN_C = _fit("sin", 8)
COS_C = _fit("cos", 8)


def horner(coef, u):
    acc = jnp.full_like(u, coef[-1])
    for c in coef[-2::-1]:
        acc = acc * u + c
    return acc


def swap4(v):
    return pltpu.roll(v, 4, 0)


def flag(cond):
    return jnp.where(cond, jnp.float32(1.0), jnp.float32(0.0))


def comm_kernel(
    vis, gains, flags_h, offs_h, first_h, weights_h, delay_h, bas_h, rate_h,
    out_ref, wt_ref,
    offs_s, first_s, weights_s, delay_s, rate_s, V, UV, Y, Y2, S, landed, gyu, gxu, gyl, gxl, bx_v, by_v, bx_s, by_s,
    m0, m1, c0, c1, q0, q1, d0, d1, G, GP, GZ,
    zflags, zfirst, zoffs, zw, zfirst_s, zoffs_s, zw_s, s1p, s1n, s2p, s2n, r1p, r1n, r2p, r2n, r3p, r3n,
    local_sem, gsend, grecv, bsend, bxr, byr, msend, mrecv,
    rsend, rrecv, zsend, zrecv, gzs, gzr, asend, arecv,
):
    n = lax.axis_index("night")
    me = lax.axis_index("bl")
    core = lax.rem(me, 2)
    x = lax.rem(me // 2, 4)
    y = me // 8

    def bl_of(yy, xx, cc):
        return (yy * 4 + xx) * 2 + cc

    def rcopy(src, dst, ss, rs, dev):
        return pltpu.make_async_remote_copy(
            src_ref=src, dst_ref=dst, send_sem=ss, recv_sem=rs, device_id=dev, device_id_type=MESH
        )

    def loop(count, body, unroll=4, start=0):
        def step(i, c):
            body(i)
            return c

        lax.fori_loop(start, count, step, 0, unroll=unroll)

    load_vis = [
        pltpu.make_async_copy(
            vis.at[:, :, :, pl.ds(st * WIDE, WIDE)], V.at[:, :, :, pl.ds(st * WIDE, WIDE)], local_sem.at[st]
        )
        for st in range(STAGES)
    ]

    def table(which, late):
        begin = ((512, 640), (0, 256))[late][which]
        return gains.at[:, :, :, pl.ds(begin, LATER if late else SOON)], ((gyu, gxu), (gyl, gxl))[late][which]

    own_gains = []
    for late in (0, 1):
        for which in (0, 1):
            src, dst = table(which, late)
            own_gains.append(pltpu.make_async_copy(src, dst.at[(y, x)[which]], local_sem.at[3 + 2 * late + which]))
    small = [
        pltpu.make_async_copy(a, b, local_sem.at[7 + i])
        for i, (a, b) in enumerate(
            (
                (first_h, first_s), (offs_h, offs_s), (weights_h, weights_s), (delay_h, delay_s), (rate_h, rate_s),
                (flags_h, zflags.at[n]), (offs_h, zoffs.at[n]), (weights_h, zw.at[n]),
                (bas_h, bx_v.at[x * 2 + core]), (bas_h, by_v.at[y * 2 + core]),
            )
        )
    ]
    for c in (load_vis[0], *small[:6]):
        c.start()

    barrier = pltpu.get_barrier_semaphore()

    def greet(device):
        pl.semaphore_signal(barrier, inc=1, device_id=device, device_id_type=MESH)

    for k in (1, 2, 3):
        greet((lax.rem(n + k, 4), me))
    greet((n, bl_of(y, x, 1 - core)))
    for k in (1, 2, 3):
        for cc in range(2):
            greet((n, bl_of(y, lax.rem(x + k, 4), cc)))
            greet((n, bl_of(lax.rem(y + k, 4), x, cc)))
    for c in (*small[6:], *own_gains, *load_vis[1:]):
        c.start()

    lane = lax.broadcasted_iota(I32, (ROWS, WIDE), 1).astype(F32)
    row = lax.broadcasted_iota(I32, (ROWS, WIDE), 0)
    sign = jnp.where(row < 4, jnp.float32(-1.0), jnp.float32(1.0))
    for c in small[:6]:
        c.wait()
    first = first_s[0]
    zfirst[n] = jnp.full((1, HALF), first, I32)
    which_row = row & 3
    rates = jnp.where(
        which_row < 2,
        jnp.where(which_row == 0, rate_s[0], rate_s[1]),
        jnp.where(which_row == 2, rate_s[2], rate_s[3]),
    ) * (1.0 / (2.0 * math.pi))

    def samples(st):
        at = st * WIDE
        load_vis[st].wait()

        def per_sample(t):
            bits = (zflags[n, :, pl.ds(at, WIDE)] >> t) & 1
            both = jnp.concatenate([V[0, t, :, pl.ds(at, WIDE)], V[1, t, :, pl.ds(at, WIDE)]], axis=0)
            UV[t, :, pl.ds(at, WIDE)] = both * (1.0 - bits.astype(F32))

        loop(SAMPLES, per_sample, unroll=5)

    def shift_of(f, night, e):
        return (lax.shift_right_logical(f, 5) + jnp.where(e < (f & 31), 1, 0) - night) & 3

    def phases(st):
        return rates * (1.0 + (lane + float(st * WIDE)) * (1.0 / CH))

    def turned(st, rate, e):
        at = st * WIDE
        l = (e - first) & 31
        off = offs_s[0, l]
        acc = weights_s[0, l] * UV[off, :, pl.ds(at, WIDE)]
        for k in range(1, TAPS):
            acc = acc + weights_s[k, l] * UV[off + k, :, pl.ds(at, WIDE)]
        turns = rate * delay_s[0, l]
        r = turns - jnp.floor(turns + 0.5)
        u = r * r
        return horner(COS_C, u) * acc + (horner(SIN_C, u) * (r * sign)) * swap4(acc)

    up = lax.rem(n + 1, 4)
    down = lax.rem(n + 3, 4)
    far = lax.rem(n + 2, 4)

    def zcopy(st, which, h):
        src = (s1p, s1n, s2p, s2n)[which].at[st, pl.ds(h * HB, HB)]
        dst = (r1p, r1n, r2p, r2n)[which].at[st, pl.ds(h * HB, HB)]
        to = up if which % 2 == 0 else down
        return rcopy(src, dst, zsend.at[st, which, h], zrecv.at[st, which, h], (to, me))

    def forward(st, which, h):
        src, dst = ((r1p, r3p), (r1n, r3n))[which]
        part = pl.ds(h * HB, HB)
        to = (up, down)[which]
        return rcopy(
            src.at[st, part], dst.at[st, part], zsend.at[STAGES + st, which, h], zrecv.at[STAGES + st, which, h], (to, me)
        )

    lo = pl.ds(0, HALF)
    hi = pl.ds(HALF, HALF)

    def first_message(st, i, s, a, b):
        two = flag(s == 2)
        s1p[st, i] = two * a + flag(s == 1) * b
        s1n[st, i] = two * b + flag(s == 3) * a

    def second_message(st, i, e, a, b):
        s = shift_of(first, n, e)
        s2p[st, i] = flag(s == 1) * a + flag(shift_of(first_down, down, e) == 2) * r1p[st, i]
        s2n[st, i] = flag(s == 3) * b + flag(shift_of(first_up, up, e) == 2) * r1n[st, i]

    def early(st):
        samples(st)
        rate = phases(st)

        def per_bin(e):
            v = turned(st, rate, e)
            Y[st, e] = v
            a, b = v[:, :HALF], v[:, HALF:]
            s = shift_of(first, n, e)
            first_message(st, e, s, a, b)
            s2p[st, e] = flag(s == 1) * a
            s2n[st, e] = flag(s == 3) * b

        loop(BINS, per_bin)

    def start_early(st, message):
        for h in (0, 1):
            for w in (0, 1):
                zcopy(st, 2 * message + w, h).start()

    early(0)
    pl.semaphore_wait(barrier, 16)
    start_early(0, 0)
    start_early(0, 1)
    for c in (*small[6:], *own_gains):
        c.wait()

    def gain_a(which, late, k):
        _, tab = table(which, late)
        mine = (y, x)[which]
        to = bl_of(lax.rem(y + k, 4), x, core) if which == 0 else bl_of(y, lax.rem(x + k, 4), core)
        return rcopy(tab.at[mine], tab.at[mine], gsend.at[which, late, k], grecv.at[which, late, mine], (n, to))

    def gain_a_wait(which, late):
        _, tab = table(which, late)
        for k in (1, 2, 3):
            o = lax.rem((y, x)[which] + k, 4)
            rcopy(tab.at[o], tab.at[o], gsend.at[which, late, k], grecv.at[which, late, o], (n, me)).wait_recv()

    def slot_dev(k, own):
        s = lax.rem(own + k, 8)
        return s, s // 2, lax.rem(s, 2)

    def bas_x(k):
        s, tx, tc = slot_dev(k, x * 2 + core)
        mine = x * 2 + core
        return rcopy(bx_v.at[mine], bx_v.at[mine], bsend.at[0, k], bxr.at[mine], (n, bl_of(y, tx, tc)))

    def bas_y(k):
        s, ty, tc = slot_dev(k, y * 2 + core)
        mine = y * 2 + core
        return rcopy(by_v.at[mine], by_v.at[mine], bsend.at[1, k], byr.at[mine], (n, bl_of(ty, x, tc)))

    for k in (1, 3, 2):
        for which in (0, 1):
            gain_a(which, 0, k).start()

    def start_bas(k):
        bas_x(k).start()
        bas_y(k).start()

    loop(8, start_bas, unroll=1, start=1)

    def meta(k):
        t = lax.rem(n + k, 4)
        return [
            rcopy(a, b, msend.at[i, k], mrecv.at[i, n], (t, me))
            for i, (a, b) in enumerate(
                (
                    (zflags.at[n], zflags.at[n]), (zoffs.at[n], zoffs.at[n]), (zw.at[n], zw.at[n]),
                    (zfirst.at[n], zfirst.at[n]),
                )
            )
        ]

    for k in (1, 3, 2):
        for c in meta(k):
            c.start()
    for k in (1, 3, 2):
        for which in (0, 1):
            gain_a(which, 1, k).start()
    early(1)
    start_early(1, 0)

    def pass_on(st):
        for h in (0, 1):
            for w in (0, 1):
                zcopy(st, w, h).wait_recv()
                forward(st, w, h).start()

    pass_on(0)
    start_early(1, 1)

    def wait_bas(k):
        sx = lax.rem(x * 2 + core + k, 8)
        sy = lax.rem(y * 2 + core + k, 8)
        rcopy(bx_v.at[sx], bx_v.at[sx], bsend.at[0, k], bxr.at[sx], (n, me)).wait_recv()
        rcopy(by_v.at[sy], by_v.at[sy], bsend.at[1, k], byr.at[sy], (n, me)).wait_recv()

    loop(8, wait_bas, unroll=1, start=1)
    to_s0 = pltpu.make_async_copy(bx_v, bx_s, local_sem.at[17])
    to_s1 = pltpu.make_async_copy(by_v, by_s, local_sem.at[18])
    to_s0.start()
    to_s1.start()
    gain_a_wait(0, 0)
    gain_a_wait(1, 0)
    to_s0.wait()
    to_s1.wait()

    slots = (lambda k: lax.rem(x * 2 + core + k, 8), lambda k: lax.rem(y * 2 + core + k, 8))
    asked_of = (bx_s, by_s)
    mine_of = (x * 2 + core, y * 2 + core)

    def pick(which, late, slot):
        out = ((m0, m1), (q0, q1))[late][which]
        _, tab = table(which, late)
        for r in range(ROWS):
            a = asked_of[which][slot, r // 4, r % 4]
            owner = lax.shift_right_logical(a * 5958, 16)
            at = a - owner * OWN_ANT
            ox, oy = (owner >> 1) & 3, owner >> 3
            fixed, moving, here = (ox, oy, x) if which == 0 else (oy, ox, y)
            w = flag((fixed == here) & ((owner & 1) == core))
            for p in range(2):
                out[slot, p, pl.ds(r, 1), :] = w * tab[moving, p, at]

    def gain_b(which, late, k):
        s, t, tc = slot_dev(k, mine_of[which])
        src = ((m0, m1), (q0, q1))[late][which]
        dst = ((c0, c1), (d0, d1))[late][which]
        to = bl_of(y, t, tc) if which == 0 else bl_of(t, x, tc)
        i = 2 * late + which
        return rcopy(src.at[s], dst.at[mine_of[which]], rsend.at[i, k], rrecv.at[i, mine_of[which]], (n, to))

    def send_rows(late):
        def go(k):
            for which in (0, 1):
                pick(which, late, slots[which](k))
                gain_b(which, late, k).start()

        loop(8, go, unroll=1, start=1)
        for which in (0, 1):
            pick(which, late, mine_of[which])
            dst = ((c0, c1), (d0, d1))[late][which]
            src = ((m0, m1), (q0, q1))[late][which]
            dst[mine_of[which]] = src[mine_of[which]]

    def gain_products(late):
        def wait(k):
            for which in (0, 1):
                s = slots[which](k)
                src = ((m0, m1), (q0, q1))[late][which]
                dst = ((c0, c1), (d0, d1))[late][which]
                i = 2 * late + which
                rcopy(src.at[s], dst.at[s], rsend.at[i, k], rrecv.at[i, s], (n, me)).wait_recv()

        loop(8, wait, unroll=1, start=1)
        for which in (0, 1):
            got = ((c0, c1), (d0, d1))[late][which]
            parts = []
            for p in range(2):
                acc = got[0, p]
                for s in range(1, 8):
                    acc = acc + got[s, p]
                parts.append(acc)
            A, B = parts
            cols = pl.ds(((512, 640), (0, 256))[late][which], LATER if late else SOON)
            G[0, :, cols] = A * swap4(A) + B * swap4(B)
            G[1, :, cols] = A * swap4(B) - B * swap4(A)

    send_rows(0)

    gain_a_wait(0, 1)
    gain_a_wait(1, 1)
    send_rows(1)

    samples(2)
    rate2 = phases(2)

    def last(e):
        Y[2, e] = turned(2, rate2, e)

    loop(BINS, last)
    gain_products(0)

    def bin_copy(st, t):
        if st >= 2:
            src = Y.at[2, t, :, pl.ds((st - 2) * HALF, HALF)]
            return rcopy(src, Y2.at[st - 2, me], asend.at[st], arecv.at[st], (n, t))
        return rcopy(S.at[st, t], landed.at[st, me], asend.at[st], arecv.at[st], (n, t))

    def all_bins(st):
        part = pl.ds(0, DEVS - 1)
        if st >= 2:
            return rcopy(Y2.at[st - 2, part], Y2.at[st - 2, part], asend.at[st], arecv.at[st], (n, me))
        return rcopy(S.at[st, part], landed.at[st, part], asend.at[st], arecv.at[st], (n, me))

    low_early = lax.broadcasted_iota(I32, (ROWS, EARLY), 0) < 4

    def gz(k):
        return rcopy(GP.at[n], GP.at[n], gzs.at[k], gzr.at[n], (lax.rem(n + k, 4), me))

    def load_meta():
        for k in (1, 2, 3):
            o = lax.rem(n + k, 4)
            for i, (a, b) in enumerate(
                ((zflags.at[o], zflags.at[o]), (zoffs.at[o], zoffs.at[o]), (zw.at[o], zw.at[o]), (zfirst.at[o], zfirst.at[o]))
            ):
                rcopy(a, b, msend.at[i, k], mrecv.at[i, o], (n, me)).wait_recv()
        to_smem = [
            pltpu.make_async_copy(a, b, local_sem.at[19 + i])
            for i, (a, b) in enumerate(((zoffs, zoffs_s), (zw, zw_s), (zfirst, zfirst_s)))
        ]
        for c in to_smem:
            c.start()
        return to_smem

    def share_gains():
        gain_products(1)
        GP[n] = jnp.where(low_early, G[0, :, pl.ds(0, EARLY)], G[1, :, pl.ds(0, EARLY)])
        for k in (2, 1, 3):
            gz(k).start()

    for g in (0, 1):
        cols = pl.ds(EARLY + g * HALF, HALF)
        gr, gs = G[0, :, cols], G[1, :, cols]
        part = pl.ds(g * HALF, HALF)

        def with_gain(t):
            v = Y[2, t, :, part]
            return gr * v + gs * swap4(v)

        def send_last(k):
            t = lax.rem(me + k, DEVS)
            Y[2, t, :, part] = with_gain(t)
            bin_copy(2 + g, t).start()

        loop(29, send_last, unroll=4, start=1)
        loop(DEVS, send_last, unroll=3, start=29)
        Y2[g, me] = with_gain(me)
        if g == 0:
            share_gains()
            to_smem = load_meta()
    pass_on(1)

    for c in to_smem:
        c.wait()
    first_down, first_up, first_far = zfirst_s[down, 0, 0], zfirst_s[up, 0, 0], zfirst_s[far, 0, 0]

    total = jnp.zeros((1, CH), F32)
    bin_here = n * BINS + me
    for k in range(NIGHTS):
        l = bin_here - zfirst_s[k, 0, 0]
        valid = flag((l >= 0) & (l < BINS))
        lc = jnp.clip(l, 0, BINS - 1)
        off = zoffs_s[k, 0, lc]
        for t in range(TAPS):
            bits = (zflags[k] >> (off + t)) & 1
            total = total + (valid * zw_s[k, t, lc]) * (1.0 - bits.astype(F32))
    wt_ref[...] = total
    scale = 1.0 / jnp.maximum(total, 0.5)

    def put(begin, k, a, b, inv):
        a, b = a * inv, b * inv
        low = lax.broadcasted_iota(I32, a.shape, 0) < 4
        at = pl.multiple_of(k * 8, 8)
        cols = pl.ds(begin, a.shape[1])
        out_ref[0, pl.ds(at, 8), cols] = jnp.where(low, a, swap4(b))
        out_ref[1, pl.ds(at, 8), cols] = jnp.where(low, swap4(a), b)

    def scale_of(st):
        return jnp.broadcast_to(scale[:, st * WIDE : (st + 1) * WIDE], (ROWS, WIDE))

    def last_first(g):
        all_bins(2 + g).wait_recv()
        s = shift_of(first, n, me)
        loop(HB, lambda j: first_message(2, g * HB + j, s, Y2[g, j], Y2[g, HB + j]))
        zcopy(2, 0, g).start()
        zcopy(2, 1, g).start()

    def last_second(g):
        zcopy(2, 0, g).wait_recv()
        zcopy(2, 1, g).wait_recv()
        loop(HB, lambda j: second_message(2, g * HB + j, me, Y2[g, j], Y2[g, HB + j]))
        zcopy(2, 2, g).start()
        zcopy(2, 3, g).start()

    def unpack_gains():
        for k in (1, 2, 3):
            o = lax.rem(n + k, 4)
            rcopy(GP.at[o], GP.at[o], gzs.at[k], gzr.at[o], (n, me)).wait_recv()
        for k in range(NIGHTS):
            packed = GP[k]
            turned_over = swap4(packed)
            GZ[k, 0] = jnp.where(low_early, packed, turned_over)
            GZ[k, 1] = jnp.where(low_early, -turned_over, packed)

    def combine(st, e):
        here = flag(shift_of(first, n, e) == 0)
        from_down = flag(shift_of(first_down, down, e) == 1)
        from_up = flag(shift_of(first_up, up, e) == 3)
        from_far = flag(shift_of(first_far, far, e) == 2)

        def part(half, terms):
            cols = pl.ds(st * WIDE + half * HALF, HALF)
            acc = None
            for night, v in terms:
                w = GZ[night, 0, :, cols] * v + GZ[night, 1, :, cols] * swap4(v)
                acc = w if acc is None else acc + w
            return acc

        a = part(
            0,
            (
                (n, here * Y[st, e, :, lo]), (up, from_up * r1n[st, e]), (down, r2p[st, e]),
                (far, from_far * r3p[st, e]),
            ),
        )
        b = part(
            1,
            (
                (n, here * Y[st, e, :, hi]), (down, from_down * r1p[st, e]), (up, r2n[st, e]),
                (far, from_far * r3n[st, e]),
            ),
        )
        return a, b

    def finish_early(st):
        for h in (0, 1):
            zcopy(st, 2, h).wait_recv()
            zcopy(st, 3, h).wait_recv()
            forward(st, 0, h).wait_recv()
            forward(st, 1, h).wait_recv()

        def go(k):
            t = lax.rem(me + k, DEVS)
            a, b = combine(st, t)
            S[st, t, :, lo] = a
            S[st, t, :, hi] = b
            bin_copy(st, t).start()

        loop(29, go, unroll=4, start=1)
        loop(DEVS, go, unroll=3, start=29)
        a, b = combine(st, me)
        landed[st, me, :, lo] = a
        landed[st, me, :, hi] = b

    last_first(0)
    unpack_gains()
    finish_early(0)
    last_first(1)
    finish_early(1)
    last_second(0)
    last_second(1)

    def assemble(st):
        all_bins(st).wait_recv()
        inv = scale_of(st)
        loop(DEVS // 2, lambda k: put(st * WIDE, k, landed[st, 2 * k], landed[st, 2 * k + 1], inv))

    assemble(0)

    for k in (1, 2, 3):
        for which in (0, 1):
            for late in (0, 1):
                gain_a(which, late, k).wait_send()
        for c in meta(k):
            c.wait_send()
        gz(k).wait_send()

    def done(k):
        bas_x(k).wait_send()
        bas_y(k).wait_send()
        for which in (0, 1):
            for late in (0, 1):
                gain_b(which, late, k).wait_send()

    loop(8, done, unroll=1, start=1)
    for h in (0, 1):
        for st in range(STAGES):
            for w in range(4 if st < 2 else 2):
                zcopy(st, w, h).wait_send()
        for w in (0, 1):
            for st in (0, 1):
                forward(st, w, h).wait_send()
    for st in (0, 2, 3):
        all_bins(st).wait_send()

    here2 = flag(shift_of(first, n, me) == 0)
    down2 = flag(shift_of(first_down, down, me) == 1)
    up2 = flag(shift_of(first_up, up, me) == 3)
    for g in (0, 1):
        zcopy(2, 2, g).wait_recv()
        zcopy(2, 3, g).wait_recv()
        inv2 = scale_of(2)[:, g * HALF : (g + 1) * HALF]

        def finish(k):
            lower = [
                here2 * Y2[g, j] + up2 * r1n[2, g * HB + j] + r2p[2, g * HB + j] for j in (2 * k, 2 * k + 1)
            ]
            upper = [
                here2 * Y2[g, HB + j] + down2 * r1p[2, g * HB + j] + r2n[2, g * HB + j] for j in (2 * k, 2 * k + 1)
            ]
            put(EARLY + g * HALF, k, *lower, inv2)
            put(EARLY + g * HALF, HB // 2 + k, *upper, inv2)

        loop(HB // 2, finish)
    assemble(1)
    for h in (0, 1):
        zcopy(2, 2, h).wait_send()
        zcopy(2, 3, h).wait_send()
    all_bins(1).wait_send()


def place_kernel(binned, wt, out, wt_out, sems):
    copies = [
        pltpu.make_async_copy(binned.at[p, pl.ds(k * 64, 64)], out.at[p, pl.ds(k * 64, 64)], sems.at[2 * p + k])
        for p in range(2)
        for k in range(2)
    ]
    copies.append(pltpu.make_async_copy(wt, wt_out, sems.at[4]))
    for c in copies:
        c.start()
    for c in copies:
        c.wait()


def per_device(
    visibilities, corrupted_sample_markers, antenna_gain_table, baseline_antennas, first_bin, tap_offsets, tap_weights,
    lst_delay, fringe_rate,
):
    vis = jnp.transpose(visibilities[:, 0], (0, 2, 1, 3))
    gains = jnp.transpose(antenna_gain_table, (0, 2, 1, 3))
    weights = jnp.transpose(tap_weights[0], (1, 0))
    bas = jnp.transpose(baseline_antennas, (1, 0))

    def held(a):
        return pltpu.with_memory_space_constraint(a, pltpu.HBM)

    vm = pl.BlockSpec(memory_space=pltpu.VMEM)
    hbm = pl.BlockSpec(memory_space=pltpu.HBM)
    D = pltpu.SemaphoreType.DMA
    msg = (STAGES, BINS, ROWS, HALF)
    binned, weight_total = pl.pallas_call(
        comm_kernel,
        out_shape=(
            pltpu.VMEM((2, 4 * DEVS, CH), F32),
            pltpu.VMEM((1, CH), F32),
        ),
        in_specs=[hbm] * 9,
        out_specs=(vm, vm),
        scratch_shapes=[
            pltpu.SMEM((1, BINS), I32),
            pltpu.SMEM((1,), I32),
            pltpu.SMEM((TAPS, BINS), F32),
            pltpu.SMEM((1, BINS), F32),
            pltpu.SMEM((4,), F32),
            pltpu.VMEM((2, SAMPLES, 4, CH), F32),
            pltpu.VMEM((SAMPLES, ROWS, CH), F32),
            pltpu.VMEM((STAGES, BINS, ROWS, WIDE), F32),
            pltpu.VMEM((2, DEVS, ROWS, HALF), F32),
            pltpu.VMEM((2, BINS, ROWS, WIDE), F32),
            pltpu.VMEM((2, DEVS, ROWS, WIDE), F32),
            *([pltpu.VMEM((4, 2, OWN_ANT, 1, SOON), F32)] * 2),
            *([pltpu.VMEM((4, 2, OWN_ANT, 1, LATER), F32)] * 2),
            pltpu.VMEM((8, 2, 4), I32),
            pltpu.VMEM((8, 2, 4), I32),
            pltpu.SMEM((8, 2, 4), I32),
            pltpu.SMEM((8, 2, 4), I32),
            *([pltpu.VMEM((8, 2, ROWS, SOON), F32)] * 4),
            *([pltpu.VMEM((8, 2, ROWS, LATER), F32)] * 4),
            pltpu.VMEM((2, ROWS, CH), F32),
            pltpu.VMEM((NIGHTS, ROWS, EARLY), F32),
            pltpu.VMEM((NIGHTS, 2, ROWS, EARLY), F32),
            pltpu.VMEM((NIGHTS, 1, CH), I32),
            pltpu.VMEM((NIGHTS, 1, HALF), I32),
            pltpu.VMEM((NIGHTS, 1, BINS), I32),
            pltpu.VMEM((NIGHTS, TAPS, BINS), F32),
            pltpu.SMEM((NIGHTS, 1, HALF), I32),
            pltpu.SMEM((NIGHTS, 1, BINS), I32),
            pltpu.SMEM((NIGHTS, TAPS, BINS), F32),
        ]
        + [pltpu.VMEM(msg, F32)] * 8
        + [pltpu.VMEM((2,) + msg[1:], F32)] * 2
        + [
            D((22,)), D((2, 2, 4)), D((2, 2, 4)), D((2, 8)), D((8,)), D((8,)), D((4, 4)), D((4, 4)),
            D((4, 8)), D((4, 8)), D((STAGES + 2, 4, 2)), D((STAGES + 2, 4, 2)), D((4,)), D((4,)),
            D((STAGES + 1,)), D((STAGES + 1,)),
        ],
        compiler_params=pltpu.CompilerParams(
            collective_id=0, has_side_effects=True, vmem_limit_bytes=48 * 1024 * 1024
        ),
        name="exchange",
    )(
        held(vis), held(gains), held(corrupted_sample_markers), held(tap_offsets), first_bin, held(weights),
        held(lst_delay), held(bas), held(fringe_rate),
    )
    binned, weight_total = pl.pallas_call(
        place_kernel,
        out_shape=(jax.ShapeDtypeStruct((2, 4 * DEVS, CH), F32), jax.ShapeDtypeStruct((1, CH), F32)),
        in_specs=[vm, vm],
        out_specs=(hbm, hbm),
        scratch_shapes=[D((5,))],
        compiler_params=pltpu.CompilerParams(vmem_limit_bytes=8 * 1024 * 1024),
        name="place",
    )(binned, weight_total)
    return binned.reshape(2, 1, 4 * DEVS, CH), weight_total


def solution(mesh):
    placed = (
        P(None, "night", "bl", None, None),
        P("night", None),
        P(None, "night", "bl", None),
        P("bl", None),
        P("night"),
        P("night", None),
        P("night", None, None),
        P("night", None),
        P("bl"),
    )
    return jax.shard_map(
        per_device,
        mesh=mesh,
        in_specs=placed,
        out_specs=(P(None, ("night", "bl"), None, None), P(("night", "bl"), None)),
        check_vma=False,
    )
```

```python
import functools
import math

import jax
import jax.numpy as jnp
import numpy as np
from jax import lax
from jax.experimental import pallas as pl
from jax.experimental.pallas import tpu as pltpu
from jax.sharding import PartitionSpec as P

MESH = pl.DeviceIdType.MESH
F32 = jnp.float32
I32 = jnp.int32

NIGHTS = 4
DEVS = 32
BINS = 32
ROWS = 8
CH = 768
SAMPLES = 30
TAPS = 4
OWN_ANT = 11
STAGES = 3
WIDE = 256
HALF = 128
SOON = 128
LATER = 256
EARLY = 512
HB = 16


def _fit(kind, terms):
    k = np.arange(200)
    u = 0.125 * (1 + np.cos(np.pi * (k + 0.5) / 200))
    r = np.sqrt(u)
    y = np.sin(2 * np.pi * r) / r if kind == "sin" else np.cos(2 * np.pi * r)
    cheb = np.polynomial.chebyshev.Chebyshev.fit(u, y, terms - 1, domain=[0, 0.25])
    return [float(v) for v in cheb.convert(kind=np.polynomial.Polynomial).coef]


SIN_C = _fit("sin", 8)
COS_C = _fit("cos", 8)


def horner(coef, u):
    acc = jnp.full_like(u, coef[-1])
    for c in coef[-2::-1]:
        acc = acc * u + c
    return acc


def swap4(v):
    return pltpu.roll(v, 4, 0)


def flag(cond):
    return jnp.where(cond, jnp.float32(1.0), jnp.float32(0.0))


def comm_kernel(
    vis, gains, flags_h, offs_h, first_h, weights_h, delay_h, bas_h, rate_h,
    out_ref, wt_ref,
    offs_s, first_s, weights_s, delay_s, rate_s, V, UV, Y, Y2, S, landed, gyu, gxu, gyl, gxl, bx_v, by_v, bx_s, by_s,
    m0, m1, c0, c1, q0, q1, d0, d1, G, GP, GZ,
    zflags, zfirst, zoffs, zw, zfirst_s, zoffs_s, zw_s, s1p, s1n, s2p, s2n, r1p, r1n, r2p, r2n, r3p, r3n,
    local_sem, gsend, grecv, bsend, bxr, byr, msend, mrecv,
    rsend, rrecv, zsend, zrecv, gzs, gzr, asend, arecv,
):
    n = lax.axis_index("night")
    me = lax.axis_index("bl")
    core = lax.rem(me, 2)
    x = lax.rem(me // 2, 4)
    y = me // 8

    def bl_of(yy, xx, cc):
        return (yy * 4 + xx) * 2 + cc

    def rcopy(src, dst, ss, rs, dev):
        return pltpu.make_async_remote_copy(
            src_ref=src, dst_ref=dst, send_sem=ss, recv_sem=rs, device_id=dev, device_id_type=MESH
        )

    def loop(count, body, unroll=4, start=0):
        def step(i, c):
            body(i)
            return c

        lax.fori_loop(start, count, step, 0, unroll=unroll)

    load_vis = [
        pltpu.make_async_copy(
            vis.at[:, :, :, pl.ds(st * WIDE, WIDE)], V.at[:, :, :, pl.ds(st * WIDE, WIDE)], local_sem.at[st]
        )
        for st in range(STAGES)
    ]

    def table(which, late):
        begin = ((512, 640), (0, 256))[late][which]
        return gains.at[:, :, :, pl.ds(begin, LATER if late else SOON)], ((gyu, gxu), (gyl, gxl))[late][which]

    own_gains = []
    for late in (0, 1):
        for which in (0, 1):
            src, dst = table(which, late)
            own_gains.append(pltpu.make_async_copy(src, dst.at[(y, x)[which]], local_sem.at[3 + 2 * late + which]))
    small = [
        pltpu.make_async_copy(a, b, local_sem.at[7 + i])
        for i, (a, b) in enumerate(
            (
                (first_h, first_s), (offs_h, offs_s), (weights_h, weights_s), (delay_h, delay_s), (rate_h, rate_s),
                (flags_h, zflags.at[n]), (offs_h, zoffs.at[n]), (weights_h, zw.at[n]),
                (bas_h, bx_v.at[x * 2 + core]), (bas_h, by_v.at[y * 2 + core]),
            )
        )
    ]
    for c in (load_vis[0], *small[:6]):
        c.start()

    barrier = pltpu.get_barrier_semaphore()

    def greet(device):
        pl.semaphore_signal(barrier, inc=1, device_id=device, device_id_type=MESH)

    for k in (1, 2, 3):
        greet((lax.rem(n + k, 4), me))
    greet((n, bl_of(y, x, 1 - core)))
    for k in (1, 2, 3):
        for cc in range(2):
            greet((n, bl_of(y, lax.rem(x + k, 4), cc)))
            greet((n, bl_of(lax.rem(y + k, 4), x, cc)))
    for c in (*small[6:], *own_gains, *load_vis[1:]):
        c.start()

    lane = lax.broadcasted_iota(I32, (ROWS, WIDE), 1).astype(F32)
    row = lax.broadcasted_iota(I32, (ROWS, WIDE), 0)
    sign = jnp.where(row < 4, jnp.float32(-1.0), jnp.float32(1.0))
    for c in small[:6]:
        c.wait()
    first = first_s[0]
    zfirst[n] = jnp.full((1, HALF), first, I32)
    which_row = row & 3
    rates = jnp.where(
        which_row < 2,
        jnp.where(which_row == 0, rate_s[0], rate_s[1]),
        jnp.where(which_row == 2, rate_s[2], rate_s[3]),
    ) * (1.0 / (2.0 * math.pi))

    def samples(st):
        at = st * WIDE
        load_vis[st].wait()

        def per_sample(t):
            bits = (zflags[n, :, pl.ds(at, WIDE)] >> t) & 1
            both = jnp.concatenate([V[0, t, :, pl.ds(at, WIDE)], V[1, t, :, pl.ds(at, WIDE)]], axis=0)
            UV[t, :, pl.ds(at, WIDE)] = both * (1.0 - bits.astype(F32))

        loop(SAMPLES, per_sample, unroll=5)

    def shift_of(f, night, e):
        return (lax.shift_right_logical(f, 5) + jnp.where(e < (f & 31), 1, 0) - night) & 3

    def phases(st):
        return rates * (1.0 + (lane + float(st * WIDE)) * (1.0 / CH))

    def turned(st, rate, e):
        at = st * WIDE
        l = (e - first) & 31
        off = offs_s[0, l]
        acc = weights_s[0, l] * UV[off, :, pl.ds(at, WIDE)]
        for k in range(1, TAPS):
            acc = acc + weights_s[k, l] * UV[off + k, :, pl.ds(at, WIDE)]
        turns = rate * delay_s[0, l]
        r = turns - jnp.floor(turns + 0.5)
        u = r * r
        return horner(COS_C, u) * acc + (horner(SIN_C, u) * (r * sign)) * swap4(acc)

    up = lax.rem(n + 1, 4)
    down = lax.rem(n + 3, 4)
    far = lax.rem(n + 2, 4)

    def zcopy(st, which, h):
        src = (s1p, s1n, s2p, s2n)[which].at[st, pl.ds(h * HB, HB)]
        dst = (r1p, r1n, r2p, r2n)[which].at[st, pl.ds(h * HB, HB)]
        to = up if which % 2 == 0 else down
        return rcopy(src, dst, zsend.at[st, which, h], zrecv.at[st, which, h], (to, me))

    def forward(st, which, h):
        src, dst = ((r1p, r3p), (r1n, r3n))[which]
        part = pl.ds(h * HB, HB)
        to = (up, down)[which]
        return rcopy(
            src.at[st, part], dst.at[st, part], zsend.at[STAGES + st, which, h], zrecv.at[STAGES + st, which, h], (to, me)
        )

    lo = pl.ds(0, HALF)
    hi = pl.ds(HALF, HALF)

    def first_message(st, i, s, a, b):
        two = flag(s == 2)
        s1p[st, i] = two * a + flag(s == 1) * b
        s1n[st, i] = two * b + flag(s == 3) * a

    def second_message(st, i, e, a, b):
        s = shift_of(first, n, e)
        s2p[st, i] = flag(s == 1) * a + flag(shift_of(first_down, down, e) == 2) * r1p[st, i]
        s2n[st, i] = flag(s == 3) * b + flag(shift_of(first_up, up, e) == 2) * r1n[st, i]

    def early(st):
        samples(st)
        rate = phases(st)

        def per_bin(e):
            v = turned(st, rate, e)
            Y[st, e] = v
            a, b = v[:, :HALF], v[:, HALF:]
            s = shift_of(first, n, e)
            first_message(st, e, s, a, b)
            s2p[st, e] = flag(s == 1) * a
            s2n[st, e] = flag(s == 3) * b

        loop(BINS, per_bin)

    def start_early(st, message):
        for h in (0, 1):
            for w in (0, 1):
                zcopy(st, 2 * message + w, h).start()

    early(0)
    pl.semaphore_wait(barrier, 16)
    start_early(0, 0)
    start_early(0, 1)
    for c in (*small[6:], *own_gains):
        c.wait()

    def gain_a(which, late, k):
        _, tab = table(which, late)
        mine = (y, x)[which]
        to = bl_of(lax.rem(y + k, 4), x, core) if which == 0 else bl_of(y, lax.rem(x + k, 4), core)
        return rcopy(tab.at[mine], tab.at[mine], gsend.at[which, late, k], grecv.at[which, late, mine], (n, to))

    def gain_a_wait(which, late):
        _, tab = table(which, late)
        for k in (1, 2, 3):
            o = lax.rem((y, x)[which] + k, 4)
            rcopy(tab.at[o], tab.at[o], gsend.at[which, late, k], grecv.at[which, late, o], (n, me)).wait_recv()

    def slot_dev(k, own):
        s = lax.rem(own + k, 8)
        return s, s // 2, lax.rem(s, 2)

    def bas_x(k):
        s, tx, tc = slot_dev(k, x * 2 + core)
        mine = x * 2 + core
        return rcopy(bx_v.at[mine], bx_v.at[mine], bsend.at[0, k], bxr.at[mine], (n, bl_of(y, tx, tc)))

    def bas_y(k):
        s, ty, tc = slot_dev(k, y * 2 + core)
        mine = y * 2 + core
        return rcopy(by_v.at[mine], by_v.at[mine], bsend.at[1, k], byr.at[mine], (n, bl_of(ty, x, tc)))

    for k in (1, 3, 2):
        for which in (0, 1):
            gain_a(which, 0, k).start()

    def start_bas(k):
        bas_x(k).start()
        bas_y(k).start()

    loop(8, start_bas, unroll=1, start=1)

    def meta(k):
        t = lax.rem(n + k, 4)
        return [
            rcopy(a, b, msend.at[i, k], mrecv.at[i, n], (t, me))
            for i, (a, b) in enumerate(
                (
                    (zflags.at[n], zflags.at[n]), (zoffs.at[n], zoffs.at[n]), (zw.at[n], zw.at[n]),
                    (zfirst.at[n], zfirst.at[n]),
                )
            )
        ]

    for k in (1, 3, 2):
        for c in meta(k):
            c.start()
    for k in (1, 3, 2):
        for which in (0, 1):
            gain_a(which, 1, k).start()
    early(1)
    start_early(1, 0)

    def pass_on(st):
        for h in (0, 1):
            for w in (0, 1):
                zcopy(st, w, h).wait_recv()
                forward(st, w, h).start()

    pass_on(0)
    start_early(1, 1)

    def wait_bas(k):
        sx = lax.rem(x * 2 + core + k, 8)
        sy = lax.rem(y * 2 + core + k, 8)
        rcopy(bx_v.at[sx], bx_v.at[sx], bsend.at[0, k], bxr.at[sx], (n, me)).wait_recv()
        rcopy(by_v.at[sy], by_v.at[sy], bsend.at[1, k], byr.at[sy], (n, me)).wait_recv()

    loop(8, wait_bas, unroll=1, start=1)
    to_s0 = pltpu.make_async_copy(bx_v, bx_s, local_sem.at[17])
    to_s1 = pltpu.make_async_copy(by_v, by_s, local_sem.at[18])
    to_s0.start()
    to_s1.start()
    gain_a_wait(0, 0)
    gain_a_wait(1, 0)
    to_s0.wait()
    to_s1.wait()

    slots = (lambda k: lax.rem(x * 2 + core + k, 8), lambda k: lax.rem(y * 2 + core + k, 8))
    asked_of = (bx_s, by_s)
    mine_of = (x * 2 + core, y * 2 + core)

    def pick(which, late, slot):
        out = ((m0, m1), (q0, q1))[late][which]
        _, tab = table(which, late)
        for r in range(ROWS):
            a = asked_of[which][slot, r // 4, r % 4]
            owner = lax.shift_right_logical(a * 5958, 16)
            at = a - owner * OWN_ANT
            ox, oy = (owner >> 1) & 3, owner >> 3
            fixed, moving, here = (ox, oy, x) if which == 0 else (oy, ox, y)
            w = flag((fixed == here) & ((owner & 1) == core))
            for p in range(2):
                out[slot, p, pl.ds(r, 1), :] = w * tab[moving, p, at]

    def gain_b(which, late, k):
        s, t, tc = slot_dev(k, mine_of[which])
        src = ((m0, m1), (q0, q1))[late][which]
        dst = ((c0, c1), (d0, d1))[late][which]
        to = bl_of(y, t, tc) if which == 0 else bl_of(t, x, tc)
        i = 2 * late + which
        return rcopy(src.at[s], dst.at[mine_of[which]], rsend.at[i, k], rrecv.at[i, mine_of[which]], (n, to))

    def send_rows(late):
        def go(k):
            for which in (0, 1):
                pick(which, late, slots[which](k))
                gain_b(which, late, k).start()

        loop(8, go, unroll=1, start=1)
        for which in (0, 1):
            pick(which, late, mine_of[which])
            dst = ((c0, c1), (d0, d1))[late][which]
            src = ((m0, m1), (q0, q1))[late][which]
            dst[mine_of[which]] = src[mine_of[which]]

    def gain_products(late):
        def wait(k):
            for which in (0, 1):
                s = slots[which](k)
                src = ((m0, m1), (q0, q1))[late][which]
                dst = ((c0, c1), (d0, d1))[late][which]
                i = 2 * late + which
                rcopy(src.at[s], dst.at[s], rsend.at[i, k], rrecv.at[i, s], (n, me)).wait_recv()

        loop(8, wait, unroll=1, start=1)
        for which in (0, 1):
            got = ((c0, c1), (d0, d1))[late][which]
            parts = []
            for p in range(2):
                acc = got[0, p]
                for s in range(1, 8):
                    acc = acc + got[s, p]
                parts.append(acc)
            A, B = parts
            cols = pl.ds(((512, 640), (0, 256))[late][which], LATER if late else SOON)
            G[0, :, cols] = A * swap4(A) + B * swap4(B)
            G[1, :, cols] = A * swap4(B) - B * swap4(A)

    send_rows(0)

    gain_a_wait(0, 1)
    gain_a_wait(1, 1)
    send_rows(1)

    samples(2)
    rate2 = phases(2)

    def last(e):
        Y[2, e] = turned(2, rate2, e)

    loop(BINS, last)
    gain_products(0)

    def bin_copy(st, t):
        if st >= 2:
            src = Y.at[2, t, :, pl.ds((st - 2) * HALF, HALF)]
            return rcopy(src, Y2.at[st - 2, me], asend.at[st], arecv.at[st], (n, t))
        return rcopy(S.at[st, t], landed.at[st, me], asend.at[st], arecv.at[st], (n, t))

    def all_bins(st):
        part = pl.ds(0, DEVS - 1)
        if st >= 2:
            return rcopy(Y2.at[st - 2, part], Y2.at[st - 2, part], asend.at[st], arecv.at[st], (n, me))
        return rcopy(S.at[st, part], landed.at[st, part], asend.at[st], arecv.at[st], (n, me))

    low_early = lax.broadcasted_iota(I32, (ROWS, EARLY), 0) < 4

    def gz(k):
        return rcopy(GP.at[n], GP.at[n], gzs.at[k], gzr.at[n], (lax.rem(n + k, 4), me))

    def load_meta():
        for k in (1, 2, 3):
            o = lax.rem(n + k, 4)
            for i, (a, b) in enumerate(
                ((zflags.at[o], zflags.at[o]), (zoffs.at[o], zoffs.at[o]), (zw.at[o], zw.at[o]), (zfirst.at[o], zfirst.at[o]))
            ):
                rcopy(a, b, msend.at[i, k], mrecv.at[i, o], (n, me)).wait_recv()
        to_smem = [
            pltpu.make_async_copy(a, b, local_sem.at[19 + i])
            for i, (a, b) in enumerate(((zoffs, zoffs_s), (zw, zw_s), (zfirst, zfirst_s)))
        ]
        for c in to_smem:
            c.start()
        return to_smem

    def share_gains():
        gain_products(1)
        GP[n] = jnp.where(low_early, G[0, :, pl.ds(0, EARLY)], G[1, :, pl.ds(0, EARLY)])
        for k in (2, 1, 3):
            gz(k).start()

    for g in (0, 1):
        cols = pl.ds(EARLY + g * HALF, HALF)
        gr, gs = G[0, :, cols], G[1, :, cols]
        part = pl.ds(g * HALF, HALF)

        def with_gain(t):
            v = Y[2, t, :, part]
            return gr * v + gs * swap4(v)

        def send_last(k):
            t = lax.rem(me + k, DEVS)
            Y[2, t, :, part] = with_gain(t)
            bin_copy(2 + g, t).start()

        loop(29, send_last, unroll=4, start=1)
        loop(DEVS, send_last, unroll=3, start=29)
        Y2[g, me] = with_gain(me)
        if g == 0:
            share_gains()
            to_smem = load_meta()
    pass_on(1)

    for c in to_smem:
        c.wait()
    first_down, first_up, first_far = zfirst_s[down, 0, 0], zfirst_s[up, 0, 0], zfirst_s[far, 0, 0]

    total = jnp.zeros((1, CH), F32)
    bin_here = n * BINS + me
    for k in range(NIGHTS):
        l = bin_here - zfirst_s[k, 0, 0]
        valid = flag((l >= 0) & (l < BINS))
        lc = jnp.clip(l, 0, BINS - 1)
        off = zoffs_s[k, 0, lc]
        for t in range(TAPS):
            bits = (zflags[k] >> (off + t)) & 1
            total = total + (valid * zw_s[k, t, lc]) * (1.0 - bits.astype(F32))
    wt_ref[...] = total
    scale = 1.0 / jnp.maximum(total, 0.5)

    def put(begin, k, a, b, inv):
        a, b = a * inv, b * inv
        low = lax.broadcasted_iota(I32, a.shape, 0) < 4
        at = pl.multiple_of(k * 8, 8)
        cols = pl.ds(begin, a.shape[1])
        out_ref[0, pl.ds(at, 8), cols] = jnp.where(low, a, swap4(b))
        out_ref[1, pl.ds(at, 8), cols] = jnp.where(low, swap4(a), b)

    def scale_of(st):
        return jnp.broadcast_to(scale[:, st * WIDE : (st + 1) * WIDE], (ROWS, WIDE))

    def last_first(g):
        all_bins(2 + g).wait_recv()
        s = shift_of(first, n, me)
        loop(HB, lambda j: first_message(2, g * HB + j, s, Y2[g, j], Y2[g, HB + j]))
        zcopy(2, 0, g).start()
        zcopy(2, 1, g).start()

    def last_second(g):
        zcopy(2, 0, g).wait_recv()
        zcopy(2, 1, g).wait_recv()
        loop(HB, lambda j: second_message(2, g * HB + j, me, Y2[g, j], Y2[g, HB + j]))
        zcopy(2, 2, g).start()
        zcopy(2, 3, g).start()

    def unpack_gains():
        for k in (1, 2, 3):
            o = lax.rem(n + k, 4)
            rcopy(GP.at[o], GP.at[o], gzs.at[k], gzr.at[o], (n, me)).wait_recv()
        for k in range(NIGHTS):
            packed = GP[k]
            turned_over = swap4(packed)
            GZ[k, 0] = jnp.where(low_early, packed, turned_over)
            GZ[k, 1] = jnp.where(low_early, -turned_over, packed)

    def combine(st, e):
        here = flag(shift_of(first, n, e) == 0)
        from_down = flag(shift_of(first_down, down, e) == 1)
        from_up = flag(shift_of(first_up, up, e) == 3)
        from_far = flag(shift_of(first_far, far, e) == 2)

        def part(half, terms):
            cols = pl.ds(st * WIDE + half * HALF, HALF)
            acc = None
            for night, v in terms:
                w = GZ[night, 0, :, cols] * v + GZ[night, 1, :, cols] * swap4(v)
                acc = w if acc is None else acc + w
            return acc

        a = part(
            0,
            (
                (n, here * Y[st, e, :, lo]), (up, from_up * r1n[st, e]), (down, r2p[st, e]),
                (far, from_far * r3p[st, e]),
            ),
        )
        b = part(
            1,
            (
                (n, here * Y[st, e, :, hi]), (down, from_down * r1p[st, e]), (up, r2n[st, e]),
                (far, from_far * r3n[st, e]),
            ),
        )
        return a, b

    def finish_early(st):
        for h in (0, 1):
            zcopy(st, 2, h).wait_recv()
            zcopy(st, 3, h).wait_recv()
            forward(st, 0, h).wait_recv()
            forward(st, 1, h).wait_recv()

        def go(k):
            t = lax.rem(me + k, DEVS)
            a, b = combine(st, t)
            S[st, t, :, lo] = a
            S[st, t, :, hi] = b
            bin_copy(st, t).start()

        loop(29, go, unroll=4, start=1)
        loop(DEVS, go, unroll=3, start=29)
        a, b = combine(st, me)
        landed[st, me, :, lo] = a
        landed[st, me, :, hi] = b

    last_first(0)
    unpack_gains()
    finish_early(0)
    last_first(1)
    finish_early(1)
    last_second(0)
    last_second(1)

    def assemble(st):
        all_bins(st).wait_recv()
        inv = scale_of(st)
        loop(DEVS // 2, lambda k: put(st * WIDE, k, landed[st, 2 * k], landed[st, 2 * k + 1], inv))

    assemble(0)

    for k in (1, 2, 3):
        for which in (0, 1):
            for late in (0, 1):
                gain_a(which, late, k).wait_send()
        for c in meta(k):
            c.wait_send()
        gz(k).wait_send()

    def done(k):
        bas_x(k).wait_send()
        bas_y(k).wait_send()
        for which in (0, 1):
            for late in (0, 1):
                gain_b(which, late, k).wait_send()

    loop(8, done, unroll=1, start=1)
    for h in (0, 1):
        for st in range(STAGES):
            for w in range(4 if st < 2 else 2):
                zcopy(st, w, h).wait_send()
        for w in (0, 1):
            for st in (0, 1):
                forward(st, w, h).wait_send()
    for st in (0, 2, 3):
        all_bins(st).wait_send()

    here2 = flag(shift_of(first, n, me) == 0)
    down2 = flag(shift_of(first_down, down, me) == 1)
    up2 = flag(shift_of(first_up, up, me) == 3)
    for g in (0, 1):
        zcopy(2, 2, g).wait_recv()
        zcopy(2, 3, g).wait_recv()
        inv2 = scale_of(2)[:, g * HALF : (g + 1) * HALF]

        def finish(k):
            lower = [
                here2 * Y2[g, j] + up2 * r1n[2, g * HB + j] + r2p[2, g * HB + j] for j in (2 * k, 2 * k + 1)
            ]
            upper = [
                here2 * Y2[g, HB + j] + down2 * r1p[2, g * HB + j] + r2n[2, g * HB + j] for j in (2 * k, 2 * k + 1)
            ]
            put(EARLY + g * HALF, k, *lower, inv2)
            put(EARLY + g * HALF, HB // 2 + k, *upper, inv2)

        loop(HB // 2, finish)
    assemble(1)
    for h in (0, 1):
        zcopy(2, 2, h).wait_send()
        zcopy(2, 3, h).wait_send()
    all_bins(1).wait_send()


def place_kernel(binned, wt, out, wt_out, sems):
    copies = [
        pltpu.make_async_copy(binned.at[p, pl.ds(k * 16, 16)], out.at[p, pl.ds(k * 16, 16)], sems.at[8 * p + k])
        for p in range(2)
        for k in range(8)
    ]
    copies.append(pltpu.make_async_copy(wt, wt_out, sems.at[16]))
    for c in copies:
        c.start()
    for c in copies:
        c.wait()


def per_device(
    visibilities, corrupted_sample_markers, antenna_gain_table, baseline_antennas, first_bin, tap_offsets, tap_weights,
    lst_delay, fringe_rate,
):
    vis = jnp.transpose(visibilities[:, 0], (0, 2, 1, 3))
    gains = jnp.transpose(antenna_gain_table, (0, 2, 1, 3))
    weights = jnp.transpose(tap_weights[0], (1, 0))
    bas = jnp.transpose(baseline_antennas, (1, 0))

    def held(a):
        return pltpu.with_memory_space_constraint(a, pltpu.HBM)

    vm = pl.BlockSpec(memory_space=pltpu.VMEM)
    hbm = pl.BlockSpec(memory_space=pltpu.HBM)
    D = pltpu.SemaphoreType.DMA
    msg = (STAGES, BINS, ROWS, HALF)
    binned, weight_total = pl.pallas_call(
        comm_kernel,
        out_shape=(
            pltpu.VMEM((2, 4 * DEVS, CH), F32),
            pltpu.VMEM((1, CH), F32),
        ),
        in_specs=[hbm] * 9,
        out_specs=(vm, vm),
        scratch_shapes=[
            pltpu.SMEM((1, BINS), I32),
            pltpu.SMEM((1,), I32),
            pltpu.SMEM((TAPS, BINS), F32),
            pltpu.SMEM((1, BINS), F32),
            pltpu.SMEM((4,), F32),
            pltpu.VMEM((2, SAMPLES, 4, CH), F32),
            pltpu.VMEM((SAMPLES, ROWS, CH), F32),
            pltpu.VMEM((STAGES, BINS, ROWS, WIDE), F32),
            pltpu.VMEM((2, DEVS, ROWS, HALF), F32),
            pltpu.VMEM((2, BINS, ROWS, WIDE), F32),
            pltpu.VMEM((2, DEVS, ROWS, WIDE), F32),
            *([pltpu.VMEM((4, 2, OWN_ANT, 1, SOON), F32)] * 2),
            *([pltpu.VMEM((4, 2, OWN_ANT, 1, LATER), F32)] * 2),
            pltpu.VMEM((8, 2, 4), I32),
            pltpu.VMEM((8, 2, 4), I32),
            pltpu.SMEM((8, 2, 4), I32),
            pltpu.SMEM((8, 2, 4), I32),
            *([pltpu.VMEM((8, 2, ROWS, SOON), F32)] * 4),
            *([pltpu.VMEM((8, 2, ROWS, LATER), F32)] * 4),
            pltpu.VMEM((2, ROWS, CH), F32),
            pltpu.VMEM((NIGHTS, ROWS, EARLY), F32),
            pltpu.VMEM((NIGHTS, 2, ROWS, EARLY), F32),
            pltpu.VMEM((NIGHTS, 1, CH), I32),
            pltpu.VMEM((NIGHTS, 1, HALF), I32),
            pltpu.VMEM((NIGHTS, 1, BINS), I32),
            pltpu.VMEM((NIGHTS, TAPS, BINS), F32),
            pltpu.SMEM((NIGHTS, 1, HALF), I32),
            pltpu.SMEM((NIGHTS, 1, BINS), I32),
            pltpu.SMEM((NIGHTS, TAPS, BINS), F32),
        ]
        + [pltpu.VMEM(msg, F32)] * 8
        + [pltpu.VMEM((2,) + msg[1:], F32)] * 2
        + [
            D((22,)), D((2, 2, 4)), D((2, 2, 4)), D((2, 8)), D((8,)), D((8,)), D((4, 4)), D((4, 4)),
            D((4, 8)), D((4, 8)), D((STAGES + 2, 4, 2)), D((STAGES + 2, 4, 2)), D((4,)), D((4,)),
            D((STAGES + 1,)), D((STAGES + 1,)),
        ],
        compiler_params=pltpu.CompilerParams(
            collective_id=0, has_side_effects=True, vmem_limit_bytes=48 * 1024 * 1024
        ),
        name="exchange",
    )(
        held(vis), held(gains), held(corrupted_sample_markers), held(tap_offsets), first_bin, held(weights),
        held(lst_delay), held(bas), held(fringe_rate),
    )
    binned, weight_total = pl.pallas_call(
        place_kernel,
        out_shape=(jax.ShapeDtypeStruct((2, 4 * DEVS, CH), F32), jax.ShapeDtypeStruct((1, CH), F32)),
        in_specs=[vm, vm],
        out_specs=(hbm, hbm),
        scratch_shapes=[D((17,))],
        compiler_params=pltpu.CompilerParams(vmem_limit_bytes=8 * 1024 * 1024),
        name="place",
    )(binned, weight_total)
    return binned.reshape(2, 1, 4 * DEVS, CH), weight_total


def solution(mesh):
    placed = (
        P(None, "night", "bl", None, None),
        P("night", None),
        P(None, "night", "bl", None),
        P("bl", None),
        P("night"),
        P("night", None),
        P("night", None, None),
        P("night", None),
        P("bl"),
    )
    return jax.shard_map(
        per_device,
        mesh=mesh,
        in_specs=placed,
        out_specs=(P(None, ("night", "bl"), None, None), P(("night", "bl"), None)),
        check_vma=False,
    )
```

```python
import functools
import math

import jax
import jax.numpy as jnp
import numpy as np
from jax import lax
from jax.experimental import pallas as pl
from jax.experimental.pallas import tpu as pltpu
from jax.sharding import PartitionSpec as P

MESH = pl.DeviceIdType.MESH
F32 = jnp.float32
I32 = jnp.int32

NIGHTS = 4
DEVS = 32
BINS = 32
ROWS = 8
CH = 768
SAMPLES = 30
TAPS = 4
OWN_ANT = 11
STAGES = 3
WIDE = 256
HALF = 128
SOON = 128
LATER = 256
EARLY = 512
HB = 16


def _fit(kind, terms):
    k = np.arange(200)
    u = 0.125 * (1 + np.cos(np.pi * (k + 0.5) / 200))
    r = np.sqrt(u)
    y = np.sin(2 * np.pi * r) / r if kind == "sin" else np.cos(2 * np.pi * r)
    cheb = np.polynomial.chebyshev.Chebyshev.fit(u, y, terms - 1, domain=[0, 0.25])
    return [float(v) for v in cheb.convert(kind=np.polynomial.Polynomial).coef]


SIN_C = _fit("sin", 8)
COS_C = _fit("cos", 8)


def horner(coef, u):
    acc = jnp.full_like(u, coef[-1])
    for c in coef[-2::-1]:
        acc = acc * u + c
    return acc


def swap4(v):
    return pltpu.roll(v, 4, 0)


def flag(cond):
    return jnp.where(cond, jnp.float32(1.0), jnp.float32(0.0))


def comm_kernel(
    vis, gains, flags_h, offs_h, first_h, weights_h, delay_h, bas_h, rate_h,
    out_ref, wt_ref,
    offs_s, first_s, weights_s, delay_s, rate_s, V, UV, Y, Y2, S, landed, gyu, gxu, gyl, gxl, bx_v, by_v, bx_s, by_s,
    m0, m1, c0, c1, q0, q1, d0, d1, G, GP, GZ,
    zflags, zfirst, zoffs, zw, zfirst_s, zoffs_s, zw_s, s1p, s1n, s2p, s2n, r1p, r1n, r2p, r2n, r3p, r3n,
    local_sem, gsend, grecv, bsend, bxr, byr, msend, mrecv,
    rsend, rrecv, zsend, zrecv, gzs, gzr, asend, arecv,
):
    n = lax.axis_index("night")
    me = lax.axis_index("bl")
    core = lax.rem(me, 2)
    x = lax.rem(me // 2, 4)
    y = me // 8

    def bl_of(yy, xx, cc):
        return (yy * 4 + xx) * 2 + cc

    def rcopy(src, dst, ss, rs, dev):
        return pltpu.make_async_remote_copy(
            src_ref=src, dst_ref=dst, send_sem=ss, recv_sem=rs, device_id=dev, device_id_type=MESH
        )

    def loop(count, body, unroll=4, start=0):
        def step(i, c):
            body(i)
            return c

        lax.fori_loop(start, count, step, 0, unroll=unroll)

    load_vis = [
        pltpu.make_async_copy(
            vis.at[:, :, :, pl.ds(st * WIDE, WIDE)], V.at[:, :, :, pl.ds(st * WIDE, WIDE)], local_sem.at[st]
        )
        for st in range(STAGES)
    ]

    def table(which, late):
        begin = ((512, 640), (0, 256))[late][which]
        return gains.at[:, :, :, pl.ds(begin, LATER if late else SOON)], ((gyu, gxu), (gyl, gxl))[late][which]

    own_gains = []
    for late in (0, 1):
        for which in (0, 1):
            src, dst = table(which, late)
            own_gains.append(pltpu.make_async_copy(src, dst.at[(y, x)[which]], local_sem.at[3 + 2 * late + which]))
    small = [
        pltpu.make_async_copy(a, b, local_sem.at[7 + i])
        for i, (a, b) in enumerate(
            (
                (first_h, first_s), (offs_h, offs_s), (weights_h, weights_s), (delay_h, delay_s), (rate_h, rate_s),
                (flags_h, zflags.at[n]), (offs_h, zoffs.at[n]), (weights_h, zw.at[n]),
                (bas_h, bx_v.at[x * 2 + core]), (bas_h, by_v.at[y * 2 + core]),
            )
        )
    ]
    for c in (load_vis[0], *small[:6]):
        c.start()

    barrier = pltpu.get_barrier_semaphore()

    def greet(device):
        pl.semaphore_signal(barrier, inc=1, device_id=device, device_id_type=MESH)

    for k in (1, 2, 3):
        greet((lax.rem(n + k, 4), me))
    greet((n, bl_of(y, x, 1 - core)))
    for k in (1, 2, 3):
        for cc in range(2):
            greet((n, bl_of(y, lax.rem(x + k, 4), cc)))
            greet((n, bl_of(lax.rem(y + k, 4), x, cc)))
    for c in (*small[6:], *own_gains, *load_vis[1:]):
        c.start()

    lane = lax.broadcasted_iota(I32, (ROWS, WIDE), 1).astype(F32)
    row = lax.broadcasted_iota(I32, (ROWS, WIDE), 0)
    sign = jnp.where(row < 4, jnp.float32(-1.0), jnp.float32(1.0))
    for c in small[:6]:
        c.wait()
    first = first_s[0]
    zfirst[n] = jnp.full((1, HALF), first, I32)
    which_row = row & 3
    rates = jnp.where(
        which_row < 2,
        jnp.where(which_row == 0, rate_s[0], rate_s[1]),
        jnp.where(which_row == 2, rate_s[2], rate_s[3]),
    ) * (1.0 / (2.0 * math.pi))

    def samples(st):
        at = st * WIDE
        load_vis[st].wait()

        def per_sample(t):
            bits = (zflags[n, :, pl.ds(at, WIDE)] >> t) & 1
            both = jnp.concatenate([V[0, t, :, pl.ds(at, WIDE)], V[1, t, :, pl.ds(at, WIDE)]], axis=0)
            UV[t, :, pl.ds(at, WIDE)] = both * (1.0 - bits.astype(F32))

        loop(SAMPLES, per_sample, unroll=5)

    def shift_of(f, night, e):
        return (lax.shift_right_logical(f, 5) + jnp.where(e < (f & 31), 1, 0) - night) & 3

    def phases(st):
        return rates * (1.0 + (lane + float(st * WIDE)) * (1.0 / CH))

    def turned(st, rate, e):
        at = st * WIDE
        l = (e - first) & 31
        off = offs_s[0, l]
        acc = weights_s[0, l] * UV[off, :, pl.ds(at, WIDE)]
        for k in range(1, TAPS):
            acc = acc + weights_s[k, l] * UV[off + k, :, pl.ds(at, WIDE)]
        turns = rate * delay_s[0, l]
        r = turns - jnp.floor(turns + 0.5)
        u = r * r
        return horner(COS_C, u) * acc + (horner(SIN_C, u) * (r * sign)) * swap4(acc)

    up = lax.rem(n + 1, 4)
    down = lax.rem(n + 3, 4)
    far = lax.rem(n + 2, 4)

    def zcopy(st, which, h):
        src = (s1p, s1n, s2p, s2n)[which].at[st, pl.ds(h * HB, HB)]
        dst = (r1p, r1n, r2p, r2n)[which].at[st, pl.ds(h * HB, HB)]
        to = up if which % 2 == 0 else down
        return rcopy(src, dst, zsend.at[st, which, h], zrecv.at[st, which, h], (to, me))

    def forward(st, which, h):
        src, dst = ((r1p, r3p), (r1n, r3n))[which]
        part = pl.ds(h * HB, HB)
        to = (up, down)[which]
        return rcopy(
            src.at[st, part], dst.at[st, part], zsend.at[STAGES + st, which, h], zrecv.at[STAGES + st, which, h], (to, me)
        )

    lo = pl.ds(0, HALF)
    hi = pl.ds(HALF, HALF)

    def first_message(st, i, s, a, b):
        two = flag(s == 2)
        s1p[st, i] = two * a + flag(s == 1) * b
        s1n[st, i] = two * b + flag(s == 3) * a

    def second_message(st, i, e, a, b):
        s = shift_of(first, n, e)
        s2p[st, i] = flag(s == 1) * a + flag(shift_of(first_down, down, e) == 2) * r1p[st, i]
        s2n[st, i] = flag(s == 3) * b + flag(shift_of(first_up, up, e) == 2) * r1n[st, i]

    def early(st):
        samples(st)
        rate = phases(st)

        def per_bin(e):
            v = turned(st, rate, e)
            Y[st, e] = v
            a, b = v[:, :HALF], v[:, HALF:]
            s = shift_of(first, n, e)
            first_message(st, e, s, a, b)
            s2p[st, e] = flag(s == 1) * a
            s2n[st, e] = flag(s == 3) * b

        loop(BINS, per_bin)

    def start_early(st, message):
        for h in (0, 1):
            for w in (0, 1):
                zcopy(st, 2 * message + w, h).start()

    early(0)
    pl.semaphore_wait(barrier, 16)
    start_early(0, 0)
    start_early(0, 1)
    for c in (*small[6:], *own_gains):
        c.wait()

    def gain_a(which, late, k):
        _, tab = table(which, late)
        mine = (y, x)[which]
        to = bl_of(lax.rem(y + k, 4), x, core) if which == 0 else bl_of(y, lax.rem(x + k, 4), core)
        return rcopy(tab.at[mine], tab.at[mine], gsend.at[which, late, k], grecv.at[which, late, mine], (n, to))

    def gain_a_wait(which, late):
        _, tab = table(which, late)
        for k in (1, 2, 3):
            o = lax.rem((y, x)[which] + k, 4)
            rcopy(tab.at[o], tab.at[o], gsend.at[which, late, k], grecv.at[which, late, o], (n, me)).wait_recv()

    def slot_dev(k, own):
        s = lax.rem(own + k, 8)
        return s, s // 2, lax.rem(s, 2)

    def bas_x(k):
        s, tx, tc = slot_dev(k, x * 2 + core)
        mine = x * 2 + core
        return rcopy(bx_v.at[mine], bx_v.at[mine], bsend.at[0, k], bxr.at[mine], (n, bl_of(y, tx, tc)))

    def bas_y(k):
        s, ty, tc = slot_dev(k, y * 2 + core)
        mine = y * 2 + core
        return rcopy(by_v.at[mine], by_v.at[mine], bsend.at[1, k], byr.at[mine], (n, bl_of(ty, x, tc)))

    for k in (1, 3, 2):
        for which in (0, 1):
            gain_a(which, 0, k).start()

    def start_bas(k):
        bas_x(k).start()
        bas_y(k).start()

    loop(8, start_bas, unroll=1, start=1)

    def meta(k):
        t = lax.rem(n + k, 4)
        return [
            rcopy(a, b, msend.at[i, k], mrecv.at[i, n], (t, me))
            for i, (a, b) in enumerate(
                (
                    (zflags.at[n], zflags.at[n]), (zoffs.at[n], zoffs.at[n]), (zw.at[n], zw.at[n]),
                    (zfirst.at[n], zfirst.at[n]),
                )
            )
        ]

    for k in (1, 3, 2):
        for c in meta(k):
            c.start()
    for k in (1, 3, 2):
        for which in (0, 1):
            gain_a(which, 1, k).start()
    early(1)
    start_early(1, 0)

    def pass_on(st):
        for h in (0, 1):
            for w in (0, 1):
                zcopy(st, w, h).wait_recv()
                forward(st, w, h).start()

    start_early(1, 1)
    pass_on(0)

    def wait_bas(k):
        sx = lax.rem(x * 2 + core + k, 8)
        sy = lax.rem(y * 2 + core + k, 8)
        rcopy(bx_v.at[sx], bx_v.at[sx], bsend.at[0, k], bxr.at[sx], (n, me)).wait_recv()
        rcopy(by_v.at[sy], by_v.at[sy], bsend.at[1, k], byr.at[sy], (n, me)).wait_recv()

    loop(8, wait_bas, unroll=1, start=1)
    to_s0 = pltpu.make_async_copy(bx_v, bx_s, local_sem.at[17])
    to_s1 = pltpu.make_async_copy(by_v, by_s, local_sem.at[18])
    to_s0.start()
    to_s1.start()
    gain_a_wait(0, 0)
    gain_a_wait(1, 0)
    to_s0.wait()
    to_s1.wait()

    slots = (lambda k: lax.rem(x * 2 + core + k, 8), lambda k: lax.rem(y * 2 + core + k, 8))
    asked_of = (bx_s, by_s)
    mine_of = (x * 2 + core, y * 2 + core)

    def pick(which, late, slot):
        out = ((m0, m1), (q0, q1))[late][which]
        _, tab = table(which, late)
        for r in range(ROWS):
            a = asked_of[which][slot, r // 4, r % 4]
            owner = lax.shift_right_logical(a * 5958, 16)
            at = a - owner * OWN_ANT
            ox, oy = (owner >> 1) & 3, owner >> 3
            fixed, moving, here = (ox, oy, x) if which == 0 else (oy, ox, y)
            w = flag((fixed == here) & ((owner & 1) == core))
            for p in range(2):
                out[slot, p, pl.ds(r, 1), :] = w * tab[moving, p, at]

    def gain_b(which, late, k):
        s, t, tc = slot_dev(k, mine_of[which])
        src = ((m0, m1), (q0, q1))[late][which]
        dst = ((c0, c1), (d0, d1))[late][which]
        to = bl_of(y, t, tc) if which == 0 else bl_of(t, x, tc)
        i = 2 * late + which
        return rcopy(src.at[s], dst.at[mine_of[which]], rsend.at[i, k], rrecv.at[i, mine_of[which]], (n, to))

    def send_rows(late):
        def go(k):
            for which in (0, 1):
                pick(which, late, slots[which](k))
                gain_b(which, late, k).start()

        loop(8, go, unroll=1, start=1)
        for which in (0, 1):
            pick(which, late, mine_of[which])
            dst = ((c0, c1), (d0, d1))[late][which]
            src = ((m0, m1), (q0, q1))[late][which]
            dst[mine_of[which]] = src[mine_of[which]]

    def gain_products(late):
        def wait(k):
            for which in (0, 1):
                s = slots[which](k)
                src = ((m0, m1), (q0, q1))[late][which]
                dst = ((c0, c1), (d0, d1))[late][which]
                i = 2 * late + which
                rcopy(src.at[s], dst.at[s], rsend.at[i, k], rrecv.at[i, s], (n, me)).wait_recv()

        loop(8, wait, unroll=1, start=1)
        for which in (0, 1):
            got = ((c0, c1), (d0, d1))[late][which]
            parts = []
            for p in range(2):
                acc = got[0, p]
                for s in range(1, 8):
                    acc = acc + got[s, p]
                parts.append(acc)
            A, B = parts
            cols = pl.ds(((512, 640), (0, 256))[late][which], LATER if late else SOON)
            G[0, :, cols] = A * swap4(A) + B * swap4(B)
            G[1, :, cols] = A * swap4(B) - B * swap4(A)

    send_rows(0)

    gain_a_wait(0, 1)
    gain_a_wait(1, 1)
    send_rows(1)

    samples(2)
    rate2 = phases(2)

    def last(e):
        Y[2, e] = turned(2, rate2, e)

    loop(BINS, last)
    gain_products(0)

    def bin_copy(st, t):
        if st >= 2:
            src = Y.at[2, t, :, pl.ds((st - 2) * HALF, HALF)]
            return rcopy(src, Y2.at[st - 2, me], asend.at[st], arecv.at[st], (n, t))
        return rcopy(S.at[st, t], landed.at[st, me], asend.at[st], arecv.at[st], (n, t))

    def all_bins(st):
        part = pl.ds(0, DEVS - 1)
        if st >= 2:
            return rcopy(Y2.at[st - 2, part], Y2.at[st - 2, part], asend.at[st], arecv.at[st], (n, me))
        return rcopy(S.at[st, part], landed.at[st, part], asend.at[st], arecv.at[st], (n, me))

    low_early = lax.broadcasted_iota(I32, (ROWS, EARLY), 0) < 4

    def gz(k):
        return rcopy(GP.at[n], GP.at[n], gzs.at[k], gzr.at[n], (lax.rem(n + k, 4), me))

    def load_meta():
        for k in (1, 2, 3):
            o = lax.rem(n + k, 4)
            for i, (a, b) in enumerate(
                ((zflags.at[o], zflags.at[o]), (zoffs.at[o], zoffs.at[o]), (zw.at[o], zw.at[o]), (zfirst.at[o], zfirst.at[o]))
            ):
                rcopy(a, b, msend.at[i, k], mrecv.at[i, o], (n, me)).wait_recv()
        to_smem = [
            pltpu.make_async_copy(a, b, local_sem.at[19 + i])
            for i, (a, b) in enumerate(((zoffs, zoffs_s), (zw, zw_s), (zfirst, zfirst_s)))
        ]
        for c in to_smem:
            c.start()
        return to_smem

    def share_gains():
        gain_products(1)
        GP[n] = jnp.where(low_early, G[0, :, pl.ds(0, EARLY)], G[1, :, pl.ds(0, EARLY)])
        for k in (2, 1, 3):
            gz(k).start()

    for g in (0, 1):
        cols = pl.ds(EARLY + g * HALF, HALF)
        gr, gs = G[0, :, cols], G[1, :, cols]
        part = pl.ds(g * HALF, HALF)

        def with_gain(t):
            v = Y[2, t, :, part]
            return gr * v + gs * swap4(v)

        def send_last(k):
            t = lax.rem(me + k, DEVS)
            Y[2, t, :, part] = with_gain(t)
            bin_copy(2 + g, t).start()

        loop(29, send_last, unroll=4, start=1)
        loop(DEVS, send_last, unroll=3, start=29)
        Y2[g, me] = with_gain(me)
        if g == 0:
            share_gains()
            to_smem = load_meta()
    pass_on(1)

    for c in to_smem:
        c.wait()
    first_down, first_up, first_far = zfirst_s[down, 0, 0], zfirst_s[up, 0, 0], zfirst_s[far, 0, 0]

    total = jnp.zeros((1, CH), F32)
    bin_here = n * BINS + me
    for k in range(NIGHTS):
        l = bin_here - zfirst_s[k, 0, 0]
        valid = flag((l >= 0) & (l < BINS))
        lc = jnp.clip(l, 0, BINS - 1)
        off = zoffs_s[k, 0, lc]
        for t in range(TAPS):
            bits = (zflags[k] >> (off + t)) & 1
            total = total + (valid * zw_s[k, t, lc]) * (1.0 - bits.astype(F32))
    wt_ref[...] = total
    scale = 1.0 / jnp.maximum(total, 0.5)

    def put(begin, k, a, b, inv):
        a, b = a * inv, b * inv
        low = lax.broadcasted_iota(I32, a.shape, 0) < 4
        at = pl.multiple_of(k * 8, 8)
        cols = pl.ds(begin, a.shape[1])
        out_ref[0, pl.ds(at, 8), cols] = jnp.where(low, a, swap4(b))
        out_ref[1, pl.ds(at, 8), cols] = jnp.where(low, swap4(a), b)

    def scale_of(st):
        return jnp.broadcast_to(scale[:, st * WIDE : (st + 1) * WIDE], (ROWS, WIDE))

    def last_first(g):
        all_bins(2 + g).wait_recv()
        s = shift_of(first, n, me)
        loop(HB, lambda j: first_message(2, g * HB + j, s, Y2[g, j], Y2[g, HB + j]))
        zcopy(2, 0, g).start()
        zcopy(2, 1, g).start()

    def last_second(g):
        zcopy(2, 0, g).wait_recv()
        zcopy(2, 1, g).wait_recv()
        loop(HB, lambda j: second_message(2, g * HB + j, me, Y2[g, j], Y2[g, HB + j]))
        zcopy(2, 2, g).start()
        zcopy(2, 3, g).start()

    def unpack_gains():
        for k in (1, 2, 3):
            o = lax.rem(n + k, 4)
            rcopy(GP.at[o], GP.at[o], gzs.at[k], gzr.at[o], (n, me)).wait_recv()
        for k in range(NIGHTS):
            packed = GP[k]
            turned_over = swap4(packed)
            GZ[k, 0] = jnp.where(low_early, packed, turned_over)
            GZ[k, 1] = jnp.where(low_early, -turned_over, packed)

    def combine(st, e):
        here = flag(shift_of(first, n, e) == 0)
        from_down = flag(shift_of(first_down, down, e) == 1)
        from_up = flag(shift_of(first_up, up, e) == 3)
        from_far = flag(shift_of(first_far, far, e) == 2)

        def part(half, terms):
            cols = pl.ds(st * WIDE + half * HALF, HALF)
            acc = None
            for night, v in terms:
                w = GZ[night, 0, :, cols] * v + GZ[night, 1, :, cols] * swap4(v)
                acc = w if acc is None else acc + w
            return acc

        a = part(
            0,
            (
                (n, here * Y[st, e, :, lo]), (up, from_up * r1n[st, e]), (down, r2p[st, e]),
                (far, from_far * r3p[st, e]),
            ),
        )
        b = part(
            1,
            (
                (n, here * Y[st, e, :, hi]), (down, from_down * r1p[st, e]), (up, r2n[st, e]),
                (far, from_far * r3n[st, e]),
            ),
        )
        return a, b

    def finish_early(st):
        for h in (0, 1):
            zcopy(st, 2, h).wait_recv()
            zcopy(st, 3, h).wait_recv()
            forward(st, 0, h).wait_recv()
            forward(st, 1, h).wait_recv()

        def go(k):
            t = lax.rem(me + k, DEVS)
            a, b = combine(st, t)
            S[st, t, :, lo] = a
            S[st, t, :, hi] = b
            bin_copy(st, t).start()

        loop(29, go, unroll=4, start=1)
        loop(DEVS, go, unroll=3, start=29)
        a, b = combine(st, me)
        landed[st, me, :, lo] = a
        landed[st, me, :, hi] = b

    last_first(0)
    unpack_gains()
    finish_early(0)
    last_first(1)
    finish_early(1)
    last_second(0)
    last_second(1)

    def assemble(st):
        all_bins(st).wait_recv()
        inv = scale_of(st)
        loop(DEVS // 2, lambda k: put(st * WIDE, k, landed[st, 2 * k], landed[st, 2 * k + 1], inv))

    assemble(0)

    for k in (1, 2, 3):
        for which in (0, 1):
            for late in (0, 1):
                gain_a(which, late, k).wait_send()
        for c in meta(k):
            c.wait_send()
        gz(k).wait_send()

    def done(k):
        bas_x(k).wait_send()
        bas_y(k).wait_send()
        for which in (0, 1):
            for late in (0, 1):
                gain_b(which, late, k).wait_send()

    loop(8, done, unroll=1, start=1)
    for h in (0, 1):
        for st in range(STAGES):
            for w in range(4 if st < 2 else 2):
                zcopy(st, w, h).wait_send()
        for w in (0, 1):
            for st in (0, 1):
                forward(st, w, h).wait_send()
    for st in (0, 2, 3):
        all_bins(st).wait_send()

    here2 = flag(shift_of(first, n, me) == 0)
    down2 = flag(shift_of(first_down, down, me) == 1)
    up2 = flag(shift_of(first_up, up, me) == 3)
    for g in (0, 1):
        zcopy(2, 2, g).wait_recv()
        zcopy(2, 3, g).wait_recv()
        inv2 = scale_of(2)[:, g * HALF : (g + 1) * HALF]

        def finish(k):
            lower = [
                here2 * Y2[g, j] + up2 * r1n[2, g * HB + j] + r2p[2, g * HB + j] for j in (2 * k, 2 * k + 1)
            ]
            upper = [
                here2 * Y2[g, HB + j] + down2 * r1p[2, g * HB + j] + r2n[2, g * HB + j] for j in (2 * k, 2 * k + 1)
            ]
            put(EARLY + g * HALF, k, *lower, inv2)
            put(EARLY + g * HALF, HB // 2 + k, *upper, inv2)

        loop(HB // 2, finish)
    assemble(1)
    for h in (0, 1):
        zcopy(2, 2, h).wait_send()
        zcopy(2, 3, h).wait_send()
    all_bins(1).wait_send()


def place_kernel(binned, wt, out, wt_out, sems):
    copies = [
        pltpu.make_async_copy(binned.at[p, pl.ds(k * 16, 16)], out.at[p, pl.ds(k * 16, 16)], sems.at[8 * p + k])
        for p in range(2)
        for k in range(8)
    ]
    copies.append(pltpu.make_async_copy(wt, wt_out, sems.at[16]))
    for c in copies:
        c.start()
    for c in copies:
        c.wait()


def per_device(
    visibilities, corrupted_sample_markers, antenna_gain_table, baseline_antennas, first_bin, tap_offsets, tap_weights,
    lst_delay, fringe_rate,
):
    vis = jnp.transpose(visibilities[:, 0], (0, 2, 1, 3))
    gains = jnp.transpose(antenna_gain_table, (0, 2, 1, 3))
    weights = jnp.transpose(tap_weights[0], (1, 0))
    bas = jnp.transpose(baseline_antennas, (1, 0))

    def held(a):
        return pltpu.with_memory_space_constraint(a, pltpu.HBM)

    vm = pl.BlockSpec(memory_space=pltpu.VMEM)
    hbm = pl.BlockSpec(memory_space=pltpu.HBM)
    D = pltpu.SemaphoreType.DMA
    msg = (STAGES, BINS, ROWS, HALF)
    binned, weight_total = pl.pallas_call(
        comm_kernel,
        out_shape=(
            pltpu.VMEM((2, 4 * DEVS, CH), F32),
            pltpu.VMEM((1, CH), F32),
        ),
        in_specs=[hbm] * 9,
        out_specs=(vm, vm),
        scratch_shapes=[
            pltpu.SMEM((1, BINS), I32),
            pltpu.SMEM((1,), I32),
            pltpu.SMEM((TAPS, BINS), F32),
            pltpu.SMEM((1, BINS), F32),
            pltpu.SMEM((4,), F32),
            pltpu.VMEM((2, SAMPLES, 4, CH), F32),
            pltpu.VMEM((SAMPLES, ROWS, CH), F32),
            pltpu.VMEM((STAGES, BINS, ROWS, WIDE), F32),
            pltpu.VMEM((2, DEVS, ROWS, HALF), F32),
            pltpu.VMEM((2, BINS, ROWS, WIDE), F32),
            pltpu.VMEM((2, DEVS, ROWS, WIDE), F32),
            *([pltpu.VMEM((4, 2, OWN_ANT, 1, SOON), F32)] * 2),
            *([pltpu.VMEM((4, 2, OWN_ANT, 1, LATER), F32)] * 2),
            pltpu.VMEM((8, 2, 4), I32),
            pltpu.VMEM((8, 2, 4), I32),
            pltpu.SMEM((8, 2, 4), I32),
            pltpu.SMEM((8, 2, 4), I32),
            *([pltpu.VMEM((8, 2, ROWS, SOON), F32)] * 4),
            *([pltpu.VMEM((8, 2, ROWS, LATER), F32)] * 4),
            pltpu.VMEM((2, ROWS, CH), F32),
            pltpu.VMEM((NIGHTS, ROWS, EARLY), F32),
            pltpu.VMEM((NIGHTS, 2, ROWS, EARLY), F32),
            pltpu.VMEM((NIGHTS, 1, CH), I32),
            pltpu.VMEM((NIGHTS, 1, HALF), I32),
            pltpu.VMEM((NIGHTS, 1, BINS), I32),
            pltpu.VMEM((NIGHTS, TAPS, BINS), F32),
            pltpu.SMEM((NIGHTS, 1, HALF), I32),
            pltpu.SMEM((NIGHTS, 1, BINS), I32),
            pltpu.SMEM((NIGHTS, TAPS, BINS), F32),
        ]
        + [pltpu.VMEM(msg, F32)] * 8
        + [pltpu.VMEM((2,) + msg[1:], F32)] * 2
        + [
            D((22,)), D((2, 2, 4)), D((2, 2, 4)), D((2, 8)), D((8,)), D((8,)), D((4, 4)), D((4, 4)),
            D((4, 8)), D((4, 8)), D((STAGES + 2, 4, 2)), D((STAGES + 2, 4, 2)), D((4,)), D((4,)),
            D((STAGES + 1,)), D((STAGES + 1,)),
        ],
        compiler_params=pltpu.CompilerParams(
            collective_id=0, has_side_effects=True, vmem_limit_bytes=48 * 1024 * 1024
        ),
        name="exchange",
    )(
        held(vis), held(gains), held(corrupted_sample_markers), held(tap_offsets), first_bin, held(weights),
        held(lst_delay), held(bas), held(fringe_rate),
    )
    binned, weight_total = pl.pallas_call(
        place_kernel,
        out_shape=(jax.ShapeDtypeStruct((2, 4 * DEVS, CH), F32), jax.ShapeDtypeStruct((1, CH), F32)),
        in_specs=[vm, vm],
        out_specs=(hbm, hbm),
        scratch_shapes=[D((17,))],
        compiler_params=pltpu.CompilerParams(vmem_limit_bytes=8 * 1024 * 1024),
        name="place",
    )(binned, weight_total)
    return binned.reshape(2, 1, 4 * DEVS, CH), weight_total


def solution(mesh):
    placed = (
        P(None, "night", "bl", None, None),
        P("night", None),
        P(None, "night", "bl", None),
        P("bl", None),
        P("night"),
        P("night", None),
        P("night", None, None),
        P("night", None),
        P("bl"),
    )
    return jax.shard_map(
        per_device,
        mesh=mesh,
        in_specs=placed,
        out_specs=(P(None, ("night", "bl"), None, None), P(("night", "bl"), None)),
        check_vma=False,
    )
```
